256 devices in a mesh: shot: 16 (over x_hi, z), gx: 8 (over y, core), gy: 2 (over x_lo).
Axes of the slice: x: 4 (x_hi: 2, x_lo: 2; x = x_hi * 2 + x_lo), y: 4, z: 8, core: 2. Of those that a mesh axis runs over, the one named last changes fastest.
Arguments:
- older_field: float32 [16, 64, 64, 256], P('shot', None, 'gx', 'gy'), may hold values from -6 to 6
- newer_field: float32 [16, 64, 64, 256], P('shot', None, 'gx', 'gy'), may hold values from -6 to 6
- velocity: float32 [64, 64, 256], P(None, 'gx', 'gy'), may hold values from 0.03 to 0.1
- preconditioner: float32 [64, 64, 256], P('shot', 'gx', 'gy'), may hold values from 0.2 to 2
- traces: float32 [16, 4, 2048], P('shot'), may hold values from -6 to 6
- receiver_z: int32 [16, 2048], P('shot'), may hold values from 0 to 63
- receiver_x: int32 [16, 2048], P('shot'), may hold values from 0 to 63
- receiver_y: int32 [16, 2048], P('shot'), may hold values from 0 to 255
- aperture_x: int32 [16], P('shot'), may hold values from 0 to 16
- aperture_y: int32 [16], P('shot'), may hold values from 0 to 64
Outputs:
- image_step: float32 [64, 64, 256], P('shot', 'gx', 'gy')
- new_residual: float32 [16, 4, 2048], P('shot')
The draws below stay inside these ranges and needn't reach their ends.
All inputs are finite; a program needn't handle non-finite values.
Results may differ from the reference program's by a relative error of at most 0.023.
Values sent between devices are 32-bit elements; how exact they have to be, the bound alone decides.
No kernel may reach another device: no remote copies, remote signals or barrier semaphores. Data moves between devices by JAX's collectives and lax.ppermute only.
A program may use at most 64 MiB of HBM per device.

```python
import math
import jax
import jax.numpy as jnp
from jax import lax

NZ = 64
NREC = 2048
STEPS = 4
SHOTS = 16
NX = 64
NY = 256
AWX = 48
AWY = 192


def with_ends(values, own_key, smallest, largest):
    shape = values.shape
    place = [jax.random.randint(jax.random.fold_in(own_key, axis), (), 0, shape[axis]) for axis in range(len(shape))]
    values = values.at[tuple(place)].set(smallest)
    longest = shape.index(max(shape))
    place[longest] = (place[longest] + 1) % shape[longest]
    return values.at[tuple(place)].set(largest)


def block_levels(key, extent, pieces, least, largest):
    loudness, own = 1.0, jax.random.fold_in(key, 6)
    for dim, blocks in pieces:
        draws = jnp.exp(jax.random.uniform(jax.random.fold_in(own, dim), (blocks,), jnp.float32, least / len(pieces), largest / len(pieces)))
        loudness = loudness * jnp.repeat(draws, extent[dim] // blocks).reshape([-1 if axis == dim else 1 for axis in range(len(extent))])
    return loudness


def bell_draw(stream_key, shape, deviation, most, pieces=(), held_as=jnp.bfloat16):
    gain = block_levels(stream_key, shape, pieces, -0.22, 0.18) if pieces else 1.0
    values = jax.random.normal(stream_key, shape, jnp.float32) * deviation * gain
    return jnp.minimum(jnp.maximum(values, -most), most).astype(held_as)


def setup_inputs(seed: int = 0) -> dict:
    seeds = jax.random.split(jax.random.key(seed), 11)
    return {
        "older_field": bell_draw(seeds[0], (SHOTS, NZ, NX, NY), 1.0, 6.0, ((0, 16), (2, 8), (3, 2)), jnp.float32),
        "newer_field": bell_draw(seeds[1], (SHOTS, NZ, NX, NY), 1.0, 6.0, ((0, 16), (2, 8), (3, 2)), jnp.float32),
        "velocity": jnp.clip(0.03 + 0.07 * jax.random.uniform(seeds[2], (NZ, NX, NY), jnp.float32) ** block_levels(seeds[2], (NZ, NX, NY), ((1, 8), (2, 2)), -0.2, 0.2), 0.03, 0.1),
        "preconditioner": jnp.clip(jnp.exp(math.log(2.0) - 2.3025851 * jax.random.uniform(seeds[3], (NZ, NX, NY), jnp.float32) ** block_levels(seeds[3], (NZ, NX, NY), ((0, 16), (1, 8), (2, 2)), -0.2, 0.2)), 0.2, 2.0),
        "traces": bell_draw(seeds[4], (SHOTS, STEPS, NREC), 1.0, 6.0, ((0, 16),), jnp.float32),
        "receiver_z": with_ends(jax.random.randint(seeds[5], (SHOTS, NREC), 0, NZ), jax.random.fold_in(seeds[5], 1), 0, NZ - 1).astype(jnp.int32),
        "receiver_x": with_ends(jax.random.randint(seeds[6], (SHOTS, NREC), 0, NX), jax.random.fold_in(seeds[6], 1), 0, NX - 1).astype(jnp.int32),
        "receiver_y": with_ends(jax.random.randint(seeds[7], (SHOTS, NREC), 0, NY), jax.random.fold_in(seeds[7], 1), 0, NY - 1).astype(jnp.int32),
        "aperture_x": with_ends(jax.random.randint(seeds[8], (SHOTS,), 0, NX - AWX + 1), jax.random.fold_in(seeds[8], 1), 0, NX - AWX).astype(jnp.int32),
        "aperture_y": with_ends(jax.random.randint(seeds[9], (SHOTS,), 0, NY - AWY + 1), jax.random.fold_in(seeds[9], 1), 0, NY - AWY).astype(jnp.int32),
    }


stencil_weights = (-205.0 / 72.0, 8.0 / 5.0, -1.0 / 5.0, 8.0 / 315.0, -1.0 / 560.0)


def lap_core(padded):
    extended = jnp.pad(padded, ((4, 4), (0, 0), (0, 0)))
    full_z, full_x, full_y = extended.shape

    def window(shift_z, shift_x, shift_y):
        return extended[4 + shift_z:full_z - 4 + shift_z, 4 + shift_x:full_x - 4 + shift_x, 4 + shift_y:full_y - 4 + shift_y]

    result = (3.0 * stencil_weights[0]) * window(0, 0, 0)
    for reach in range(1, 5):
        pairs = ((window(reach, 0, 0) + window(-reach, 0, 0)) + (window(0, reach, 0) + window(0, -reach, 0))) + (window(0, 0, reach) + window(0, 0, -reach))
        result = result + stencil_weights[reach] * pairs
    return result


def laplace(field):
    return lap_core(jnp.pad(field, ((0, 0), (4, 4), (4, 4))))


def background(older, newer, velocity):
    accels = []
    for moment in range(STEPS):
        accel = velocity * laplace(newer)
        nxt = (2.0 * newer - older) + accel
        accels.append(accel)
        older, newer = newer, nxt
    return accels


def aperture(start_x, start_y):
    cells_x = jnp.arange(NX, dtype=jnp.int32)
    cells_y = jnp.arange(NY, dtype=jnp.int32)
    inside_x = (cells_x >= start_x) & (cells_x < start_x + AWX)
    inside_y = (cells_y >= start_y) & (cells_y < start_y + AWY)
    return (inside_x[:, None] & inside_y[None, :]).astype(jnp.float32)[None]


def reference(older_field, newer_field, velocity, preconditioner, traces, receiver_z, receiver_x, receiver_y, aperture_x, aperture_y):
    items = (older_field, newer_field, traces, receiver_z, receiver_x, receiver_y, aperture_x, aperture_y)

    def image_part(total, item):
        older, newer, shot_traces, depth_idx, lat_x, lat_y, start_x, start_y = item
        accels = background(older, newer, velocity)
        later = jnp.zeros_like(older)
        latest = jnp.zeros_like(older)
        grad = jnp.zeros_like(older)
        for moment in reversed(range(STEPS)):
            inject = jnp.zeros_like(older).at[depth_idx, lat_x, lat_y].add(shot_traces[moment])
            adjoint = ((2.0 * later - latest) + laplace(velocity * later)) + inject
            grad = grad + accels[moment] * adjoint
            latest, later = later, adjoint
        return total + aperture(start_x, start_y) * grad, None

    gradient, unused = lax.scan(image_part, jnp.zeros(velocity.shape, jnp.float32), items)
    scaled = preconditioner * gradient
    descent_dot = jnp.sum(gradient * scaled)

    def predict(item):
        older, newer, shot_traces, depth_idx, lat_x, lat_y, start_x, start_y = item
        accels = background(older, newer, velocity)
        source = aperture(start_x, start_y) * scaled
        before = jnp.zeros_like(older)
        current = jnp.zeros_like(older)
        samples = []
        for moment in range(STEPS):
            nxt = ((2.0 * current - before) + velocity * laplace(current)) + source * accels[moment]
            samples.append(nxt[depth_idx, lat_x, lat_y])
            before, current = current, nxt
        return jnp.stack(samples)

    predicted = lax.map(predict, items)
    trace_energy = jnp.sum(predicted * predicted)
    step_length = descent_dot / (trace_energy + 1e-6)
    return step_length * scaled, traces - step_length * predicted
```

```python
import jax
import jax.numpy as jnp
from jax import lax
from jax.experimental import pallas as pl
from jax.experimental.pallas import tpu as pltpu
from jax.sharding import PartitionSpec as P

STEPS = 4
NZ, BX, BY = 64, 8, 128
NREC = 2048
F32, BF16, I32 = jnp.float32, jnp.bfloat16, jnp.int32
weights = (-205.0 / 72.0, 8.0 / 5.0, -1.0 / 5.0, 8.0 / 315.0, -1.0 / 560.0)


def call(kernel, outs, scratch=(), limit=24, flops=10_000_000):
    def run(*args, smem=0):
        specs = [
            pl.BlockSpec(memory_space=pltpu.SMEM if i < smem else pltpu.VMEM)
            for i in range(len(args))
        ]
        return pl.pallas_call(
            kernel,
            out_shape=[jax.ShapeDtypeStruct(s, d) for s, d in outs],
            in_specs=specs,
            out_specs=[pl.BlockSpec(memory_space=pltpu.VMEM) for _ in outs],
            scratch_shapes=list(scratch),
            compiler_params=pltpu.CompilerParams(vmem_limit_bytes=limit * 1024 * 1024),
            cost_estimate=pl.CostEstimate(
                flops=flops, bytes_accessed=2_000_000, transcendentals=0
            ),
        )(*args)

    return run


def lanes(rows):
    return lax.broadcasted_iota(I32, (rows, BY), 1)


def near_edge(gy, lane):
    return ((gy == 0) & (lane >= BY - 4)) | ((gy == 1) & (lane < 4))


def far_edge(gy, lane):
    return ((gy == 0) & (lane < 4)) | ((gy == 1) & (lane >= BY - 4))


def send_edges(load, outer_ref, inner_ref, strip_ref, slot, scal):
    core, gy = scal[0], scal[1]
    keep = near_edge(gy, lanes(8))
    for i in range(4):
        outer_ref[slot, i] = load(4 * core + i)
        inner_ref[slot, i] = load(4 * (1 - core) + i)
    for half in range(2):
        packed = jnp.zeros((8, BY), F32)
        for j in range(32):
            index = half * 32 + j
            plane = load(index // 8)[8 * (index % 8) : 8 * (index % 8) + 8]
            packed = packed + pltpu.roll(jnp.where(keep, plane, 0.0), 4 * j, 1)
        strip_ref[slot, 8 * half : 8 * half + 8] = packed


def fill(padded, side, load, outer_ref, inner_ref, strip_ref, slot, scal):
    core, gy = scal[0], scal[1]
    keep = far_edge(gy, lanes(8))
    zero = jnp.zeros((8, BY), F32)
    for x in range(BX):
        padded[4 + x, 0:8] = zero
        padded[4 + x, 72:80] = zero
        padded[4 + x, 8:72] = load(x)
    for i in range(4):
        padded[12 * core + i, 8:72] = outer_ref[slot, i]
        padded[12 * (1 - core) + i, 8:72] = inner_ref[slot, i]
    for half in range(2):
        packed = strip_ref[slot, 8 * half : 8 * half + 8]
        for j in range(32):
            index = half * 32 + j
            turned = pltpu.roll(packed, (BY - 4 * j) % BY, 1)
            side[index // 8, 8 * (index % 8) : 8 * (index % 8) + 8] = jnp.where(keep, turned, 0.0)


def lap(padded, side, x):
    lane = lanes(NZ)
    centre = padded[4 + x, 8:72]
    other = side[x]
    result = (3.0 * weights[0]) * centre
    for k in range(1, 5):
        along_z = padded[4 + x, 8 + k : 72 + k] + padded[4 + x, 8 - k : 72 - k]
        along_x = padded[4 + x + k, 8:72] + padded[4 + x - k, 8:72]
        right = pltpu.roll(jnp.where(lane < k, other, centre), BY - k, 1)
        left = pltpu.roll(jnp.where(lane >= BY - k, other, centre), k, 1)
        result = result + weights[k] * ((along_z + along_x) + (right + left))
    return result


FIELD = ((BX, NZ, BY), F32)
PADDED = pltpu.VMEM((16, 80, BY), F32)
SIDE = pltpu.VMEM((BX, NZ, BY), F32)


def edges(count):
    return [((count, 4, NZ, BY), F32), ((count, 4, NZ, BY), F32), ((count, 16, BY), F32)]


def first_kernel(scal, newer, older, newer_out, older_out, outer, inner, strip):
    for x in range(BX):
        newer_out[x] = newer[pl.ds(x, NZ, stride=8), :]
        older_out[x] = older[pl.ds(x, NZ, stride=8), :]
    send_edges(lambda x: newer_out[x], outer, inner, strip, 0, scal)


def two_pieces(values):
    high = values.astype(BF16)
    return high, (values - high.astype(F32)).astype(BF16)


def prepare_kernel(scal, vel, traces, rz, rx, ry, vel_out, inj, pick_cell, pick_y, spread):
    for x in range(BX):
        vel_out[x] = vel[pl.ds(x, NZ, stride=8), :]
    lat_x = rx[...] - scal[2]
    lat_y = ry[...] - scal[3]
    present = (lat_x >= 0) & (lat_x < BX) & (lat_y >= 0) & (lat_y < BY)
    row = jnp.where(present, lat_x * NZ + rz[...], -1)
    col = jnp.where(present, lat_y, -1)

    def rows(i, carry):
        number = lax.broadcasted_iota(I32, (16, NREC), 0) + 16 * i
        pick_cell[pl.ds(pl.multiple_of(16 * i, 16), 16), :] = jnp.where(number == row, 1.0, 0.0).astype(BF16)
        return carry

    lax.fori_loop(0, 32, rows, 0)
    for n in range(STEPS):
        value = traces[n : n + 1, :]
        high, low = two_pieces(value)
        high, low = high.astype(F32), low.astype(F32)

        def columns(i, carry):
            number = lax.broadcasted_iota(I32, (16, NREC), 0) + 16 * i
            hit = number == col
            at = pl.multiple_of(16 * i, 16)
            if n == 0:
                pick_y[pl.ds(at, 16), :] = jnp.where(hit, 1.0, 0.0).astype(BF16)
            spread[pl.ds(at, 16), :] = jnp.where(hit, high, 0.0).astype(BF16)
            spread[pl.ds(pl.multiple_of(BY + at, 16), 16), :] = jnp.where(hit, low, 0.0).astype(BF16)
            return carry

        lax.fori_loop(0, 8, columns, 0)
        both = lax.dot_general(
            pick_cell[...], spread[...], (((1,), (1,)), ((), ())), preferred_element_type=F32
        )
        for x in range(BX):
            part = both[NZ * x : NZ * x + NZ]
            inj[n, x] = part[:, :BY] + part[:, BY:]


def forward1_kernel(scal, newer, older, vel, inj, outer, inner, strip, acc, nxt, q, outer_o, inner_o, strip_o, padded, side):
    fill(padded, side, lambda x: newer[x], outer, inner, strip, 0, scal)
    for x in range(BX):
        a = vel[x] * lap(padded, side, x)
        acc[x] = a
        nxt[x] = (2.0 * newer[x] - older[x]) + a
        q[x] = vel[x] * inj[3, x]
    send_edges(lambda x: nxt[x], outer_o, inner_o, strip_o, 0, scal)
    send_edges(lambda x: q[x], outer_o, inner_o, strip_o, 1, scal)


def make_forward(moment):
    def kernel(scal, newer, older, vel, inj, q_in, latest, later, outer, inner, strip,
               acc, nxt, p, q, outer_o, inner_o, strip_o, padded, side):
        fill(padded, side, lambda x: newer[x], outer, inner, strip, 0, scal)
        for x in range(BX):
            a = vel[x] * lap(padded, side, x)
            acc[x] = a
            nxt[x] = (2.0 * newer[x] - older[x]) + a
        send_edges(lambda x: nxt[x], outer_o, inner_o, strip_o, 0, scal)
        fill(padded, side, lambda x: q_in[x], outer, inner, strip, 1, scal)
        for x in range(BX):
            before = 2.0 * inj[3, x] if moment == 1 else 2.0 * later[x] - latest[x]
            value = (before + lap(padded, side, x)) + inj[3 - moment, x]
            p[x] = value
            q[x] = vel[x] * value
        send_edges(lambda x: q[x], outer_o, inner_o, strip_o, 1, scal)

    return kernel


def window(scal, x):
    column = lanes(NZ) + scal[3]
    at_x = scal[2] + x
    inside_x = (at_x >= scal[4]) & (at_x < scal[4] + 48)
    return (column >= scal[5]) & (column < scal[5] + 192) & inside_x


def last_kernel(scal, newer, vel, inj, q_in, latest, later, acc0, acc1, acc2, outer, inner, strip, acc3, grad, padded, side, padded2, side2):
    fill(padded, side, lambda x: newer[x], outer, inner, strip, 0, scal)
    fill(padded2, side2, lambda x: q_in[x], outer, inner, strip, 1, scal)
    for x in range(BX):
        a = vel[x] * lap(padded, side, x)
        acc3[x] = a
        p0 = ((2.0 * later[x] - latest[x]) + lap(padded2, side2, x)) + inj[0, x]
        total = ((a * inj[3, x] + acc2[x] * latest[x]) + acc1[x] * later[x]) + acc0[x] * p0
        grad[pl.ds(x, NZ, stride=8), :] = jnp.where(window(scal, x), total, 0.0)


def gradient_kernel(parts, pre, scaled, copies, dot):
    total = parts[0:32]
    for s in range(1, 16):
        total = total + parts[32 * s : 32 * s + 32]
    value = pre[...] * total
    scaled[...] = value
    for s in range(16):
        copies[32 * s : 32 * s + 32] = value
    product = total * value
    dot[...] = (product[0:8] + product[8:16]) + (product[16:24] + product[24:32])


def born1_kernel(scal, full, acc0, source, d, outer_o, inner_o, strip_o):
    for x in range(BX):
        s = jnp.where(window(scal, x), full[pl.ds(x, NZ, stride=8), :], 0.0)
        source[x] = s
        d[x] = s * acc0[x]
    send_edges(lambda x: d[x], outer_o, inner_o, strip_o, 0, scal)


def make_born(moment, last):
    def kernel(scal, now, before, source, acc, vel, outer, inner, strip, *rest):
        if last:
            pick_cell, pick_y, s1, s2, s3, dot, payload, padded, side, d, pieces, block = rest
        else:
            d, outer_o, inner_o, strip_o, padded, side = rest
        fill(padded, side, lambda x: now[x], outer, inner, strip, 0, scal)
        for x in range(BX):
            base = 2.0 * now[x]
            if moment > 1:
                base = base - before[x]
            d[x] = (base + vel[x] * lap(padded, side, x)) + source[x] * acc[x]
        if not last:
            send_edges(lambda x: d[x], outer_o, inner_o, strip_o, 0, scal)
            return
        s4 = sampled(d, pieces, pick_cell, pick_y)
        energy = jnp.zeros((1, BY), F32)
        for n, values in enumerate((s1[...], s2[...], s3[...], s4)):
            for j in range(16):
                piece = values[:, BY * j : BY * j + BY]
                block[16 * n + j : 16 * n + j + 1, :] = piece
                energy = energy + piece * piece
        block[64:72, :] = jnp.zeros((8, BY), F32)
        block[64:65, :] = energy
        block[65:66, :] = jnp.sum(dot[...], axis=0, keepdims=True)
        for i in range(16):
            payload[i] = block[...]

    return kernel


def sampled(field, pieces, pick_cell, pick_y):
    for x in range(BX):
        high, low = two_pieces(field[x])
        pieces[NZ * x : NZ * x + NZ, :BY] = high
        pieces[NZ * x : NZ * x + NZ, BY:] = low
    at_cell = lax.dot_general(
        pieces[...], pick_cell[...], (((0,), (0,)), ((), ())), preferred_element_type=F32
    )
    chosen = (at_cell[:BY] + at_cell[BY:]) * pick_y[...].astype(F32)
    return jnp.sum(chosen, axis=0, keepdims=True)


def sample_kernel(field, pick_cell, pick_y, out, pieces):
    out[...] = sampled(field, pieces, pick_cell, pick_y)


def exchange(outer, inner, strip):
    chips = [(2 * i + 1, 2 * i + 2) for i in range(3)]
    across = chips + [(b, a) for a, b in chips]
    swap = [(i, i ^ 1) for i in range(8)]
    return (
        lax.ppermute(outer, "gx", across),
        lax.ppermute(inner, "gx", swap),
        lax.ppermute(strip, "gy", [(0, 1), (1, 0)]),
    )


def on_device(older_field, newer_field, velocity, preconditioner, traces,
              receiver_z, receiver_x, receiver_y, aperture_x, aperture_y):
    flat = (NZ * BX, BY)
    gx, gy = lax.axis_index("gx"), lax.axis_index("gy")
    scal = jnp.stack([gx % 2, gy, gx * BX, gy * BY, aperture_x[0], aperture_y[0]]).astype(I32)
    newer, older, *e = call(first_kernel, [FIELD, FIELD] + edges(1))(
        scal, newer_field.reshape(flat), older_field.reshape(flat), smem=1)
    e = exchange(*e)
    vel, inj, pick_cell, pick_y = call(
        prepare_kernel,
        [FIELD, ((4, BX, NZ, BY), F32), ((512, NREC), BF16), ((BY, NREC), BF16)],
        [pltpu.VMEM((2 * BY, NREC), BF16)], limit=40,
    )(scal, velocity.reshape(flat), traces[0], receiver_z, receiver_x, receiver_y, smem=1)
    acc0, u1, q, *e = call(forward1_kernel, [FIELD] * 3 + edges(2), [PADDED, SIDE])(
        scal, newer, older, vel, inj, *e, smem=1)
    e = exchange(*e)
    acc1, u2, p2, q, *e = call(make_forward(1), [FIELD] * 4 + edges(2), [PADDED, SIDE])(
        scal, u1, newer, vel, inj, q, q, q, *e, smem=1)
    e = exchange(*e)
    acc2, u3, p1, q, *e = call(
        make_forward_later, [FIELD] * 4 + edges(2), [PADDED, SIDE])(
        scal, u2, u1, vel, inj, q, p2, *e, smem=1)
    e = exchange(*e)
    acc3, grad = call(last_kernel, [FIELD, (flat, F32)], [PADDED, SIDE, PADDED, SIDE])(
        scal, u3, vel, inj, q, p2, p1, acc0, acc1, acc2, *e, smem=1)
    parts = lax.all_to_all(grad.reshape(16, 4, BX, BY), "shot", 0, 0, tiled=True)
    scaled, copies, dot = call(
        gradient_kernel, [((32, BY), F32), (flat, F32), ((8, BY), F32)])(
        parts.reshape(flat), preconditioner.reshape(32, BY))
    full = lax.all_to_all(copies.reshape(16, 4, BX, BY), "shot", 0, 0, tiled=True)
    source, d1, *e = call(born1_kernel, [FIELD, FIELD] + edges(1))(
        scal, full.reshape(flat), acc0, smem=1)
    e = exchange(*e)
    sample = call(sample_kernel, [((1, NREC), F32)], [pltpu.VMEM((512, 2 * BY), BF16)], flops=600_000_000)
    s1, = sample(d1, pick_cell, pick_y)
    d2, *e = call(make_born(1, False), [FIELD] + edges(1), [PADDED, SIDE])(
        scal, d1, d1, source, acc1, vel, *e, smem=1)
    e = exchange(*e)
    s2, = sample(d2, pick_cell, pick_y)
    d3, *e = call(make_born(2, False), [FIELD] + edges(1), [PADDED, SIDE])(
        scal, d2, d1, source, acc2, vel, *e, smem=1)
    e = exchange(*e)
    s3, = sample(d3, pick_cell, pick_y)
    payload, = call(
        make_born(3, True), [((16, 72, BY), F32)],
        [PADDED, SIDE, pltpu.VMEM((BX, NZ, BY), F32), pltpu.VMEM((512, 2 * BY), BF16), pltpu.VMEM((72, BY), F32)],
    )(scal, d3, d2, source, acc3, vel, *e, pick_cell, pick_y, s1, s2, s3, dot, smem=1)
    arrived = lax.all_to_all(payload, ("gx", "gy"), 0, 0, tiled=True)
    summed = jnp.sum(arrived, axis=0)
    stats = lax.all_to_all(jnp.broadcast_to(summed[None, 64:72], (16, 8, BY)), "shot", 0, 0, tiled=True)
    trace_energy = jnp.sum(stats[:, 0])
    descent_dot = jnp.sum(stats[:, 1])
    step_length = descent_dot / (trace_energy + 1e-6)
    predicted = summed[:64].reshape(4, NREC)
    return (step_length * scaled.reshape(4, BX, BY), (traces[0] - step_length * predicted)[None])


def make_forward_later(scal, newer, older, vel, inj, q_in, later, outer, inner, strip,
                       acc, nxt, p, q, outer_o, inner_o, strip_o, padded, side):
    fill(padded, side, lambda x: newer[x], outer, inner, strip, 0, scal)
    for x in range(BX):
        a = vel[x] * lap(padded, side, x)
        acc[x] = a
        nxt[x] = (2.0 * newer[x] - older[x]) + a
    send_edges(lambda x: nxt[x], outer_o, inner_o, strip_o, 0, scal)
    fill(padded, side, lambda x: q_in[x], outer, inner, strip, 1, scal)
    for x in range(BX):
        value = ((2.0 * later[x] - inj[3, x]) + lap(padded, side, x)) + inj[1, x]
        p[x] = value
        q[x] = vel[x] * value
    send_edges(lambda x: q[x], outer_o, inner_o, strip_o, 1, scal)


def solution(mesh):
    return jax.shard_map(
        on_device,
        mesh=mesh,
        in_specs=(
            P("shot", None, "gx", "gy"),
            P("shot", None, "gx", "gy"),
            P(None, "gx", "gy"),
            P("shot", "gx", "gy"),
            P("shot", None, None),
            P("shot", None),
            P("shot", None),
            P("shot", None),
            P("shot"),
            P("shot"),
        ),
        out_specs=(P("shot", "gx", "gy"), P("shot", None, None)),
        check_vma=False,
    )
```

```python
import jax
import jax.numpy as jnp
from jax import lax
from jax.experimental import pallas as pl
from jax.experimental.pallas import tpu as pltpu
from jax.sharding import PartitionSpec as P

STEPS = 4
NZ, BX, BY = 64, 8, 128
NREC = 2048
F32, BF16, I32 = jnp.float32, jnp.bfloat16, jnp.int32
weights = (-205.0 / 72.0, 8.0 / 5.0, -1.0 / 5.0, 8.0 / 315.0, -1.0 / 560.0)


def call(kernel, outs, scratch=(), limit=24, flops=10_000_000):
    def run(*args, smem=0, hbm=0):
        spaces = [pltpu.SMEM] * smem + [pltpu.HBM] * hbm
        spaces = spaces + [pltpu.VMEM] * (len(args) - smem - hbm)
        specs = [pl.BlockSpec(memory_space=space) for space in spaces]
        return pl.pallas_call(
            kernel,
            out_shape=[jax.ShapeDtypeStruct(s, d) for s, d in outs],
            in_specs=specs,
            out_specs=[pl.BlockSpec(memory_space=pltpu.VMEM) for _ in outs],
            scratch_shapes=list(scratch),
            compiler_params=pltpu.CompilerParams(vmem_limit_bytes=limit * 1024 * 1024),
            cost_estimate=pl.CostEstimate(
                flops=flops, bytes_accessed=2_000_000, transcendentals=0
            ),
        )(*args)

    return run


def lanes(rows):
    return lax.broadcasted_iota(I32, (rows, BY), 1)


def near_edge(gy, lane):
    return ((gy == 0) & (lane >= BY - 4)) | ((gy == 1) & (lane < 4))


def far_edge(gy, lane):
    return ((gy == 0) & (lane < 4)) | ((gy == 1) & (lane >= BY - 4))


def send_edges(load, outer_ref, inner_ref, strip_ref, slot, scal):
    core, gy = scal[0], scal[1]
    keep = near_edge(gy, lanes(8))
    for i in range(4):
        outer_ref[slot, i] = load(4 * core + i)
        inner_ref[slot, i] = load(4 * (1 - core) + i)
    for half in range(2):
        packed = jnp.zeros((8, BY), F32)
        for j in range(32):
            index = half * 32 + j
            plane = load(index // 8)[8 * (index % 8) : 8 * (index % 8) + 8]
            packed = packed + pltpu.roll(jnp.where(keep, plane, 0.0), 4 * j, 1)
        strip_ref[slot, 8 * half : 8 * half + 8] = packed


def fill(padded, side, load, outer_ref, inner_ref, strip_ref, slot, scal):
    core, gy = scal[0], scal[1]
    keep = far_edge(gy, lanes(8))
    zero = jnp.zeros((8, BY), F32)
    for x in range(BX):
        padded[4 + x, 0:8] = zero
        padded[4 + x, 72:80] = zero
        padded[4 + x, 8:72] = load(x)
    inside = ((scal[2] > 0) | (core == 1)) & ((scal[2] < 7 * BX) | (core == 0))
    for i in range(4):
        padded[12 * core + i, 8:72] = jnp.where(inside, outer_ref[slot, i], 0.0)
        padded[12 * (1 - core) + i, 8:72] = inner_ref[slot, i]
    for half in range(2):
        packed = strip_ref[slot, 8 * half : 8 * half + 8]
        for j in range(32):
            index = half * 32 + j
            turned = pltpu.roll(packed, (BY - 4 * j) % BY, 1)
            side[index // 8, 8 * (index % 8) : 8 * (index % 8) + 8] = jnp.where(keep, turned, 0.0)


def lap(padded, side, x):
    lane = lanes(NZ)
    centre = padded[4 + x, 8:72]
    other = side[x]
    result = (3.0 * weights[0]) * centre
    for k in range(1, 5):
        along_z = padded[4 + x, 8 + k : 72 + k] + padded[4 + x, 8 - k : 72 - k]
        along_x = padded[4 + x + k, 8:72] + padded[4 + x - k, 8:72]
        right = pltpu.roll(jnp.where(lane < k, other, centre), BY - k, 1)
        left = pltpu.roll(jnp.where(lane >= BY - k, other, centre), k, 1)
        result = result + weights[k] * ((along_z + along_x) + (right + left))
    return result


FIELD = ((BX, NZ, BY), F32)
PADDED = pltpu.VMEM((16, 80, BY), F32)
SIDE = pltpu.VMEM((BX, NZ, BY), F32)


def edges(count):
    return [((count, 4, NZ, BY), F32), ((count, 4, NZ, BY), F32), ((count, 16, BY), F32)]


def first_kernel(scal, newer, newer_out, outer, inner, strip, raw, sem):
    copies = [
        pltpu.make_async_copy(newer.at[pl.ds(128 * i, 128)], raw.at[pl.ds(128 * i, 128)], sem.at[i])
        for i in range(4)
    ]
    for copy in copies:
        copy.start()
    for copy in copies:
        copy.wait()
    for x in range(BX):
        newer_out[x] = raw[pl.ds(x, NZ, stride=8), :]
    send_edges(lambda x: newer_out[x], outer, inner, strip, 0, scal)


def two_pieces(values):
    high = values.astype(BF16)
    return high, (values - high.astype(F32)).astype(BF16)


def prepare_kernel(scal, rz_in, rx_in, ry_in, traces_in, vel_in, older_in,
                   vel_out, older_out, inj, pick_cell, pick_y,
                   rz, rx, ry, traces, vel, older, at_depth, spread, sem):
    copies = [
        pltpu.make_async_copy(source, target, sem.at[i])
        for i, (source, target) in enumerate(
            ((rz_in, rz), (rx_in, rx), (ry_in, ry), (traces_in, traces), (vel_in, vel), (older_in, older))
        )
    ]
    for copy in copies:
        copy.start()
    for copy in copies[:4]:
        copy.wait()
    lat_x = rx[...] - scal[2]
    lat_y = ry[...] - scal[3]
    present = (lat_x >= 0) & (lat_x < BX) & (lat_y >= 0) & (lat_y < BY)
    depth = jnp.where(present, rz[...], -1)
    col = jnp.where(present, lat_y, -1)

    def block(i):
        return pl.ds(pl.multiple_of(16 * i, 16), 16)

    def wide(row):
        return jnp.broadcast_to(row, (16, NREC)).astype(BF16)

    def hits(i, wanted):
        number = lax.broadcasted_iota(I32, (16, NREC), 0) + 16 * i
        return jnp.where(number == wanted, 1.0, 0.0).astype(BF16)

    def depths(i, carry):
        at_depth[block(i), :] = hits(i, depth)
        return carry

    lax.fori_loop(0, 4, depths, 0)

    def planes(x, carry):
        here = wide(jnp.where(lat_x == x, 1.0, 0.0))
        for i in range(4):
            pick_cell[block(4 * x + i), :] = at_depth[16 * i : 16 * i + 16] * here
        return carry

    lax.fori_loop(0, BX, planes, 0)

    def columns(i, carry):
        pick_y[block(i), :] = hits(i, col)
        return carry

    lax.fori_loop(0, 8, columns, 0)
    for n in range(STEPS):
        value = traces[n : n + 1, :]
        coarse = value.astype(BF16).astype(F32)
        high, low = wide(coarse), wide(value - coarse)

        def weigh(i, carry):
            picked = pick_y[block(i), :]
            spread[block(i), :] = picked * high
            spread[block(8 + i), :] = picked * low
            return carry

        lax.fori_loop(0, 8, weigh, 0)
        both = lax.dot_general(
            pick_cell[...], spread[...], (((1,), (1,)), ((), ())), preferred_element_type=F32
        )
        for x in range(BX):
            part = both[NZ * x : NZ * x + NZ]
            inj[n, x] = part[:, :BY] + part[:, BY:]
    for copy in copies[4:]:
        copy.wait()
    for x in range(BX):
        vel_out[x] = vel[pl.ds(x, NZ, stride=8), :]
        older_out[x] = older[pl.ds(x, NZ, stride=8), :]


def forward1_kernel(scal, newer, older, vel, inj, outer, inner, strip, acc, nxt, q, outer_o, inner_o, strip_o, padded, side):
    fill(padded, side, lambda x: newer[x], outer, inner, strip, 0, scal)
    for x in range(BX):
        a = vel[x] * lap(padded, side, x)
        acc[x] = a
        nxt[x] = (2.0 * newer[x] - older[x]) + a
        q[x] = vel[x] * inj[3, x]
    send_edges(lambda x: nxt[x], outer_o, inner_o, strip_o, 0, scal)
    send_edges(lambda x: q[x], outer_o, inner_o, strip_o, 1, scal)


def make_forward(moment):
    def kernel(scal, newer, older, vel, inj, q_in, latest, later, outer, inner, strip,
               acc, nxt, p, q, outer_o, inner_o, strip_o, padded, side):
        fill(padded, side, lambda x: newer[x], outer, inner, strip, 0, scal)
        for x in range(BX):
            a = vel[x] * lap(padded, side, x)
            acc[x] = a
            nxt[x] = (2.0 * newer[x] - older[x]) + a
        send_edges(lambda x: nxt[x], outer_o, inner_o, strip_o, 0, scal)
        fill(padded, side, lambda x: q_in[x], outer, inner, strip, 1, scal)
        for x in range(BX):
            before = 2.0 * inj[3, x] if moment == 1 else 2.0 * later[x] - latest[x]
            value = (before + lap(padded, side, x)) + inj[3 - moment, x]
            p[x] = value
            q[x] = vel[x] * value
        send_edges(lambda x: q[x], outer_o, inner_o, strip_o, 1, scal)

    return kernel


def window(scal, x):
    column = lanes(NZ) + scal[3]
    at_x = scal[2] + x
    inside_x = (at_x >= scal[4]) & (at_x < scal[4] + 48)
    return (column >= scal[5]) & (column < scal[5] + 192) & inside_x


def last_kernel(scal, newer, vel, inj, q_in, latest, later, acc0, acc1, acc2, outer, inner, strip, acc3, grad, padded, side, padded2, side2):
    fill(padded, side, lambda x: newer[x], outer, inner, strip, 0, scal)
    fill(padded2, side2, lambda x: q_in[x], outer, inner, strip, 1, scal)
    for x in range(BX):
        a = vel[x] * lap(padded, side, x)
        acc3[x] = a
        p0 = ((2.0 * later[x] - latest[x]) + lap(padded2, side2, x)) + inj[0, x]
        total = ((a * inj[3, x] + acc2[x] * latest[x]) + acc1[x] * later[x]) + acc0[x] * p0
        grad[pl.ds(x, NZ, stride=8), :] = jnp.where(window(scal, x), total, 0.0)


def gradient_kernel(parts, pre, scaled, copies, dot):
    total = parts[0:32]
    for s in range(1, 16):
        total = total + parts[32 * s : 32 * s + 32]
    value = pre[...] * total
    scaled[...] = value
    for s in range(16):
        copies[32 * s : 32 * s + 32] = value
    product = total * value
    dot[...] = (product[0:8] + product[8:16]) + (product[16:24] + product[24:32])


def born1_kernel(scal, full, acc0, source, d, outer_o, inner_o, strip_o):
    for x in range(BX):
        s = jnp.where(window(scal, x), full[pl.ds(x, NZ, stride=8), :], 0.0)
        source[x] = s
        d[x] = s * acc0[x]
    send_edges(lambda x: d[x], outer_o, inner_o, strip_o, 0, scal)


def make_born(moment, last):
    def kernel(scal, now, before, source, acc, vel, outer, inner, strip, *rest):
        if last:
            pick_cell, pick_y, s1, s2, s3, dot, block, padded, side, d, pieces = rest
        else:
            d, outer_o, inner_o, strip_o, padded, side = rest
        fill(padded, side, lambda x: now[x], outer, inner, strip, 0, scal)
        for x in range(BX):
            base = 2.0 * now[x]
            if moment > 1:
                base = base - before[x]
            d[x] = (base + vel[x] * lap(padded, side, x)) + source[x] * acc[x]
        if not last:
            send_edges(lambda x: d[x], outer_o, inner_o, strip_o, 0, scal)
            return
        s4 = sampled(d, pieces, pick_cell, pick_y)
        energy = jnp.zeros((1, BY), F32)
        for n, values in enumerate((s1[...], s2[...], s3[...], s4)):
            for j in range(16):
                piece = values[:, BY * j : BY * j + BY]
                block[16 * n + j : 16 * n + j + 1, :] = piece
                energy = energy + piece * piece
        block[64:72, :] = jnp.zeros((8, BY), F32)
        block[64:65, :] = energy
        block[65:66, :] = jnp.sum(dot[...], axis=0, keepdims=True)

    return kernel


def sampled(field, pieces, pick_cell, pick_y):
    for x in range(BX):
        high, low = two_pieces(field[x])
        pieces[NZ * x : NZ * x + NZ, :BY] = high
        pieces[NZ * x : NZ * x + NZ, BY:] = low
    at_cell = lax.dot_general(
        pieces[...], pick_cell[...], (((0,), (0,)), ((), ())), preferred_element_type=F32
    )
    chosen = (at_cell[:BY] + at_cell[BY:]) * pick_y[...].astype(F32)
    return jnp.sum(chosen, axis=0, keepdims=True)


def sample_kernel(field, pick_cell, pick_y, out, pieces):
    out[...] = sampled(field, pieces, pick_cell, pick_y)


def pair_kernel(mine, theirs, copies):
    total = mine[...] + theirs[...]
    for i in range(8):
        copies[i] = total


def collect_kernel(arrived, predicted, copies):
    total = arrived[0]
    for i in range(1, 8):
        total = total + arrived[i]
    predicted[...] = total[0:64]
    for i in range(16):
        copies[i] = total[64:72]


def finish_kernel(stats, predicted, scaled, traces, image, residual):
    total = stats[0]
    for i in range(1, 16):
        total = total + stats[i]
    energy = jnp.sum(total[0:1], axis=1, keepdims=True)
    dot = jnp.sum(total[1:2], axis=1, keepdims=True)
    step = dot / (energy + 1e-6)
    image[...] = step * scaled[...]
    for n in range(STEPS):
        for j in range(16):
            at = pl.ds(BY * j, BY)
            row = predicted[16 * n + j : 16 * n + j + 1, :]
            residual[n : n + 1, at] = traces[n : n + 1, at] - step * row


def exchange(outer, inner, strip):
    chips = [(2 * i + 1, (2 * i + 2) % 8) for i in range(4)]
    across = chips + [(b, a) for a, b in chips]
    swap = [(i, i ^ 1) for i in range(8)]
    return (
        lax.ppermute(outer, "gx", across),
        lax.ppermute(inner, "gx", swap),
        lax.ppermute(strip, "gy", [(0, 1), (1, 0)]),
    )


def on_device(older_field, newer_field, velocity, preconditioner, traces,
              receiver_z, receiver_x, receiver_y, aperture_x, aperture_y):
    flat = (NZ * BX, BY)
    gx, gy = lax.axis_index("gx"), lax.axis_index("gy")
    scal = jnp.stack([gx % 2, gy, gx * BX, gy * BY, aperture_x[0], aperture_y[0]]).astype(I32)
    newer, *e = call(
        first_kernel, [FIELD] + edges(1), [pltpu.VMEM(flat, F32), pltpu.SemaphoreType.DMA((4,))]
    )(scal, newer_field.reshape(flat), smem=1, hbm=1)
    e = exchange(*e)
    vel, older, inj, pick_cell, pick_y = call(
        prepare_kernel,
        [FIELD, FIELD, ((4, BX, NZ, BY), F32), ((512, NREC), BF16), ((BY, NREC), BF16)],
        [pltpu.VMEM((1, NREC), I32)] * 3
        + [
            pltpu.VMEM((4, NREC), F32),
            pltpu.VMEM(flat, F32),
            pltpu.VMEM(flat, F32),
            pltpu.VMEM((NZ, NREC), BF16),
            pltpu.VMEM((2 * BY, NREC), BF16),
            pltpu.SemaphoreType.DMA((6,)),
        ],
        limit=40,
    )(scal, receiver_z, receiver_x, receiver_y, traces[0], velocity.reshape(flat),
      older_field.reshape(flat), smem=1, hbm=6)
    acc0, u1, q, *e = call(forward1_kernel, [FIELD] * 3 + edges(2), [PADDED, SIDE])(
        scal, newer, older, vel, inj, *e, smem=1)
    e = exchange(*e)
    acc1, u2, p2, q, *e = call(make_forward(1), [FIELD] * 4 + edges(2), [PADDED, SIDE])(
        scal, u1, newer, vel, inj, q, q, q, *e, smem=1)
    e = exchange(*e)
    acc2, u3, p1, q, *e = call(
        forward2_kernel, [FIELD] * 4 + edges(2), [PADDED, SIDE])(
        scal, u2, u1, vel, inj, q, p2, *e, smem=1)
    e = exchange(*e)
    acc3, grad = call(last_kernel, [FIELD, (flat, F32)], [PADDED, SIDE, PADDED, SIDE])(
        scal, u3, vel, inj, q, p2, p1, acc0, acc1, acc2, *e, smem=1)
    parts = lax.all_to_all(grad.reshape(16, 4, BX, BY), "shot", 0, 0, tiled=True)
    scaled, copies, dot = call(
        gradient_kernel, [((32, BY), F32), (flat, F32), ((8, BY), F32)])(
        parts.reshape(flat), preconditioner.reshape(32, BY))
    full = lax.all_to_all(copies.reshape(16, 4, BX, BY), "shot", 0, 0, tiled=True)
    source, d1, *e = call(born1_kernel, [FIELD, FIELD] + edges(1))(
        scal, full.reshape(flat), acc0, smem=1)
    e = exchange(*e)
    sample = call(sample_kernel, [((1, NREC), F32)], [pltpu.VMEM((512, 2 * BY), BF16)], flops=600_000_000)
    s1, = sample(d1, pick_cell, pick_y)
    d2, *e = call(make_born(1, False), [FIELD] + edges(1), [PADDED, SIDE])(
        scal, d1, d1, source, acc1, vel, *e, smem=1)
    e = exchange(*e)
    s2, = sample(d2, pick_cell, pick_y)
    d3, *e = call(make_born(2, False), [FIELD] + edges(1), [PADDED, SIDE])(
        scal, d2, d1, source, acc2, vel, *e, smem=1)
    e = exchange(*e)
    s3, = sample(d3, pick_cell, pick_y)
    block, = call(
        make_born(3, True), [((72, BY), F32)],
        [PADDED, SIDE, pltpu.VMEM((BX, NZ, BY), F32), pltpu.VMEM((512, 2 * BY), BF16)],
    )(scal, d3, d2, source, acc3, vel, *e, pick_cell, pick_y, s1, s2, s3, dot, smem=1)
    theirs = lax.ppermute(block, "gx", [(i, i ^ 1) for i in range(8)])
    payload, = call(pair_kernel, [((8, 72, BY), F32)])(block, theirs)
    same_core = [[2 * (2 * c + k) + g for c in range(4) for g in range(2)] for k in range(2)]
    arrived = lax.all_to_all(payload, ("gx", "gy"), 0, 0, axis_index_groups=same_core, tiled=True)
    predicted, stats = call(collect_kernel, [((64, BY), F32), ((16, 8, BY), F32)])(arrived)
    stats = lax.all_to_all(stats, "shot", 0, 0, tiled=True)
    image, residual = call(finish_kernel, [((32, BY), F32), ((4, NREC), F32)])(
        stats, predicted, scaled, traces[0])
    return image.reshape(4, BX, BY), residual[None]


def forward2_kernel(scal, newer, older, vel, inj, q_in, later, outer, inner, strip,
                       acc, nxt, p, q, outer_o, inner_o, strip_o, padded, side):
    fill(padded, side, lambda x: newer[x], outer, inner, strip, 0, scal)
    for x in range(BX):
        a = vel[x] * lap(padded, side, x)
        acc[x] = a
        nxt[x] = (2.0 * newer[x] - older[x]) + a
    send_edges(lambda x: nxt[x], outer_o, inner_o, strip_o, 0, scal)
    fill(padded, side, lambda x: q_in[x], outer, inner, strip, 1, scal)
    for x in range(BX):
        value = ((2.0 * later[x] - inj[3, x]) + lap(padded, side, x)) + inj[1, x]
        p[x] = value
        q[x] = vel[x] * value
    send_edges(lambda x: q[x], outer_o, inner_o, strip_o, 1, scal)


def solution(mesh):
    return jax.shard_map(
        on_device,
        mesh=mesh,
        in_specs=(
            P("shot", None, "gx", "gy"),
            P("shot", None, "gx", "gy"),
            P(None, "gx", "gy"),
            P("shot", "gx", "gy"),
            P("shot", None, None),
            P("shot", None),
            P("shot", None),
            P("shot", None),
            P("shot"),
            P("shot"),
        ),
        out_specs=(P("shot", "gx", "gy"), P("shot", None, None)),
        check_vma=False,
    )
```

```python
import jax
import jax.numpy as jnp
from jax import lax
from jax.experimental import pallas as pl
from jax.experimental.pallas import tpu as pltpu
from jax.sharding import PartitionSpec as P

STEPS = 4
NZ, BX, BY = 64, 8, 128
NREC = 2048
F32, BF16, I32 = jnp.float32, jnp.bfloat16, jnp.int32
weights = (-205.0 / 72.0, 8.0 / 5.0, -1.0 / 5.0, 8.0 / 315.0, -1.0 / 560.0)


def call(kernel, outs, scratch=(), limit=24, flops=10_000_000):
    def run(*args, smem=0, hbm=0):
        spaces = [pltpu.SMEM] * smem + [pltpu.HBM] * hbm
        spaces = spaces + [pltpu.VMEM] * (len(args) - smem - hbm)
        specs = [pl.BlockSpec(memory_space=space) for space in spaces]
        return pl.pallas_call(
            kernel,
            out_shape=[jax.ShapeDtypeStruct(s, d) for s, d in outs],
            in_specs=specs,
            out_specs=[pl.BlockSpec(memory_space=pltpu.VMEM) for _ in outs],
            scratch_shapes=list(scratch),
            compiler_params=pltpu.CompilerParams(vmem_limit_bytes=limit * 1024 * 1024),
            cost_estimate=pl.CostEstimate(
                flops=flops, bytes_accessed=2_000_000, transcendentals=0
            ),
        )(*args)

    return run


def lanes(rows):
    return lax.broadcasted_iota(I32, (rows, BY), 1)


def near_edge(gy, lane):
    return ((gy == 0) & (lane >= BY - 4)) | ((gy == 1) & (lane < 4))


def far_edge(gy, lane):
    return ((gy == 0) & (lane < 4)) | ((gy == 1) & (lane >= BY - 4))


def send_edges(load, outer_ref, inner_ref, strip_ref, slot, scal):
    core, gy = scal[0], scal[1]
    keep = near_edge(gy, lanes(8))
    for i in range(4):
        outer_ref[slot, i] = load(4 * core + i)
        inner_ref[slot, i] = load(4 * (1 - core) + i)
    for half in range(2):
        packed = jnp.zeros((8, BY), F32)
        for j in range(32):
            index = half * 32 + j
            plane = load(index // 8)[8 * (index % 8) : 8 * (index % 8) + 8]
            packed = packed + pltpu.roll(jnp.where(keep, plane, 0.0), 4 * j, 1)
        strip_ref[slot, 8 * half : 8 * half + 8] = packed


def fill(padded, side, load, outer_ref, inner_ref, strip_ref, slot, scal):
    core, gy = scal[0], scal[1]
    keep = far_edge(gy, lanes(8))
    zero = jnp.zeros((8, BY), F32)
    for x in range(BX):
        padded[4 + x, 0:8] = zero
        padded[4 + x, 72:80] = zero
        padded[4 + x, 8:72] = load(x)
    inside = ((scal[2] > 0) | (core == 1)) & ((scal[2] < 7 * BX) | (core == 0))
    for i in range(4):
        padded[12 * core + i, 8:72] = jnp.where(inside, outer_ref[slot, i], 0.0)
        padded[12 * (1 - core) + i, 8:72] = inner_ref[slot, i]
    for half in range(2):
        packed = strip_ref[slot, 8 * half : 8 * half + 8]
        for j in range(32):
            index = half * 32 + j
            turned = pltpu.roll(packed, (BY - 4 * j) % BY, 1)
            side[index // 8, 8 * (index % 8) : 8 * (index % 8) + 8] = jnp.where(keep, turned, 0.0)


def lap(padded, side, x):
    lane = lanes(NZ)
    centre = padded[4 + x, 8:72]
    other = side[x]
    result = (3.0 * weights[0]) * centre
    for k in range(1, 5):
        along_z = padded[4 + x, 8 + k : 72 + k] + padded[4 + x, 8 - k : 72 - k]
        along_x = padded[4 + x + k, 8:72] + padded[4 + x - k, 8:72]
        right = pltpu.roll(jnp.where(lane < k, other, centre), BY - k, 1)
        left = pltpu.roll(jnp.where(lane >= BY - k, other, centre), k, 1)
        result = result + weights[k] * ((along_z + along_x) + (right + left))
    return result


FIELD = ((BX, NZ, BY), F32)
PADDED = pltpu.VMEM((16, 80, BY), F32)
SIDE = pltpu.VMEM((BX, NZ, BY), F32)


def edges(count):
    return [((count, 4, NZ, BY), F32), ((count, 4, NZ, BY), F32), ((count, 16, BY), F32)]


def first_kernel(scal, newer, newer_out, outer, inner, strip):
    for x in range(BX):
        newer_out[x] = newer[pl.ds(x, NZ, stride=8), :]
    send_edges(lambda x: newer_out[x], outer, inner, strip, 0, scal)


def two_pieces(values):
    high = values.astype(BF16)
    return high, (values - high.astype(F32)).astype(BF16)


def block(i):
    return pl.ds(pl.multiple_of(16 * i, 16), 16)


def wide(row):
    return jnp.broadcast_to(row, (16, NREC)).astype(BF16)


def inject(n, traces, pick_cell, pick_y, spread, inj, slot=0):
    value = traces[n : n + 1, :]
    coarse = value.astype(BF16).astype(F32)
    high, low = wide(coarse), wide(value - coarse)

    def weigh(i, carry):
        picked = pick_y[block(i), :]
        spread[block(i), :] = picked * high
        spread[block(8 + i), :] = picked * low
        return carry

    lax.fori_loop(0, 8, weigh, 0)
    both = lax.dot_general(
        pick_cell[...], spread[...], (((1,), (1,)), ((), ())), preferred_element_type=F32
    )
    for x in range(BX):
        part = both[NZ * x : NZ * x + NZ]
        inj[slot, x] = part[:, :BY] + part[:, BY:]


def inject_kernel(shot, pick_cell, pick_y, inj, spread):
    for n in range(3):
        inject(n, shot, pick_cell, pick_y, spread, inj, n)


def prepare_kernel(scal, shot, inj, pick_cell, pick_y, at_depth, spread):
    code = shot[4:5, :].astype(I32)
    lat_x = ((code >> 6) & 63) - scal[2]
    lat_y = (code >> 12) - scal[3]
    present = (lat_x >= 0) & (lat_x < BX) & (lat_y >= 0) & (lat_y < BY)
    depth = jnp.where(present, code & 63, -1)
    col = jnp.where(present, lat_y, -1)

    def hits(i, wanted):
        number = lax.broadcasted_iota(I32, (16, NREC), 0) + 16 * i
        return jnp.where(number == wanted, 1.0, 0.0).astype(BF16)

    def depths(i, carry):
        at_depth[block(i), :] = hits(i, depth)
        return carry

    lax.fori_loop(0, 4, depths, 0)

    def planes(x, carry):
        here = wide(jnp.where(lat_x == x, 1.0, 0.0))
        for i in range(4):
            pick_cell[block(4 * x + i), :] = at_depth[16 * i : 16 * i + 16] * here
        return carry

    lax.fori_loop(0, BX, planes, 0)

    def columns(i, carry):
        pick_y[block(i), :] = hits(i, col)
        return carry

    lax.fori_loop(0, 8, columns, 0)
    inject(3, shot, pick_cell, pick_y, spread, inj)


def planes_kernel(older_in, vel_in, older, vel):
    for x in range(BX):
        older[x] = older_in[pl.ds(x, NZ, stride=8), :]
        vel[x] = vel_in[pl.ds(x, NZ, stride=8), :]


def forward1_kernel(scal, newer, older, vel, inj3, outer, inner, strip, acc, nxt, q, outer_o, inner_o, strip_o, padded, side):
    fill(padded, side, lambda x: newer[x], outer, inner, strip, 0, scal)
    for x in range(BX):
        a = vel[x] * lap(padded, side, x)
        acc[x] = a
        nxt[x] = (2.0 * newer[x] - older[x]) + a
        q[x] = vel[x] * inj3[0, x]
    send_edges(lambda x: nxt[x], outer_o, inner_o, strip_o, 0, scal)
    send_edges(lambda x: q[x], outer_o, inner_o, strip_o, 1, scal)


def make_forward(moment):
    def kernel(scal, newer, older, vel, inj, inj3, q_in, *rest):
        if moment == 2:
            later, rest = rest[0], rest[1:]
        outer, inner, strip, acc, nxt, p, q, outer_o, inner_o, strip_o, padded, side = rest
        fill(padded, side, lambda x: newer[x], outer, inner, strip, 0, scal)
        for x in range(BX):
            a = vel[x] * lap(padded, side, x)
            acc[x] = a
            nxt[x] = (2.0 * newer[x] - older[x]) + a
        send_edges(lambda x: nxt[x], outer_o, inner_o, strip_o, 0, scal)
        fill(padded, side, lambda x: q_in[x], outer, inner, strip, 1, scal)
        for x in range(BX):
            before = 2.0 * inj3[0, x] if moment == 1 else 2.0 * later[x] - inj3[0, x]
            value = (before + lap(padded, side, x)) + inj[3 - moment, x]
            p[x] = value
            q[x] = vel[x] * value
        send_edges(lambda x: q[x], outer_o, inner_o, strip_o, 1, scal)

    return kernel


def window(scal, x):
    column = lanes(NZ) + scal[3]
    at_x = scal[2] + x
    inside_x = (at_x >= scal[4]) & (at_x < scal[4] + 48)
    return (column >= scal[5]) & (column < scal[5] + 192) & inside_x


def last_kernel(scal, newer, vel, inj, inj3, q_in, latest, later, acc0, acc1, acc2, outer, inner, strip, acc3, grad, padded, side, padded2, side2):
    fill(padded, side, lambda x: newer[x], outer, inner, strip, 0, scal)
    fill(padded2, side2, lambda x: q_in[x], outer, inner, strip, 1, scal)
    for x in range(BX):
        a = vel[x] * lap(padded, side, x)
        acc3[x] = a
        p0 = ((2.0 * later[x] - latest[x]) + lap(padded2, side2, x)) + inj[0, x]
        total = ((a * inj3[0, x] + acc2[x] * latest[x]) + acc1[x] * later[x]) + acc0[x] * p0
        grad[pl.ds(x, NZ, stride=8), :] = jnp.where(window(scal, x), total, 0.0)


def gradient_kernel(parts, pre, scaled, copies, dot):
    total = parts[0:32]
    for s in range(1, 16):
        total = total + parts[32 * s : 32 * s + 32]
    value = pre[...] * total
    scaled[...] = value
    for s in range(16):
        copies[32 * s : 32 * s + 32] = value
    product = total * value
    dot[...] = (product[0:8] + product[8:16]) + (product[16:24] + product[24:32])


def born1_kernel(scal, full, acc0, source, d, outer_o, inner_o, strip_o):
    for x in range(BX):
        s = jnp.where(window(scal, x), full[pl.ds(x, NZ, stride=8), :], 0.0)
        source[x] = s
        d[x] = s * acc0[x]
    send_edges(lambda x: d[x], outer_o, inner_o, strip_o, 0, scal)


def make_born(moment, last):
    def kernel(scal, now, before, source, acc, vel, outer, inner, strip, *rest):
        if last:
            pick_cell, pick_y, s1, s2, s3, dot, block, padded, side, d, pieces = rest
        else:
            d, outer_o, inner_o, strip_o, padded, side = rest
        fill(padded, side, lambda x: now[x], outer, inner, strip, 0, scal)
        for x in range(BX):
            base = 2.0 * now[x]
            if moment > 1:
                base = base - before[x]
            d[x] = (base + vel[x] * lap(padded, side, x)) + source[x] * acc[x]
        if not last:
            send_edges(lambda x: d[x], outer_o, inner_o, strip_o, 0, scal)
            return
        s4 = sampled(d, pieces, pick_cell, pick_y)
        energy = jnp.zeros((1, BY), F32)
        for n, values in enumerate((s1[...], s2[...], s3[...], s4)):
            for j in range(16):
                piece = values[:, BY * j : BY * j + BY]
                block[16 * n + j : 16 * n + j + 1, :] = piece
                energy = energy + piece * piece
        block[64:72, :] = jnp.zeros((8, BY), F32)
        block[64:65, :] = energy
        block[65:66, :] = jnp.sum(dot[...], axis=0, keepdims=True)

    return kernel


def sampled(field, pieces, pick_cell, pick_y):
    for x in range(BX):
        high, low = two_pieces(field[x])
        pieces[NZ * x : NZ * x + NZ, :BY] = high
        pieces[NZ * x : NZ * x + NZ, BY:] = low
    at_cell = lax.dot_general(
        pieces[...], pick_cell[...], (((0,), (0,)), ((), ())), preferred_element_type=F32
    )
    chosen = (at_cell[:BY] + at_cell[BY:]) * pick_y[...].astype(F32)
    return jnp.sum(chosen, axis=0, keepdims=True)


def sample_kernel(field, pick_cell, pick_y, out, pieces):
    out[...] = sampled(field, pieces, pick_cell, pick_y)


def pair_kernel(mine, theirs, copies):
    total = mine[...] + theirs[...]
    for i in range(8):
        copies[i] = total


def collect_kernel(arrived, predicted, copies):
    total = arrived[0]
    for i in range(1, 8):
        total = total + arrived[i]
    predicted[...] = total[0:64]
    for i in range(16):
        copies[i] = total[64:72]


def finish_kernel(stats, predicted, scaled, traces, image, residual):
    total = stats[0]
    for i in range(1, 16):
        total = total + stats[i]
    energy = jnp.sum(total[0:1], axis=1, keepdims=True)
    dot = jnp.sum(total[1:2], axis=1, keepdims=True)
    step = dot / (energy + 1e-6)
    image[...] = step * scaled[...]
    for n in range(STEPS):
        for j in range(16):
            at = pl.ds(BY * j, BY)
            row = predicted[16 * n + j : 16 * n + j + 1, :]
            residual[n : n + 1, at] = traces[n : n + 1, at] - step * row


def exchange(outer, inner, strip):
    chips = [(2 * i + 1, (2 * i + 2) % 8) for i in range(4)]
    across = chips + [(b, a) for a, b in chips]
    swap = [(i, i ^ 1) for i in range(8)]
    return (
        lax.ppermute(outer, "gx", across),
        lax.ppermute(inner, "gx", swap),
        lax.ppermute(strip, "gy", [(0, 1), (1, 0)]),
    )


def on_device(older_field, newer_field, velocity, preconditioner, traces,
              receiver_z, receiver_x, receiver_y, aperture_x, aperture_y):
    flat = (NZ * BX, BY)
    gx, gy = lax.axis_index("gx"), lax.axis_index("gy")
    scal = jnp.stack([gx % 2, gy, gx * BX, gy * BY, aperture_x[0], aperture_y[0]]).astype(I32)
    newer, *e = call(first_kernel, [FIELD] + edges(1))(scal, newer_field.reshape(flat), smem=1)
    e = exchange(*e)
    code = receiver_z | (receiver_x << 6) | (receiver_y << 12)
    shot = jnp.concatenate([traces[0], code.astype(F32)], axis=0)
    inj3, pick_cell, pick_y = call(
        prepare_kernel,
        [((1, BX, NZ, BY), F32), ((512, NREC), BF16), ((BY, NREC), BF16)],
        [pltpu.VMEM((NZ, NREC), BF16), pltpu.VMEM((2 * BY, NREC), BF16)],
    )(scal, shot, smem=1)
    older, vel = call(planes_kernel, [FIELD, FIELD])(older_field.reshape(flat), velocity.reshape(flat))
    acc0, u1, q, *e = call(forward1_kernel, [FIELD] * 3 + edges(2), [PADDED, SIDE])(
        scal, newer, older, vel, inj3, *e, smem=1)
    e = exchange(*e)
    inj, = call(inject_kernel, [((3, BX, NZ, BY), F32)], [pltpu.VMEM((2 * BY, NREC), BF16)], flops=2_000_000_000)(
        shot, pick_cell, pick_y)
    acc1, u2, p2, q, *e = call(make_forward(1), [FIELD] * 4 + edges(2), [PADDED, SIDE])(
        scal, u1, newer, vel, inj, inj3, q, *e, smem=1)
    e = exchange(*e)
    acc2, u3, p1, q, *e = call(
        make_forward(2), [FIELD] * 4 + edges(2), [PADDED, SIDE])(
        scal, u2, u1, vel, inj, inj3, q, p2, *e, smem=1)
    e = exchange(*e)
    acc3, grad = call(last_kernel, [FIELD, (flat, F32)], [PADDED, SIDE, PADDED, SIDE])(
        scal, u3, vel, inj, inj3, q, p2, p1, acc0, acc1, acc2, *e, smem=1)
    parts = lax.all_to_all(grad.reshape(16, 4, BX, BY), "shot", 0, 0, tiled=True)
    scaled, copies, dot = call(
        gradient_kernel, [((32, BY), F32), (flat, F32), ((8, BY), F32)])(
        parts.reshape(flat), preconditioner.reshape(32, BY))
    full = lax.all_to_all(copies.reshape(16, 4, BX, BY), "shot", 0, 0, tiled=True)
    source, d1, *e = call(born1_kernel, [FIELD, FIELD] + edges(1))(
        scal, full.reshape(flat), acc0, smem=1)
    e = exchange(*e)
    sample = call(sample_kernel, [((1, NREC), F32)], [pltpu.VMEM((512, 2 * BY), BF16)], flops=600_000_000)
    s1, = sample(d1, pick_cell, pick_y)
    d2, *e = call(make_born(1, False), [FIELD] + edges(1), [PADDED, SIDE])(
        scal, d1, d1, source, acc1, vel, *e, smem=1)
    e = exchange(*e)
    s2, = sample(d2, pick_cell, pick_y)
    d3, *e = call(make_born(2, False), [FIELD] + edges(1), [PADDED, SIDE])(
        scal, d2, d1, source, acc2, vel, *e, smem=1)
    e = exchange(*e)
    s3, = sample(d3, pick_cell, pick_y)
    block, = call(
        make_born(3, True), [((72, BY), F32)],
        [PADDED, SIDE, pltpu.VMEM((BX, NZ, BY), F32), pltpu.VMEM((512, 2 * BY), BF16)],
    )(scal, d3, d2, source, acc3, vel, *e, pick_cell, pick_y, s1, s2, s3, dot, smem=1)
    theirs = lax.ppermute(block, "gx", [(i, i ^ 1) for i in range(8)])
    payload, = call(pair_kernel, [((8, 72, BY), F32)])(block, theirs)
    same_core = [[2 * (2 * c + k) + g for c in range(4) for g in range(2)] for k in range(2)]
    arrived = lax.all_to_all(payload, ("gx", "gy"), 0, 0, axis_index_groups=same_core, tiled=True)
    predicted, stats = call(collect_kernel, [((64, BY), F32), ((16, 8, BY), F32)])(arrived)
    stats = lax.all_to_all(stats, "shot", 0, 0, tiled=True)
    image, residual = call(finish_kernel, [((32, BY), F32), ((4, NREC), F32)])(
        stats, predicted, scaled, traces[0])
    return image.reshape(4, BX, BY), residual[None]


def solution(mesh):
    return jax.shard_map(
        on_device,
        mesh=mesh,
        in_specs=(
            P("shot", None, "gx", "gy"),
            P("shot", None, "gx", "gy"),
            P(None, "gx", "gy"),
            P("shot", "gx", "gy"),
            P("shot", None, None),
            P("shot", None),
            P("shot", None),
            P("shot", None),
            P("shot"),
            P("shot"),
        ),
        out_specs=(P("shot", "gx", "gy"), P("shot", None, None)),
        check_vma=False,
    )
```

```python
import jax
import jax.numpy as jnp
from jax import lax
from jax.experimental import pallas as pl
from jax.experimental.pallas import tpu as pltpu
from jax.sharding import PartitionSpec as P

STEPS = 4
NZ, BX, BY = 64, 8, 128
NREC = 2048
F32, BF16, I32 = jnp.float32, jnp.bfloat16, jnp.int32
weights = (-205.0 / 72.0, 8.0 / 5.0, -1.0 / 5.0, 8.0 / 315.0, -1.0 / 560.0)


def call(kernel, outs, scratch=(), limit=24, flops=10_000_000):
    def run(*args, smem=0, hbm=0):
        spaces = [pltpu.SMEM] * smem + [pltpu.HBM] * hbm
        spaces = spaces + [pltpu.VMEM] * (len(args) - smem - hbm)
        specs = [pl.BlockSpec(memory_space=space) for space in spaces]
        return pl.pallas_call(
            kernel,
            out_shape=[jax.ShapeDtypeStruct(s, d) for s, d in outs],
            in_specs=specs,
            out_specs=[pl.BlockSpec(memory_space=pltpu.VMEM) for _ in outs],
            scratch_shapes=list(scratch),
            compiler_params=pltpu.CompilerParams(vmem_limit_bytes=limit * 1024 * 1024),
            cost_estimate=pl.CostEstimate(
                flops=flops, bytes_accessed=2_000_000, transcendentals=0
            ),
        )(*args)

    return run


def lanes(rows):
    return lax.broadcasted_iota(I32, (rows, BY), 1)


def near_edge(gy, lane):
    return ((gy == 0) & (lane >= BY - 4)) | ((gy == 1) & (lane < 4))


def send_edges(field, outer_ref, inner_ref, strip_ref, slot, scal):
    core, gy = scal[0], scal[1]
    keep = near_edge(gy, lanes(8))
    for i in range(4):
        outer_ref[slot, i] = field[4 * core + i]
        inner_ref[slot, i] = field[4 * (1 - core) + i]
    for half in range(2):
        sums = []
        for j in range(32):
            x, z = 4 * half + j // 8, 8 * (j % 8)
            turned = pltpu.roll(jnp.where(keep, field[x, z : z + 8], 0.0), 4 * j, 1)
            if j < 4:
                sums.append(turned)
            else:
                sums[j % 4] = sums[j % 4] + turned
        strip_ref[slot, 8 * half : 8 * half + 8] = (sums[0] + sums[1]) + (sums[2] + sums[3])


def interior(field, padded, part):
    lane = lanes(NZ)
    zero = jnp.zeros((8, BY), F32)
    for x in range(BX):
        padded[x, 0:8] = zero
        padded[x, 72:80] = zero
        padded[x, 8:72] = field[x]
    for x in range(BX):
        centre = field[x]
        result = (3.0 * weights[0]) * centre
        for k in range(1, 5):
            pairs = padded[x, 8 + k : 72 + k] + padded[x, 8 - k : 72 - k]
            if x + k < BX:
                pairs = pairs + field[x + k]
            if x - k >= 0:
                pairs = pairs + field[x - k]
            right = pltpu.roll(jnp.where(lane < k, 0.0, centre), BY - k, 1)
            left = pltpu.roll(jnp.where(lane >= BY - k, 0.0, centre), k, 1)
            result = result + weights[k] * (pairs + (right + left))
        part[x] = result


def interior_kernel(*refs):
    count = (len(refs) - 1) // 2
    for i in range(count):
        interior(refs[i], refs[-1], refs[count + i])


def receive(halo, outer_ref, inner_ref, strip_ref, slot, scal):
    core, gy = scal[0], scal[1]
    inside = ((scal[2] > 0) | (core == 1)) & ((scal[2] < 7 * BX) | (core == 0))
    for i in range(4):
        halo[4 * core + i] = jnp.where(inside, outer_ref[slot, i], 0.0)
        halo[4 * (1 - core) + i] = inner_ref[slot, i]
    packed = strip_ref[slot]
    place = lanes(16) & 3
    after, before = weights[4] * packed, weights[4] * packed
    for m in range(1, 4):
        after = after + weights[4 - m] * jnp.where(place >= m, pltpu.roll(packed, m, 1), 0.0)
        before = before + weights[4 - m] * jnp.where(place < 4 - m, pltpu.roll(packed, BY - m, 1), 0.0)
    return jnp.where(gy == 0, pltpu.roll(after, BY - 4, 1), pltpu.roll(before, 4, 1))


def complete(part, halo, strips, x, scal):
    keep = near_edge(scal[1], lanes(8))
    pieces = []
    for z in range(8):
        j = 8 * (x % 4) + z
        row = 8 * (x // 4)
        turned = pltpu.roll(strips[row : row + 8], (BY - 4 * j) % BY, 1)
        pieces.append(jnp.where(keep, turned, 0.0))
    result = part[x] + jnp.concatenate(pieces, axis=0)
    for k in range(1, 5):
        if x - k < 0:
            result = result + weights[k] * halo[4 + x - k]
        if x + k >= BX:
            result = result + weights[k] * halo[x + k - 4]
    return result


FIELD = ((BX, NZ, BY), F32)
PADDED = pltpu.VMEM((BX, 80, BY), F32)
HALO = pltpu.VMEM((BX, NZ, BY), F32)


def edges(count):
    return [((count, 4, NZ, BY), F32), ((count, 4, NZ, BY), F32), ((count, 16, BY), F32)]


def first_kernel(scal, newer, newer_out, outer, inner, strip):
    for x in range(BX):
        newer_out[x] = newer[pl.ds(x, NZ, stride=8), :]
    send_edges(newer_out, outer, inner, strip, 0, scal)


def two_pieces(values):
    high = values.astype(BF16)
    return high, (values - high.astype(F32)).astype(BF16)


def block(i):
    return pl.ds(pl.multiple_of(16 * i, 16), 16)


def wide(row):
    return jnp.broadcast_to(row, (16, NREC)).astype(BF16)


def inject(n, traces, pick_cell, pick_y, spread, inj):
    value = traces[n : n + 1, :]
    coarse = value.astype(BF16).astype(F32)
    high, low = wide(coarse), wide(value - coarse)

    def weigh(i, carry):
        picked = pick_y[block(i), :]
        spread[block(i), :] = picked * high
        spread[block(8 + i), :] = picked * low
        return carry

    lax.fori_loop(0, 8, weigh, 0)
    both = lax.dot_general(
        pick_cell[...], spread[...], (((1,), (1,)), ((), ())), preferred_element_type=F32
    )
    for x in range(BX):
        part = both[NZ * x : NZ * x + NZ]
        inj[x] = part[:, :BY] + part[:, BY:]


def make_inject(n):
    def kernel(shot, pick_cell, pick_y, inj, spread):
        inject(n, shot, pick_cell, pick_y, spread, inj)

    return kernel


def prepare_kernel(scal, shot, inj, pick_cell, pick_y, at_depth, spread):
    code = shot[4:5, :].astype(I32)
    lat_x = ((code >> 6) & 63) - scal[2]
    lat_y = (code >> 12) - scal[3]
    present = (lat_x >= 0) & (lat_x < BX) & (lat_y >= 0) & (lat_y < BY)
    depth = jnp.where(present, code & 63, -1)
    col = jnp.where(present, lat_y, -1)

    def hits(i, wanted):
        number = lax.broadcasted_iota(I32, (16, NREC), 0) + 16 * i
        return jnp.where(number == wanted, 1.0, 0.0).astype(BF16)

    def depths(i, carry):
        at_depth[block(i), :] = hits(i, depth)
        return carry

    lax.fori_loop(0, 4, depths, 0)

    def planes(x, carry):
        here = wide(jnp.where(lat_x == x, 1.0, 0.0))
        for i in range(4):
            pick_cell[block(4 * x + i), :] = at_depth[16 * i : 16 * i + 16] * here
        return carry

    lax.fori_loop(0, BX, planes, 0)

    def columns(i, carry):
        pick_y[block(i), :] = hits(i, col)
        return carry

    lax.fori_loop(0, 8, columns, 0)
    inject(3, shot, pick_cell, pick_y, spread, inj)


def planes_kernel(older_in, vel_in, older, vel):
    for x in range(BX):
        older[x] = older_in[pl.ds(x, NZ, stride=8), :]
        vel[x] = vel_in[pl.ds(x, NZ, stride=8), :]


def forward1_kernel(scal, part, newer, older, vel, inj3, outer, inner, strip, acc, nxt, q, outer_o, inner_o, strip_o, halo):
    strips = receive(halo, outer, inner, strip, 0, scal)
    for x in range(BX):
        a = vel[x] * complete(part, halo, strips, x, scal)
        acc[x] = a
        nxt[x] = (2.0 * newer[x] - older[x]) + a
        q[x] = vel[x] * inj3[x]
    send_edges(nxt, outer_o, inner_o, strip_o, 0, scal)
    send_edges(q, outer_o, inner_o, strip_o, 1, scal)


def make_forward(moment):
    def kernel(scal, part, part_q, newer, older, vel, inj, inj3, *rest):
        if moment == 2:
            later, rest = rest[0], rest[1:]
        outer, inner, strip, acc, nxt, p, q, outer_o, inner_o, strip_o, halo, halo_q = rest
        strips = receive(halo, outer, inner, strip, 0, scal)
        for x in range(BX):
            a = vel[x] * complete(part, halo, strips, x, scal)
            acc[x] = a
            nxt[x] = (2.0 * newer[x] - older[x]) + a
        send_edges(nxt, outer_o, inner_o, strip_o, 0, scal)
        strips = receive(halo_q, outer, inner, strip, 1, scal)
        for x in range(BX):
            before = 2.0 * inj3[x] if moment == 1 else 2.0 * later[x] - inj3[x]
            value = (before + complete(part_q, halo_q, strips, x, scal)) + inj[x]
            p[x] = value
            q[x] = vel[x] * value
        send_edges(q, outer_o, inner_o, strip_o, 1, scal)

    return kernel


def window(scal, x):
    column = lanes(NZ) + scal[3]
    at_x = scal[2] + x
    inside_x = (at_x >= scal[4]) & (at_x < scal[4] + 48)
    return (column >= scal[5]) & (column < scal[5] + 192) & inside_x


def last_kernel(scal, part, part_q, vel, inj0, inj3, latest, later, acc0, acc1, acc2, outer, inner, strip, acc3, grad, halo, halo_q):
    strips = receive(halo, outer, inner, strip, 0, scal)
    strips_q = receive(halo_q, outer, inner, strip, 1, scal)
    for x in range(BX):
        a = vel[x] * complete(part, halo, strips, x, scal)
        acc3[x] = a
        p0 = ((2.0 * later[x] - latest[x]) + complete(part_q, halo_q, strips_q, x, scal)) + inj0[x]
        total = ((a * inj3[x] + acc2[x] * latest[x]) + acc1[x] * later[x]) + acc0[x] * p0
        grad[pl.ds(x, NZ, stride=8), :] = jnp.where(window(scal, x), total, 0.0)


def gradient_kernel(parts, pre, scaled, copies, dot):
    total = parts[0:32]
    for s in range(1, 16):
        total = total + parts[32 * s : 32 * s + 32]
    value = pre[...] * total
    scaled[...] = value
    for s in range(16):
        copies[32 * s : 32 * s + 32] = value
    product = total * value
    dot[...] = (product[0:8] + product[8:16]) + (product[16:24] + product[24:32])


def born1_kernel(scal, full, acc0, source, d, outer_o, inner_o, strip_o):
    for x in range(BX):
        s = jnp.where(window(scal, x), full[pl.ds(x, NZ, stride=8), :], 0.0)
        source[x] = s
        d[x] = s * acc0[x]
    send_edges(d, outer_o, inner_o, strip_o, 0, scal)


def make_born(moment, last):
    def kernel(scal, part, now, before, source, acc, vel, outer, inner, strip, *rest):
        if last:
            pick_cell, pick_y, s1, s2, s3, dot, block, halo, d, pieces = rest
        else:
            samples, d, outer_o, inner_o, strip_o, halo = rest
        strips = receive(halo, outer, inner, strip, 0, scal)
        for x in range(BX):
            base = 2.0 * now[x]
            if moment > 1:
                base = base - before[x]
            d[x] = (base + vel[x] * complete(part, halo, strips, x, scal)) + source[x] * acc[x]
        if not last:
            send_edges(d, outer_o, inner_o, strip_o, 0, scal)
            return
        s4 = sampled(d, pieces, pick_cell, pick_y)
        energy = jnp.zeros((1, BY), F32)
        for n, values in enumerate((s1[...], s2[...], s3[...], s4)):
            for j in range(16):
                piece = values[:, BY * j : BY * j + BY]
                block[16 * n + j : 16 * n + j + 1, :] = piece
                energy = energy + piece * piece
        block[64:72, :] = jnp.zeros((8, BY), F32)
        block[64:65, :] = energy
        block[65:66, :] = jnp.sum(dot[...], axis=0, keepdims=True)

    return kernel


def sampled(field, pieces, pick_cell, pick_y):
    for x in range(BX):
        high, low = two_pieces(field[x])
        pieces[NZ * x : NZ * x + NZ, :BY] = high
        pieces[NZ * x : NZ * x + NZ, BY:] = low
    at_cell = lax.dot_general(
        pieces[...], pick_cell[...], (((0,), (0,)), ((), ())), preferred_element_type=F32
    )
    chosen = (at_cell[:BY] + at_cell[BY:]) * pick_y[...].astype(F32)
    return jnp.sum(chosen, axis=0, keepdims=True)


def sample_kernel(field, pick_cell, pick_y, out, pieces):
    out[...] = sampled(field, pieces, pick_cell, pick_y)


def pair_kernel(mine, theirs, copies):
    total = mine[...] + theirs[...]
    for i in range(8):
        copies[i] = total


def collect_kernel(arrived, predicted, copies):
    total = arrived[0]
    for i in range(1, 8):
        total = total + arrived[i]
    predicted[...] = total[0:64]
    for i in range(16):
        copies[i] = total[64:72]


def finish_kernel(stats, predicted, scaled, traces, image, residual):
    total = stats[0]
    for i in range(1, 16):
        total = total + stats[i]
    energy = jnp.sum(total[0:1], axis=1, keepdims=True)
    dot = jnp.sum(total[1:2], axis=1, keepdims=True)
    step = dot / (energy + 1e-6)
    image[...] = step * scaled[...]
    for n in range(STEPS):
        for j in range(16):
            at = pl.ds(BY * j, BY)
            row = predicted[16 * n + j : 16 * n + j + 1, :]
            residual[n : n + 1, at] = traces[n : n + 1, at] - step * row


def exchange(outer, inner, strip):
    chips = [(2 * i + 1, (2 * i + 2) % 8) for i in range(4)]
    across = chips + [(b, a) for a, b in chips]
    swap = [(i, i ^ 1) for i in range(8)]
    return (
        lax.ppermute(outer, "gx", across),
        lax.ppermute(inner, "gx", swap),
        lax.ppermute(strip, "gy", [(0, 1), (1, 0)]),
    )


def on_device(older_field, newer_field, velocity, preconditioner, traces,
              receiver_z, receiver_x, receiver_y, aperture_x, aperture_y):
    flat = (NZ * BX, BY)
    gx, gy = lax.axis_index("gx"), lax.axis_index("gy")
    scal = jnp.stack([gx % 2, gy, gx * BX, gy * BY, aperture_x[0], aperture_y[0]]).astype(I32)
    newer, *e = call(first_kernel, [FIELD] + edges(1))(scal, newer_field.reshape(flat), smem=1)
    e = exchange(*e)
    code = receiver_z | (receiver_x << 6) | (receiver_y << 12)
    shot = jnp.concatenate([traces[0], code.astype(F32)], axis=0)
    inj3, pick_cell, pick_y = call(
        prepare_kernel,
        [FIELD, ((512, NREC), BF16), ((BY, NREC), BF16)],
        [pltpu.VMEM((NZ, NREC), BF16), pltpu.VMEM((2 * BY, NREC), BF16)],
    )(scal, shot, smem=1)

    def injection(n):
        return call(make_inject(n), [FIELD], [pltpu.VMEM((2 * BY, NREC), BF16)], flops=1_000_000_000)(
            shot, pick_cell, pick_y)[0]

    one = call(interior_kernel, [FIELD], [PADDED])
    two = call(interior_kernel, [FIELD] * 2, [PADDED])
    older, vel = call(planes_kernel, [FIELD, FIELD])(older_field.reshape(flat), velocity.reshape(flat))
    acc0, u1, q, *e = call(forward1_kernel, [FIELD] * 3 + edges(2), [HALO])(
        scal, *one(newer), newer, older, vel, inj3, *e, smem=1)
    e = exchange(*e)
    acc1, u2, p2, q, *e = call(make_forward(1), [FIELD] * 4 + edges(2), [HALO] * 2)(
        scal, *two(u1, q), u1, newer, vel, injection(2), inj3, *e, smem=1)
    e = exchange(*e)
    acc2, u3, p1, q, *e = call(make_forward(2), [FIELD] * 4 + edges(2), [HALO] * 2)(
        scal, *two(u2, q), u2, u1, vel, injection(1), inj3, p2, *e, smem=1)
    e = exchange(*e)
    acc3, grad = call(last_kernel, [FIELD, (flat, F32)], [HALO] * 2)(
        scal, *two(u3, q), vel, injection(0), inj3, p2, p1, acc0, acc1, acc2, *e, smem=1)
    parts = lax.all_to_all(grad.reshape(16, 4, BX, BY), "shot", 0, 0, tiled=True)
    scaled, copies, dot = call(
        gradient_kernel, [((32, BY), F32), (flat, F32), ((8, BY), F32)])(
        parts.reshape(flat), preconditioner.reshape(32, BY))
    full = lax.all_to_all(copies.reshape(16, 4, BX, BY), "shot", 0, 0, tiled=True)
    source, d1, *e = call(born1_kernel, [FIELD, FIELD] + edges(1))(
        scal, full.reshape(flat), acc0, smem=1)
    e = exchange(*e)
    sample = call(sample_kernel, [((1, NREC), F32)], [pltpu.VMEM((512, 2 * BY), BF16)], flops=600_000_000)
    s1, = sample(d1, pick_cell, pick_y)
    d2, *e = call(make_born(1, False), [FIELD] + edges(1), [HALO])(
        scal, *one(d1), d1, d1, source, acc1, vel, *e, s1, smem=1)
    e = exchange(*e)
    s2, = sample(d2, pick_cell, pick_y)
    d3, *e = call(make_born(2, False), [FIELD] + edges(1), [HALO])(
        scal, *one(d2), d2, d1, source, acc2, vel, *e, s2, smem=1)
    e = exchange(*e)
    s3, = sample(d3, pick_cell, pick_y)
    block, = call(
        make_born(3, True), [((72, BY), F32)],
        [HALO, pltpu.VMEM((BX, NZ, BY), F32), pltpu.VMEM((512, 2 * BY), BF16)],
    )(scal, *one(d3), d3, d2, source, acc3, vel, *e, pick_cell, pick_y, s1, s2, s3, dot, smem=1)
    theirs = lax.ppermute(block, "gx", [(i, i ^ 1) for i in range(8)])
    payload, = call(pair_kernel, [((8, 72, BY), F32)])(block, theirs)
    same_core = [[2 * (2 * c + k) + g for c in range(4) for g in range(2)] for k in range(2)]
    arrived = lax.all_to_all(payload, ("gx", "gy"), 0, 0, axis_index_groups=same_core, tiled=True)
    predicted, stats = call(collect_kernel, [((64, BY), F32), ((16, 8, BY), F32)])(arrived)
    stats = lax.all_to_all(stats, "shot", 0, 0, tiled=True)
    image, residual = call(finish_kernel, [((32, BY), F32), ((4, NREC), F32)])(
        stats, predicted, scaled, traces[0])
    return image.reshape(4, BX, BY), residual[None]


def solution(mesh):
    return jax.shard_map(
        on_device,
        mesh=mesh,
        in_specs=(
            P("shot", None, "gx", "gy"),
            P("shot", None, "gx", "gy"),
            P(None, "gx", "gy"),
            P("shot", "gx", "gy"),
            P("shot", None, None),
            P("shot", None),
            P("shot", None),
            P("shot", None),
            P("shot"),
            P("shot"),
        ),
        out_specs=(P("shot", "gx", "gy"), P("shot", None, None)),
        check_vma=False,
    )
```

```python
import jax
import jax.numpy as jnp
from jax import lax
from jax.experimental import pallas as pl
from jax.experimental.pallas import tpu as pltpu
from jax.sharding import PartitionSpec as P

STEPS = 4
NZ, BX, BY = 64, 8, 128
NREC = 2048
F32, BF16, I32 = jnp.float32, jnp.bfloat16, jnp.int32
weights = (-205.0 / 72.0, 8.0 / 5.0, -1.0 / 5.0, 8.0 / 315.0, -1.0 / 560.0)


def call(kernel, outs, scratch=(), limit=24, flops=10_000_000):
    def run(*args, smem=0, hbm=0):
        spaces = [pltpu.SMEM] * smem + [pltpu.HBM] * hbm
        spaces = spaces + [pltpu.VMEM] * (len(args) - smem - hbm)
        specs = [pl.BlockSpec(memory_space=space) for space in spaces]
        return pl.pallas_call(
            kernel,
            out_shape=[jax.ShapeDtypeStruct(s, d) for s, d in outs],
            in_specs=specs,
            out_specs=[pl.BlockSpec(memory_space=pltpu.VMEM) for _ in outs],
            scratch_shapes=list(scratch),
            compiler_params=pltpu.CompilerParams(vmem_limit_bytes=limit * 1024 * 1024),
            cost_estimate=pl.CostEstimate(
                flops=flops, bytes_accessed=2_000_000, transcendentals=0
            ),
        )(*args)

    return run


def lanes(rows):
    return lax.broadcasted_iota(I32, (rows, BY), 1)


def near_edge(gy, lane):
    return ((gy == 0) & (lane >= BY - 4)) | ((gy == 1) & (lane < 4))


def send_rows(field, outer_ref, inner_ref, slot, scal):
    core = scal[0]
    for i in range(4):
        outer_ref[slot, i] = field[4 * core + i]
        inner_ref[slot, i] = field[4 * (1 - core) + i]


def pack_kernel(scal, *refs):
    strip_ref = refs[-1]
    keep = near_edge(scal[1], lanes(8))
    for slot, field in enumerate(refs[:-1]):
        for half in range(2):
            sums = []
            for j in range(32):
                x, z = 4 * half + j // 8, 8 * (j % 8)
                turned = pltpu.roll(jnp.where(keep, field[x, z : z + 8], 0.0), 4 * j, 1)
                if j < 4:
                    sums.append(turned)
                else:
                    sums[j % 4] = sums[j % 4] + turned
            strip_ref[slot, 8 * half : 8 * half + 8] = (sums[0] + sums[1]) + (sums[2] + sums[3])


def interior(field, padded, part):
    lane = lanes(NZ)
    zero = jnp.zeros((8, BY), F32)
    for x in range(BX):
        padded[x, 0:8] = zero
        padded[x, 72:80] = zero
        padded[x, 8:72] = field[x]
    for x in range(BX):
        centre = field[x]
        result = (3.0 * weights[0]) * centre
        for k in range(1, 5):
            pairs = padded[x, 8 + k : 72 + k] + padded[x, 8 - k : 72 - k]
            if x + k < BX:
                pairs = pairs + field[x + k]
            if x - k >= 0:
                pairs = pairs + field[x - k]
            right = pltpu.roll(jnp.where(lane < k, 0.0, centre), BY - k, 1)
            left = pltpu.roll(jnp.where(lane >= BY - k, 0.0, centre), k, 1)
            result = result + weights[k] * (pairs + (right + left))
        part[x] = result


def interior_kernel(*refs):
    count = (len(refs) - 1) // 2
    for i in range(count):
        interior(refs[i], refs[-1], refs[count + i])


def receive(halo, outer_ref, inner_ref, strip_ref, slot, scal):
    core, gy = scal[0], scal[1]
    inside = ((scal[2] > 0) | (core == 1)) & ((scal[2] < 7 * BX) | (core == 0))
    for i in range(4):
        halo[4 * core + i] = jnp.where(inside, outer_ref[slot, i], 0.0)
        halo[4 * (1 - core) + i] = inner_ref[slot, i]
    packed = strip_ref[slot]
    place = lanes(16) & 3
    after, before = weights[4] * packed, weights[4] * packed
    for m in range(1, 4):
        after = after + weights[4 - m] * jnp.where(place >= m, pltpu.roll(packed, m, 1), 0.0)
        before = before + weights[4 - m] * jnp.where(place < 4 - m, pltpu.roll(packed, BY - m, 1), 0.0)
    return jnp.where(gy == 0, pltpu.roll(after, BY - 4, 1), pltpu.roll(before, 4, 1))


def complete(part, halo, strips, x, scal):
    keep = near_edge(scal[1], lanes(8))
    pieces = []
    for z in range(8):
        j = 8 * (x % 4) + z
        row = 8 * (x // 4)
        turned = pltpu.roll(strips[row : row + 8], (BY - 4 * j) % BY, 1)
        pieces.append(jnp.where(keep, turned, 0.0))
    result = part[x] + jnp.concatenate(pieces, axis=0)
    for k in range(1, 5):
        if x - k < 0:
            result = result + weights[k] * halo[4 + x - k]
        if x + k >= BX:
            result = result + weights[k] * halo[x + k - 4]
    return result


FIELD = ((BX, NZ, BY), F32)
PADDED = pltpu.VMEM((BX, 80, BY), F32)
HALO = pltpu.VMEM((BX, NZ, BY), F32)


def edges(count):
    return [((count, 4, NZ, BY), F32), ((count, 4, NZ, BY), F32)]


def first_kernel(scal, newer, newer_out, outer, inner):
    for x in range(BX):
        newer_out[x] = newer[pl.ds(x, NZ, stride=8), :]
    send_rows(newer_out, outer, inner, 0, scal)


def two_pieces(values):
    high = values.astype(BF16)
    return high, (values - high.astype(F32)).astype(BF16)


def block(i):
    return pl.ds(pl.multiple_of(16 * i, 16), 16)


def wide(row):
    return jnp.broadcast_to(row, (16, NREC)).astype(BF16)


def inject(n, traces, pick_cell, pick_y, spread, inj):
    value = traces[n : n + 1, :]
    coarse = value.astype(BF16).astype(F32)
    high, low = wide(coarse), wide(value - coarse)

    def weigh(i, carry):
        picked = pick_y[block(i), :]
        spread[block(i), :] = picked * high
        spread[block(8 + i), :] = picked * low
        return carry

    lax.fori_loop(0, 8, weigh, 0)
    both = lax.dot_general(
        pick_cell[...], spread[...], (((1,), (1,)), ((), ())), preferred_element_type=F32
    )
    for x in range(BX):
        part = both[NZ * x : NZ * x + NZ]
        inj[x] = part[:, :BY] + part[:, BY:]


def make_inject(n):
    def kernel(shot, pick_cell, pick_y, inj, spread):
        inject(n, shot, pick_cell, pick_y, spread, inj)

    return kernel


def prepare_kernel(scal, shot, inj, pick_cell, pick_y, at_depth, spread):
    code = shot[4:5, :].astype(I32)
    lat_x = ((code >> 6) & 63) - scal[2]
    lat_y = (code >> 12) - scal[3]
    present = (lat_x >= 0) & (lat_x < BX) & (lat_y >= 0) & (lat_y < BY)
    depth = jnp.where(present, code & 63, -1)
    col = jnp.where(present, lat_y, -1)

    def hits(i, wanted):
        number = lax.broadcasted_iota(I32, (16, NREC), 0) + 16 * i
        return jnp.where(number == wanted, 1.0, 0.0).astype(BF16)

    def depths(i, carry):
        at_depth[block(i), :] = hits(i, depth)
        return carry

    lax.fori_loop(0, 4, depths, 0)

    def planes(x, carry):
        here = wide(jnp.where(lat_x == x, 1.0, 0.0))
        for i in range(4):
            pick_cell[block(4 * x + i), :] = at_depth[16 * i : 16 * i + 16] * here
        return carry

    lax.fori_loop(0, BX, planes, 0)

    def columns(i, carry):
        pick_y[block(i), :] = hits(i, col)
        return carry

    lax.fori_loop(0, 8, columns, 0)
    inject(3, shot, pick_cell, pick_y, spread, inj)


def planes_kernel(older_in, vel_in, older, vel):
    for x in range(BX):
        older[x] = older_in[pl.ds(x, NZ, stride=8), :]
        vel[x] = vel_in[pl.ds(x, NZ, stride=8), :]


def forward1_kernel(scal, part, newer, older, vel, inj3, outer, inner, strip, acc, nxt, q, outer_o, inner_o, halo):
    strips = receive(halo, outer, inner, strip, 0, scal)
    for x in range(BX):
        a = vel[x] * complete(part, halo, strips, x, scal)
        acc[x] = a
        nxt[x] = (2.0 * newer[x] - older[x]) + a
        q[x] = vel[x] * inj3[x]
    send_rows(nxt, outer_o, inner_o, 0, scal)
    send_rows(q, outer_o, inner_o, 1, scal)


def make_forward(moment):
    def kernel(scal, part, part_q, newer, older, vel, inj, inj3, *rest):
        if moment == 2:
            later, rest = rest[0], rest[1:]
        outer, inner, strip, acc, nxt, p, q, outer_o, inner_o, halo, halo_q = rest
        strips = receive(halo, outer, inner, strip, 0, scal)
        for x in range(BX):
            a = vel[x] * complete(part, halo, strips, x, scal)
            acc[x] = a
            nxt[x] = (2.0 * newer[x] - older[x]) + a
        send_rows(nxt, outer_o, inner_o, 0, scal)
        strips = receive(halo_q, outer, inner, strip, 1, scal)
        for x in range(BX):
            before = 2.0 * inj3[x] if moment == 1 else 2.0 * later[x] - inj3[x]
            value = (before + complete(part_q, halo_q, strips, x, scal)) + inj[x]
            p[x] = value
            q[x] = vel[x] * value
        send_rows(q, outer_o, inner_o, 1, scal)

    return kernel


def window(scal, x):
    column = lanes(NZ) + scal[3]
    at_x = scal[2] + x
    inside_x = (at_x >= scal[4]) & (at_x < scal[4] + 48)
    return (column >= scal[5]) & (column < scal[5] + 192) & inside_x


def last_kernel(scal, part, part_q, vel, inj0, inj3, latest, later, acc0, acc1, acc2, outer, inner, strip, acc3, grad, halo, halo_q):
    strips = receive(halo, outer, inner, strip, 0, scal)
    strips_q = receive(halo_q, outer, inner, strip, 1, scal)
    for x in range(BX):
        a = vel[x] * complete(part, halo, strips, x, scal)
        acc3[x] = a
        p0 = ((2.0 * later[x] - latest[x]) + complete(part_q, halo_q, strips_q, x, scal)) + inj0[x]
        total = ((a * inj3[x] + acc2[x] * latest[x]) + acc1[x] * later[x]) + acc0[x] * p0
        grad[pl.ds(x, NZ, stride=8), :] = jnp.where(window(scal, x), total, 0.0)


def gradient_kernel(parts, pre, scaled, copies, dot):
    total = parts[0:32]
    for s in range(1, 16):
        total = total + parts[32 * s : 32 * s + 32]
    value = pre[...] * total
    scaled[...] = value
    for s in range(16):
        copies[32 * s : 32 * s + 32] = value
    product = total * value
    dot[...] = (product[0:8] + product[8:16]) + (product[16:24] + product[24:32])


def born1_kernel(scal, full, acc0, source, d, outer_o, inner_o):
    for x in range(BX):
        s = jnp.where(window(scal, x), full[pl.ds(x, NZ, stride=8), :], 0.0)
        source[x] = s
        d[x] = s * acc0[x]
    send_rows(d, outer_o, inner_o, 0, scal)


def make_born(moment, last):
    def kernel(scal, part, now, before, source, acc, vel, outer, inner, strip, *rest):
        if last:
            pick_cell, pick_y, s1, s2, s3, dot, block, halo, d, pieces = rest
        else:
            samples, d, outer_o, inner_o, halo = rest
        strips = receive(halo, outer, inner, strip, 0, scal)
        for x in range(BX):
            base = 2.0 * now[x]
            if moment > 1:
                base = base - before[x]
            d[x] = (base + vel[x] * complete(part, halo, strips, x, scal)) + source[x] * acc[x]
        if not last:
            send_rows(d, outer_o, inner_o, 0, scal)
            return
        s4 = sampled(d, pieces, pick_cell, pick_y)
        energy = jnp.zeros((1, BY), F32)
        for n, values in enumerate((s1[...], s2[...], s3[...], s4)):
            for j in range(16):
                piece = values[:, BY * j : BY * j + BY]
                block[16 * n + j : 16 * n + j + 1, :] = piece
                energy = energy + piece * piece
        block[64:72, :] = jnp.zeros((8, BY), F32)
        block[64:65, :] = energy
        block[65:66, :] = jnp.sum(dot[...], axis=0, keepdims=True)

    return kernel


def sampled(field, pieces, pick_cell, pick_y):
    for x in range(BX):
        high, low = two_pieces(field[x])
        pieces[NZ * x : NZ * x + NZ, :BY] = high
        pieces[NZ * x : NZ * x + NZ, BY:] = low
    at_cell = lax.dot_general(
        pieces[...], pick_cell[...], (((0,), (0,)), ((), ())), preferred_element_type=F32
    )
    chosen = (at_cell[:BY] + at_cell[BY:]) * pick_y[...].astype(F32)
    return jnp.sum(chosen, axis=0, keepdims=True)


def sample_kernel(field, pick_cell, pick_y, out, pieces):
    out[...] = sampled(field, pieces, pick_cell, pick_y)


def pair_kernel(mine, theirs, copies):
    total = mine[...] + theirs[...]
    for i in range(8):
        copies[i] = total


def collect_kernel(arrived, predicted, copies):
    total = arrived[0]
    for i in range(1, 8):
        total = total + arrived[i]
    predicted[...] = total[0:64]
    for i in range(16):
        copies[i] = total[64:72]


def finish_kernel(stats, predicted, scaled, traces, image, residual):
    total = stats[0]
    for i in range(1, 16):
        total = total + stats[i]
    energy = jnp.sum(total[0:1], axis=1, keepdims=True)
    dot = jnp.sum(total[1:2], axis=1, keepdims=True)
    step = dot / (energy + 1e-6)
    image[...] = step * scaled[...]
    for n in range(STEPS):
        for j in range(16):
            at = pl.ds(BY * j, BY)
            row = predicted[16 * n + j : 16 * n + j + 1, :]
            residual[n : n + 1, at] = traces[n : n + 1, at] - step * row


def exchange(scal, outer, inner, *fields):
    chips = [(2 * i + 1, (2 * i + 2) % 8) for i in range(4)]
    across = chips + [(b, a) for a, b in chips]
    swap = [(i, i ^ 1) for i in range(8)]
    strip, = call(pack_kernel, [((len(fields), 16, BY), F32)])(scal, *fields, smem=1)
    return (
        lax.ppermute(outer, "gx", across),
        lax.ppermute(inner, "gx", swap),
        lax.ppermute(strip, "gy", [(0, 1), (1, 0)]),
    )


def on_device(older_field, newer_field, velocity, preconditioner, traces,
              receiver_z, receiver_x, receiver_y, aperture_x, aperture_y):
    flat = (NZ * BX, BY)
    gx, gy = lax.axis_index("gx"), lax.axis_index("gy")
    scal = jnp.stack([gx % 2, gy, gx * BX, gy * BY, aperture_x[0], aperture_y[0]]).astype(I32)
    newer, *e = call(first_kernel, [FIELD] + edges(1))(scal, newer_field.reshape(flat), smem=1)
    e = exchange(scal, *e, newer)
    code = receiver_z | (receiver_x << 6) | (receiver_y << 12)
    shot = jnp.concatenate([traces[0], code.astype(F32)], axis=0)
    inj3, pick_cell, pick_y = call(
        prepare_kernel,
        [FIELD, ((512, NREC), BF16), ((BY, NREC), BF16)],
        [pltpu.VMEM((NZ, NREC), BF16), pltpu.VMEM((2 * BY, NREC), BF16)],
    )(scal, shot, smem=1)

    def injection(n):
        return call(make_inject(n), [FIELD], [pltpu.VMEM((2 * BY, NREC), BF16)], flops=1_000_000_000)(
            shot, pick_cell, pick_y)[0]

    one = call(interior_kernel, [FIELD], [PADDED])
    two = call(interior_kernel, [FIELD] * 2, [PADDED])
    older, vel = call(planes_kernel, [FIELD, FIELD])(older_field.reshape(flat), velocity.reshape(flat))
    acc0, u1, q, *e = call(forward1_kernel, [FIELD] * 3 + edges(2), [HALO])(
        scal, *one(newer), newer, older, vel, inj3, *e, smem=1)
    e = exchange(scal, *e, u1, q)
    acc1, u2, p2, q, *e = call(make_forward(1), [FIELD] * 4 + edges(2), [HALO] * 2)(
        scal, *two(u1, q), u1, newer, vel, injection(2), inj3, *e, smem=1)
    e = exchange(scal, *e, u2, q)
    acc2, u3, p1, q, *e = call(make_forward(2), [FIELD] * 4 + edges(2), [HALO] * 2)(
        scal, *two(u2, q), u2, u1, vel, injection(1), inj3, p2, *e, smem=1)
    e = exchange(scal, *e, u3, q)
    acc3, grad = call(last_kernel, [FIELD, (flat, F32)], [HALO] * 2)(
        scal, *two(u3, q), vel, injection(0), inj3, p2, p1, acc0, acc1, acc2, *e, smem=1)
    parts = lax.all_to_all(grad.reshape(16, 4, BX, BY), "shot", 0, 0, tiled=True)
    scaled, copies, dot = call(
        gradient_kernel, [((32, BY), F32), (flat, F32), ((8, BY), F32)])(
        parts.reshape(flat), preconditioner.reshape(32, BY))
    full = lax.all_to_all(copies.reshape(16, 4, BX, BY), "shot", 0, 0, tiled=True)
    source, d1, *e = call(born1_kernel, [FIELD, FIELD] + edges(1))(
        scal, full.reshape(flat), acc0, smem=1)
    e = exchange(scal, *e, d1)
    sample = call(sample_kernel, [((1, NREC), F32)], [pltpu.VMEM((512, 2 * BY), BF16)], flops=600_000_000)
    s1, = sample(d1, pick_cell, pick_y)
    d2, *e = call(make_born(1, False), [FIELD] + edges(1), [HALO])(
        scal, *one(d1), d1, d1, source, acc1, vel, *e, s1, smem=1)
    e = exchange(scal, *e, d2)
    s2, = sample(d2, pick_cell, pick_y)
    d3, *e = call(make_born(2, False), [FIELD] + edges(1), [HALO])(
        scal, *one(d2), d2, d1, source, acc2, vel, *e, s2, smem=1)
    e = exchange(scal, *e, d3)
    s3, = sample(d3, pick_cell, pick_y)
    block, = call(
        make_born(3, True), [((72, BY), F32)],
        [HALO, pltpu.VMEM((BX, NZ, BY), F32), pltpu.VMEM((512, 2 * BY), BF16)],
    )(scal, *one(d3), d3, d2, source, acc3, vel, *e, pick_cell, pick_y, s1, s2, s3, dot, smem=1)
    theirs = lax.ppermute(block, "gx", [(i, i ^ 1) for i in range(8)])
    payload, = call(pair_kernel, [((8, 72, BY), F32)])(block, theirs)
    same_core = [[2 * (2 * c + k) + g for c in range(4) for g in range(2)] for k in range(2)]
    arrived = lax.all_to_all(payload, ("gx", "gy"), 0, 0, axis_index_groups=same_core, tiled=True)
    predicted, stats = call(collect_kernel, [((64, BY), F32), ((16, 8, BY), F32)])(arrived)
    stats = lax.all_to_all(stats, "shot", 0, 0, tiled=True)
    image, residual = call(finish_kernel, [((32, BY), F32), ((4, NREC), F32)])(
        stats, predicted, scaled, traces[0])
    return image.reshape(4, BX, BY), residual[None]


def solution(mesh):
    return jax.shard_map(
        on_device,
        mesh=mesh,
        in_specs=(
            P("shot", None, "gx", "gy"),
            P("shot", None, "gx", "gy"),
            P(None, "gx", "gy"),
            P("shot", "gx", "gy"),
            P("shot", None, None),
            P("shot", None),
            P("shot", None),
            P("shot", None),
            P("shot"),
            P("shot"),
        ),
        out_specs=(P("shot", "gx", "gy"), P("shot", None, None)),
        check_vma=False,
    )
```

```python
import jax
import jax.numpy as jnp
from jax import lax
from jax.experimental import pallas as pl
from jax.experimental.pallas import tpu as pltpu
from jax.sharding import PartitionSpec as P

STEPS = 4
NZ, BX, BY = 64, 8, 128
NREC = 2048
F32, BF16, I32 = jnp.float32, jnp.bfloat16, jnp.int32
weights = (-205.0 / 72.0, 8.0 / 5.0, -1.0 / 5.0, 8.0 / 315.0, -1.0 / 560.0)


def position():
    gx, gy = lax.axis_index("gx"), lax.axis_index("gy")
    return gx & 1, gy, gx * BX, gy * BY


def call(kernel, outs, scratch=(), limit=24, flops=10_000_000):
    def run(*args, smem=0, hbm=0):
        spaces = [pltpu.SMEM] * smem + [pltpu.HBM] * hbm
        spaces = spaces + [pltpu.VMEM] * (len(args) - smem - hbm)
        specs = [pl.BlockSpec(memory_space=space) for space in spaces]
        return pl.pallas_call(
            kernel,
            out_shape=[jax.ShapeDtypeStruct(s, d) for s, d in outs],
            in_specs=specs,
            out_specs=[pl.BlockSpec(memory_space=pltpu.VMEM) for _ in outs],
            scratch_shapes=list(scratch),
            compiler_params=pltpu.CompilerParams(vmem_limit_bytes=limit * 1024 * 1024),
            cost_estimate=pl.CostEstimate(
                flops=flops, bytes_accessed=2_000_000, transcendentals=0
            ),
        )(*args)

    return run


def lanes(rows):
    return lax.broadcasted_iota(I32, (rows, BY), 1)


def near_edge(gy, lane):
    return ((gy == 0) & (lane >= BY - 4)) | ((gy == 1) & (lane < 4))


def send_edges(field, outer_ref, inner_ref, strip_ref, slot, scal):
    core, gy = scal[0], scal[1]
    keep = near_edge(gy, lanes(8))
    for i in range(4):
        outer_ref[slot, i] = field[4 * core + i]
        inner_ref[slot, i] = field[4 * (1 - core) + i]
    for half in range(2):
        sums = []
        for j in range(32):
            x, z = 4 * half + j // 8, 8 * (j % 8)
            turned = pltpu.roll(jnp.where(keep, field[x, z : z + 8], 0.0), 4 * j, 1)
            if j < 4:
                sums.append(turned)
            else:
                sums[j % 4] = sums[j % 4] + turned
        strip_ref[slot, 8 * half : 8 * half + 8] = (sums[0] + sums[1]) + (sums[2] + sums[3])


def interior(field, padded, part):
    lane = lanes(NZ)
    zero = jnp.zeros((8, BY), F32)
    for x in range(BX):
        padded[x, 0:8] = zero
        padded[x, 72:80] = zero
        padded[x, 8:72] = field[x]
    for x in range(BX):
        centre = field[x]
        result = (3.0 * weights[0]) * centre
        for k in range(1, 5):
            pairs = padded[x, 8 + k : 72 + k] + padded[x, 8 - k : 72 - k]
            if x + k < BX:
                pairs = pairs + field[x + k]
            if x - k >= 0:
                pairs = pairs + field[x - k]
            right = pltpu.roll(jnp.where(lane < k, 0.0, centre), BY - k, 1)
            left = pltpu.roll(jnp.where(lane >= BY - k, 0.0, centre), k, 1)
            result = result + weights[k] * (pairs + (right + left))
        part[x] = result


def interior_kernel(*refs):
    count = (len(refs) - 1) // 2
    for i in range(count):
        interior(refs[i], refs[-1], refs[count + i])


def receive(halo, outer_ref, inner_ref, strip_ref, slot, scal):
    core, gy = scal[0], scal[1]
    inside = ((scal[2] > 0) | (core == 1)) & ((scal[2] < 7 * BX) | (core == 0))
    for i in range(4):
        halo[4 * core + i] = jnp.where(inside, outer_ref[slot, i], 0.0)
        halo[4 * (1 - core) + i] = inner_ref[slot, i]
    packed = strip_ref[slot]
    place = lanes(16) & 3
    after, before = weights[4] * packed, weights[4] * packed
    for m in range(1, 4):
        after = after + weights[4 - m] * jnp.where(place >= m, pltpu.roll(packed, m, 1), 0.0)
        before = before + weights[4 - m] * jnp.where(place < 4 - m, pltpu.roll(packed, BY - m, 1), 0.0)
    return jnp.where(gy == 0, pltpu.roll(after, BY - 4, 1), pltpu.roll(before, 4, 1))


def complete(part, halo, strips, x, scal):
    keep = near_edge(scal[1], lanes(8))
    pieces = []
    for z in range(8):
        j = 8 * (x % 4) + z
        row = 8 * (x // 4)
        turned = pltpu.roll(strips[row : row + 8], (BY - 4 * j) % BY, 1)
        pieces.append(jnp.where(keep, turned, 0.0))
    result = part[x] + jnp.concatenate(pieces, axis=0)
    for k in range(1, 5):
        if x - k < 0:
            result = result + weights[k] * halo[4 + x - k]
        if x + k >= BX:
            result = result + weights[k] * halo[x + k - 4]
    return result


FIELD = ((BX, NZ, BY), F32)
PADDED = pltpu.VMEM((BX, 80, BY), F32)
HALO = pltpu.VMEM((BX, NZ, BY), F32)


def edges(count):
    return [((count, 4, NZ, BY), F32), ((count, 4, NZ, BY), F32), ((count, 16, BY), F32)]


def first_kernel(newer, newer_out, outer, inner, strip):
    scal = position()
    for x in range(BX):
        newer_out[x] = newer[pl.ds(x, NZ, stride=8), :]
    send_edges(newer_out, outer, inner, strip, 0, scal)


def two_pieces(values):
    high = values.astype(BF16)
    return high, (values - high.astype(F32)).astype(BF16)


def block(i):
    return pl.ds(pl.multiple_of(16 * i, 16), 16)


def wide(row):
    return jnp.broadcast_to(row, (16, NREC)).astype(BF16)


def inject(n, traces, pick_cell, pick_y, spread, inj):
    value = traces[n : n + 1, :]
    coarse = value.astype(BF16).astype(F32)
    high, low = wide(coarse), wide(value - coarse)

    def weigh(i, carry):
        picked = pick_y[block(i), :]
        spread[block(i), :] = picked * high
        spread[block(8 + i), :] = picked * low
        return carry

    lax.fori_loop(0, 8, weigh, 0)
    both = lax.dot_general(
        pick_cell[...], spread[...], (((1,), (1,)), ((), ())), preferred_element_type=F32
    )
    for x in range(BX):
        part = both[NZ * x : NZ * x + NZ]
        inj[x] = part[:, :BY] + part[:, BY:]


def make_inject(n):
    def kernel(shot, pick_cell, pick_y, inj, spread):
        inject(n, shot, pick_cell, pick_y, spread, inj)

    return kernel


def prepare_kernel(shot, inj, pick_cell, pick_y, at_depth, spread):
    scal = position()
    code = shot[4:5, :].astype(I32)
    lat_x = ((code >> 6) & 63) - scal[2]
    lat_y = (code >> 12) - scal[3]
    present = (lat_x >= 0) & (lat_x < BX) & (lat_y >= 0) & (lat_y < BY)
    depth = jnp.where(present, code & 63, -1)
    col = jnp.where(present, lat_y, -1)

    def hits(i, wanted):
        number = lax.broadcasted_iota(I32, (16, NREC), 0) + 16 * i
        return jnp.where(number == wanted, 1.0, 0.0).astype(BF16)

    def depths(i, carry):
        at_depth[block(i), :] = hits(i, depth)
        return carry

    lax.fori_loop(0, 4, depths, 0)

    def planes(x, carry):
        here = wide(jnp.where(lat_x == x, 1.0, 0.0))
        for i in range(4):
            pick_cell[block(4 * x + i), :] = at_depth[16 * i : 16 * i + 16] * here
        return carry

    lax.fori_loop(0, BX, planes, 0)

    def columns(i, carry):
        pick_y[block(i), :] = hits(i, col)
        return carry

    lax.fori_loop(0, 8, columns, 0)
    inject(3, shot, pick_cell, pick_y, spread, inj)


def planes_kernel(older_in, vel_in, older, vel):
    for x in range(BX):
        older[x] = older_in[pl.ds(x, NZ, stride=8), :]
        vel[x] = vel_in[pl.ds(x, NZ, stride=8), :]


def forward1_kernel(part, newer, older, vel, inj3, outer, inner, strip, acc, nxt, q, outer_o, inner_o, strip_o, halo):
    scal = position()
    strips = receive(halo, outer, inner, strip, 0, scal)
    for x in range(BX):
        a = vel[x] * complete(part, halo, strips, x, scal)
        acc[x] = a
        nxt[x] = (2.0 * newer[x] - older[x]) + a
        q[x] = vel[x] * inj3[x]
    send_edges(nxt, outer_o, inner_o, strip_o, 0, scal)
    send_edges(q, outer_o, inner_o, strip_o, 1, scal)


def make_forward(moment):
    def kernel(part, part_q, newer, older, vel, inj, inj3, *rest):
        scal = position()
        if moment == 2:
            later, rest = rest[0], rest[1:]
        outer, inner, strip, acc, nxt, p, q, outer_o, inner_o, strip_o, halo, halo_q = rest
        strips = receive(halo, outer, inner, strip, 0, scal)
        for x in range(BX):
            a = vel[x] * complete(part, halo, strips, x, scal)
            acc[x] = a
            nxt[x] = (2.0 * newer[x] - older[x]) + a
        send_edges(nxt, outer_o, inner_o, strip_o, 0, scal)
        strips = receive(halo_q, outer, inner, strip, 1, scal)
        for x in range(BX):
            before = 2.0 * inj3[x] if moment == 1 else 2.0 * later[x] - inj3[x]
            value = (before + complete(part_q, halo_q, strips, x, scal)) + inj[x]
            p[x] = value
            q[x] = vel[x] * value
        send_edges(q, outer_o, inner_o, strip_o, 1, scal)

    return kernel


def window_kernel(aperture_x, aperture_y, after, mask):
    _, _, first_x, first_y = position()
    column = lanes(8) + first_y
    inside_y = (column >= aperture_y[0]) & (column < aperture_y[0] + 192)
    for x in range(BX):
        inside_x = (first_x + x >= aperture_x[0]) & (first_x + x < aperture_x[0] + 48)
        mask[x] = jnp.where(inside_y & inside_x, 1.0, 0.0)


def masked(mask, x, values):
    inside = jnp.broadcast_to(mask[x, 0:1], (NZ, BY)) > 0.5
    return jnp.where(inside, values, 0.0)


def last_kernel(mask, part, part_q, vel, inj0, inj3, latest, later, acc0, acc1, acc2, outer, inner, strip, acc3, grad, halo, halo_q):
    scal = position()
    strips = receive(halo, outer, inner, strip, 0, scal)
    strips_q = receive(halo_q, outer, inner, strip, 1, scal)
    for x in range(BX):
        a = vel[x] * complete(part, halo, strips, x, scal)
        acc3[x] = a
        p0 = ((2.0 * later[x] - latest[x]) + complete(part_q, halo_q, strips_q, x, scal)) + inj0[x]
        total = ((a * inj3[x] + acc2[x] * latest[x]) + acc1[x] * later[x]) + acc0[x] * p0
        grad[pl.ds(x, NZ, stride=8), :] = masked(mask, x, total)


def gradient_kernel(parts, pre, scaled, copies, dot):
    total = parts[0:32]
    for s in range(1, 16):
        total = total + parts[32 * s : 32 * s + 32]
    value = pre[...] * total
    scaled[...] = value
    for s in range(16):
        copies[32 * s : 32 * s + 32] = value
    product = total * value
    dot[...] = (product[0:8] + product[8:16]) + (product[16:24] + product[24:32])


def born1_kernel(mask, full, acc0, source, d, outer_o, inner_o, strip_o):
    scal = position()
    for x in range(BX):
        s = masked(mask, x, full[pl.ds(x, NZ, stride=8), :])
        source[x] = s
        d[x] = s * acc0[x]
    send_edges(d, outer_o, inner_o, strip_o, 0, scal)


def make_born(moment, last):
    def kernel(part, now, before, source, acc, vel, outer, inner, strip, *rest):
        scal = position()
        if last:
            pick_cell, pick_y, s1, s2, s3, dot, block, halo, d, pieces = rest
        else:
            samples, d, outer_o, inner_o, strip_o, halo = rest
        strips = receive(halo, outer, inner, strip, 0, scal)
        for x in range(BX):
            base = 2.0 * now[x]
            if moment > 1:
                base = base - before[x]
            d[x] = (base + vel[x] * complete(part, halo, strips, x, scal)) + source[x] * acc[x]
        if not last:
            send_edges(d, outer_o, inner_o, strip_o, 0, scal)
            return
        s4 = sampled(d, pieces, pick_cell, pick_y)
        energy = jnp.zeros((1, BY), F32)
        for n, values in enumerate((s1[...], s2[...], s3[...], s4)):
            for j in range(16):
                piece = values[:, BY * j : BY * j + BY]
                block[16 * n + j : 16 * n + j + 1, :] = piece
                energy = energy + piece * piece
        block[64:72, :] = jnp.zeros((8, BY), F32)
        block[64:65, :] = energy
        block[65:66, :] = jnp.sum(dot[...], axis=0, keepdims=True)

    return kernel


def sampled(field, pieces, pick_cell, pick_y):
    for x in range(BX):
        high, low = two_pieces(field[x])
        pieces[NZ * x : NZ * x + NZ, :BY] = high
        pieces[NZ * x : NZ * x + NZ, BY:] = low
    at_cell = lax.dot_general(
        pieces[...], pick_cell[...], (((0,), (0,)), ((), ())), preferred_element_type=F32
    )
    chosen = (at_cell[:BY] + at_cell[BY:]) * pick_y[...].astype(F32)
    return jnp.sum(chosen, axis=0, keepdims=True)


def sample_kernel(field, pick_cell, pick_y, out, pieces):
    out[...] = sampled(field, pieces, pick_cell, pick_y)


def pair_kernel(mine, theirs, copies):
    total = mine[...] + theirs[...]
    for i in range(8):
        copies[i] = total


def collect_kernel(arrived, predicted, copies):
    total = arrived[0]
    for i in range(1, 8):
        total = total + arrived[i]
    predicted[...] = total[0:64]
    for i in range(16):
        copies[i] = total[64:72]


def finish_kernel(stats, predicted, scaled, traces, image, residual):
    total = stats[0]
    for i in range(1, 16):
        total = total + stats[i]
    energy = jnp.sum(total[0:1], axis=1, keepdims=True)
    dot = jnp.sum(total[1:2], axis=1, keepdims=True)
    step = dot / (energy + 1e-6)
    image[...] = step * scaled[...]
    for n in range(STEPS):
        for j in range(16):
            at = pl.ds(BY * j, BY)
            row = predicted[16 * n + j : 16 * n + j + 1, :]
            residual[n : n + 1, at] = traces[n : n + 1, at] - step * row


def exchange(outer, inner, strip):
    chips = [(2 * i + 1, (2 * i + 2) % 8) for i in range(4)]
    across = chips + [(b, a) for a, b in chips]
    swap = [(i, i ^ 1) for i in range(8)]
    return (
        lax.ppermute(outer, "gx", across),
        lax.ppermute(inner, "gx", swap),
        lax.ppermute(strip, "gy", [(0, 1), (1, 0)]),
    )


def on_device(older_field, newer_field, velocity, preconditioner, traces,
              receiver_z, receiver_x, receiver_y, aperture_x, aperture_y):
    flat = (NZ * BX, BY)
    newer, *e = call(first_kernel, [FIELD] + edges(1))(newer_field.reshape(flat))
    e = exchange(*e)
    code = receiver_z | (receiver_x << 6) | (receiver_y << 12)
    shot = jnp.concatenate([traces[0], code.astype(F32)], axis=0)
    inj3, pick_cell, pick_y = call(
        prepare_kernel,
        [FIELD, ((512, NREC), BF16), ((BY, NREC), BF16)],
        [pltpu.VMEM((NZ, NREC), BF16), pltpu.VMEM((2 * BY, NREC), BF16)],
    )(shot)

    def injection(n):
        return call(make_inject(n), [FIELD], [pltpu.VMEM((2 * BY, NREC), BF16)], flops=1_000_000_000)(
            shot, pick_cell, pick_y)[0]

    one = call(interior_kernel, [FIELD], [PADDED])
    two = call(interior_kernel, [FIELD] * 2, [PADDED])
    older, vel = call(planes_kernel, [FIELD, FIELD])(older_field.reshape(flat), velocity.reshape(flat))
    acc0, u1, q, *e = call(forward1_kernel, [FIELD] * 3 + edges(2), [HALO])(
        *one(newer), newer, older, vel, inj3, *e)
    e = exchange(*e)
    acc1, u2, p2, q, *e = call(make_forward(1), [FIELD] * 4 + edges(2), [HALO] * 2)(
        *two(u1, q), u1, newer, vel, injection(2), inj3, *e)
    e = exchange(*e)
    acc2, u3, p1, q, *e = call(make_forward(2), [FIELD] * 4 + edges(2), [HALO] * 2)(
        *two(u2, q), u2, u1, vel, injection(1), inj3, p2, *e)
    e = exchange(*e)
    mask, = call(window_kernel, [((BX, 8, BY), F32)])(aperture_x, aperture_y, u2, smem=2)
    acc3, grad = call(last_kernel, [FIELD, (flat, F32)], [HALO] * 2)(
        mask, *two(u3, q), vel, injection(0), inj3, p2, p1, acc0, acc1, acc2, *e)
    parts = lax.all_to_all(grad.reshape(16, 4, BX, BY), "shot", 0, 0, tiled=True)
    scaled, copies, dot = call(
        gradient_kernel, [((32, BY), F32), (flat, F32), ((8, BY), F32)])(
        parts.reshape(flat), preconditioner.reshape(32, BY))
    full = lax.all_to_all(copies.reshape(16, 4, BX, BY), "shot", 0, 0, tiled=True)
    source, d1, *e = call(born1_kernel, [FIELD, FIELD] + edges(1))(
        mask, full.reshape(flat), acc0)
    e = exchange(*e)
    sample = call(sample_kernel, [((1, NREC), F32)], [pltpu.VMEM((512, 2 * BY), BF16)], flops=600_000_000)
    s1, = sample(d1, pick_cell, pick_y)
    d2, *e = call(make_born(1, False), [FIELD] + edges(1), [HALO])(
        *one(d1), d1, d1, source, acc1, vel, *e, s1)
    e = exchange(*e)
    s2, = sample(d2, pick_cell, pick_y)
    d3, *e = call(make_born(2, False), [FIELD] + edges(1), [HALO])(
        *one(d2), d2, d1, source, acc2, vel, *e, s2)
    e = exchange(*e)
    s3, = sample(d3, pick_cell, pick_y)
    block, = call(
        make_born(3, True), [((72, BY), F32)],
        [HALO, pltpu.VMEM((BX, NZ, BY), F32), pltpu.VMEM((512, 2 * BY), BF16)],
    )(*one(d3), d3, d2, source, acc3, vel, *e, pick_cell, pick_y, s1, s2, s3, dot)
    theirs = lax.ppermute(block, "gx", [(i, i ^ 1) for i in range(8)])
    payload, = call(pair_kernel, [((8, 72, BY), F32)])(block, theirs)
    same_core = [[2 * (2 * c + k) + g for c in range(4) for g in range(2)] for k in range(2)]
    arrived = lax.all_to_all(payload, ("gx", "gy"), 0, 0, axis_index_groups=same_core, tiled=True)
    predicted, stats = call(collect_kernel, [((64, BY), F32), ((16, 8, BY), F32)])(arrived)
    stats = lax.all_to_all(stats, "shot", 0, 0, tiled=True)
    image, residual = call(finish_kernel, [((32, BY), F32), ((4, NREC), F32)])(
        stats, predicted, scaled, traces[0])
    return image.reshape(4, BX, BY), residual[None]


def solution(mesh):
    return jax.shard_map(
        on_device,
        mesh=mesh,
        in_specs=(
            P("shot", None, "gx", "gy"),
            P("shot", None, "gx", "gy"),
            P(None, "gx", "gy"),
            P("shot", "gx", "gy"),
            P("shot", None, None),
            P("shot", None),
            P("shot", None),
            P("shot", None),
            P("shot"),
            P("shot"),
        ),
        out_specs=(P("shot", "gx", "gy"), P("shot", None, None)),
        check_vma=False,
    )
```

```python
import jax
import jax.numpy as jnp
from jax import lax
from jax.experimental import pallas as pl
from jax.experimental.pallas import tpu as pltpu
from jax.sharding import PartitionSpec as P

STEPS = 4
NZ, BX, BY = 64, 8, 128
NREC = 2048
F32, BF16, I32 = jnp.float32, jnp.bfloat16, jnp.int32
weights = (-205.0 / 72.0, 8.0 / 5.0, -1.0 / 5.0, 8.0 / 315.0, -1.0 / 560.0)


def position():
    gx, gy = lax.axis_index("gx"), lax.axis_index("gy")
    return gx & 1, gy, gx * BX, gy * BY


def call(kernel, outs, scratch=(), limit=24, flops=10_000_000):
    def run(*args, smem=0, hbm=0):
        spaces = [pltpu.SMEM] * smem + [pltpu.HBM] * hbm
        spaces = spaces + [pltpu.VMEM] * (len(args) - smem - hbm)
        specs = [pl.BlockSpec(memory_space=space) for space in spaces]
        return pl.pallas_call(
            kernel,
            out_shape=[jax.ShapeDtypeStruct(s, d) for s, d in outs],
            in_specs=specs,
            out_specs=[pl.BlockSpec(memory_space=pltpu.VMEM) for _ in outs],
            scratch_shapes=list(scratch),
            compiler_params=pltpu.CompilerParams(vmem_limit_bytes=limit * 1024 * 1024),
            cost_estimate=pl.CostEstimate(
                flops=flops, bytes_accessed=2_000_000, transcendentals=0
            ),
        )(*args)

    return run


def lanes(rows):
    return lax.broadcasted_iota(I32, (rows, BY), 1)


def near_edge(gy, lane):
    return ((gy == 0) & (lane >= BY - 4)) | ((gy == 1) & (lane < 4))


def send_edges(field, outer_ref, inner_ref, strip_ref, slot, scal):
    core, gy = scal[0], scal[1]
    keep = near_edge(gy, lanes(8))
    for i in range(4):
        outer_ref[slot, i] = field[4 * core + i]
        inner_ref[slot, i] = field[4 * (1 - core) + i]
    for half in range(2):
        sums = []
        for j in range(32):
            x, z = 4 * half + j // 8, 8 * (j % 8)
            turned = pltpu.roll(jnp.where(keep, field[x, z : z + 8], 0.0), 4 * j, 1)
            if j < 4:
                sums.append(turned)
            else:
                sums[j % 4] = sums[j % 4] + turned
        strip_ref[slot, 8 * half : 8 * half + 8] = (sums[0] + sums[1]) + (sums[2] + sums[3])


def interior(field, padded, part):
    lane = lanes(NZ)
    zero = jnp.zeros((8, BY), F32)
    for x in range(BX):
        padded[x, 0:8] = zero
        padded[x, 72:80] = zero
        padded[x, 8:72] = field[x]
    for x in range(BX):
        centre = field[x]
        result = (3.0 * weights[0]) * centre
        for k in range(1, 5):
            pairs = padded[x, 8 + k : 72 + k] + padded[x, 8 - k : 72 - k]
            if x + k < BX:
                pairs = pairs + field[x + k]
            if x - k >= 0:
                pairs = pairs + field[x - k]
            right = pltpu.roll(jnp.where(lane < k, 0.0, centre), BY - k, 1)
            left = pltpu.roll(jnp.where(lane >= BY - k, 0.0, centre), k, 1)
            result = result + weights[k] * (pairs + (right + left))
        part[x] = result


def interior_kernel(*refs):
    count = (len(refs) - 1) // 2
    for i in range(count):
        interior(refs[i], refs[-1], refs[count + i])


def receive(halo, outer_ref, inner_ref, strip_ref, slot, scal):
    core, gy = scal[0], scal[1]
    inside = ((scal[2] > 0) | (core == 1)) & ((scal[2] < 7 * BX) | (core == 0))
    for i in range(4):
        halo[4 * core + i] = jnp.where(inside, outer_ref[slot, i], 0.0)
        halo[4 * (1 - core) + i] = inner_ref[slot, i]
    packed = strip_ref[slot]
    place = lanes(16) & 3
    after, before = weights[4] * packed, weights[4] * packed
    for m in range(1, 4):
        after = after + weights[4 - m] * jnp.where(place >= m, pltpu.roll(packed, m, 1), 0.0)
        before = before + weights[4 - m] * jnp.where(place < 4 - m, pltpu.roll(packed, BY - m, 1), 0.0)
    return jnp.where(gy == 0, pltpu.roll(after, BY - 4, 1), pltpu.roll(before, 4, 1))


def complete(part, halo, strips, x, scal):
    keep = near_edge(scal[1], lanes(8))
    pieces = []
    for z in range(8):
        j = 8 * (x % 4) + z
        row = 8 * (x // 4)
        turned = pltpu.roll(strips[row : row + 8], (BY - 4 * j) % BY, 1)
        pieces.append(jnp.where(keep, turned, 0.0))
    result = part[x] + jnp.concatenate(pieces, axis=0)
    for k in range(1, 5):
        if x - k < 0:
            result = result + weights[k] * halo[4 + x - k]
        if x + k >= BX:
            result = result + weights[k] * halo[x + k - 4]
    return result


FIELD = ((BX, NZ, BY), F32)
PADDED = pltpu.VMEM((BX, 80, BY), F32)
HALO = pltpu.VMEM((BX, NZ, BY), F32)


def edges(count):
    return [((count, 4, NZ, BY), F32), ((count, 4, NZ, BY), F32), ((count, 16, BY), F32)]


def first_kernel(newer, newer_out, outer, inner, strip):
    scal = position()
    for x in range(BX):
        newer_out[x] = newer[pl.ds(x, NZ, stride=8), :]
    send_edges(newer_out, outer, inner, strip, 0, scal)


def two_pieces(values):
    high = values.astype(BF16)
    return high, (values - high.astype(F32)).astype(BF16)


def block(i):
    return pl.ds(pl.multiple_of(16 * i, 16), 16)


def wide(row):
    return jnp.broadcast_to(row, (16, NREC)).astype(BF16)


def inject(n, traces, pick_cell, pick_y, spread, inj):
    value = traces[n : n + 1, :]
    coarse = value.astype(BF16).astype(F32)
    high, low = wide(coarse), wide(value - coarse)

    def weigh(i, carry):
        picked = pick_y[block(i), :]
        spread[block(i), :] = picked * high
        spread[block(8 + i), :] = picked * low
        return carry

    lax.fori_loop(0, 8, weigh, 0)
    both = lax.dot_general(
        pick_cell[...], spread[...], (((1,), (1,)), ((), ())), preferred_element_type=F32
    )
    for x in range(BX):
        part = both[NZ * x : NZ * x + NZ]
        inj[x] = part[:, :BY] + part[:, BY:]


def make_inject(n):
    def kernel(shot, pick_cell, pick_y, inj, spread):
        inject(n, shot, pick_cell, pick_y, spread, inj)

    return kernel


def prepare_kernel(shot, inj, pick_cell, pick_y, at_depth, spread):
    scal = position()
    code = shot[4:5, :].astype(I32)
    lat_x = ((code >> 6) & 63) - scal[2]
    lat_y = (code >> 12) - scal[3]
    present = (lat_x >= 0) & (lat_x < BX) & (lat_y >= 0) & (lat_y < BY)
    depth = jnp.where(present, code & 63, -1)
    col = jnp.where(present, lat_y, -1)

    def hits(i, wanted):
        number = lax.broadcasted_iota(I32, (16, NREC), 0) + 16 * i
        return jnp.where(number == wanted, 1.0, 0.0).astype(BF16)

    def depths(i, carry):
        at_depth[block(i), :] = hits(i, depth)
        return carry

    lax.fori_loop(0, 4, depths, 0)

    def planes(x, carry):
        here = wide(jnp.where(lat_x == x, 1.0, 0.0))
        for i in range(4):
            pick_cell[block(4 * x + i), :] = at_depth[16 * i : 16 * i + 16] * here
        return carry

    lax.fori_loop(0, BX, planes, 0)

    def columns(i, carry):
        pick_y[block(i), :] = hits(i, col)
        return carry

    lax.fori_loop(0, 8, columns, 0)
    inject(3, shot, pick_cell, pick_y, spread, inj)


def planes_kernel(both, older, vel):
    for x in range(BX):
        older[x] = both[pl.ds(x, NZ, stride=8), :]
        vel[x] = both[pl.ds(NZ * BX + x, NZ, stride=8), :]


def forward1_kernel(part, newer, older, vel, inj3, outer, inner, strip, acc, nxt, q, outer_o, inner_o, strip_o, halo):
    scal = position()
    strips = receive(halo, outer, inner, strip, 0, scal)
    for x in range(BX):
        a = vel[x] * complete(part, halo, strips, x, scal)
        acc[x] = a
        nxt[x] = (2.0 * newer[x] - older[x]) + a
        q[x] = vel[x] * inj3[x]
    send_edges(nxt, outer_o, inner_o, strip_o, 0, scal)
    send_edges(q, outer_o, inner_o, strip_o, 1, scal)


def make_forward(moment):
    def kernel(part, part_q, newer, older, vel, inj, inj3, *rest):
        scal = position()
        if moment == 2:
            later, rest = rest[0], rest[1:]
        outer, inner, strip, acc, nxt, p, q, outer_o, inner_o, strip_o, halo, halo_q = rest
        strips = receive(halo, outer, inner, strip, 0, scal)
        for x in range(BX):
            a = vel[x] * complete(part, halo, strips, x, scal)
            acc[x] = a
            nxt[x] = (2.0 * newer[x] - older[x]) + a
        send_edges(nxt, outer_o, inner_o, strip_o, 0, scal)
        strips = receive(halo_q, outer, inner, strip, 1, scal)
        for x in range(BX):
            before = 2.0 * inj3[x] if moment == 1 else 2.0 * later[x] - inj3[x]
            value = (before + complete(part_q, halo_q, strips, x, scal)) + inj[x]
            p[x] = value
            q[x] = vel[x] * value
        send_edges(q, outer_o, inner_o, strip_o, 1, scal)

    return kernel


def window_kernel(aperture_x, aperture_y, after, mask):
    _, _, first_x, first_y = position()
    column = lanes(8) + first_y
    inside_y = (column >= aperture_y[0]) & (column < aperture_y[0] + 192)
    for x in range(BX):
        inside_x = (first_x + x >= aperture_x[0]) & (first_x + x < aperture_x[0] + 48)
        mask[x] = jnp.where(inside_y & inside_x, 1.0, 0.0)


def masked(mask, x, values):
    inside = jnp.broadcast_to(mask[x, 0:1], (NZ, BY)) > 0.5
    return jnp.where(inside, values, 0.0)


def last_kernel(mask, part, part_q, vel, inj0, inj3, latest, later, acc0, acc1, acc2, outer, inner, strip, acc3, grad, halo, halo_q):
    scal = position()
    strips = receive(halo, outer, inner, strip, 0, scal)
    strips_q = receive(halo_q, outer, inner, strip, 1, scal)
    for x in range(BX):
        a = vel[x] * complete(part, halo, strips, x, scal)
        acc3[x] = a
        p0 = ((2.0 * later[x] - latest[x]) + complete(part_q, halo_q, strips_q, x, scal)) + inj0[x]
        total = ((a * inj3[x] + acc2[x] * latest[x]) + acc1[x] * later[x]) + acc0[x] * p0
        grad[pl.ds(x, NZ, stride=8), :] = masked(mask, x, total)


def gradient_kernel(parts, pre, scaled, copies, dot):
    total = parts[0:32]
    for s in range(1, 16):
        total = total + parts[32 * s : 32 * s + 32]
    value = pre[...] * total
    scaled[...] = value
    for s in range(16):
        copies[32 * s : 32 * s + 32] = value
    product = total * value
    dot[...] = (product[0:8] + product[8:16]) + (product[16:24] + product[24:32])


def born1_kernel(mask, full, acc0, source, d, outer_o, inner_o, strip_o):
    scal = position()
    for x in range(BX):
        s = masked(mask, x, full[pl.ds(x, NZ, stride=8), :])
        source[x] = s
        d[x] = s * acc0[x]
    send_edges(d, outer_o, inner_o, strip_o, 0, scal)


def make_born(moment, last):
    def kernel(part, now, before, source, acc, vel, outer, inner, strip, *rest):
        scal = position()
        if last:
            pick_cell, pick_y, s1, s2, s3, dot, block, halo, d, pieces = rest
        else:
            samples, d, outer_o, inner_o, strip_o, halo = rest
        strips = receive(halo, outer, inner, strip, 0, scal)
        for x in range(BX):
            base = 2.0 * now[x]
            if moment > 1:
                base = base - before[x]
            d[x] = (base + vel[x] * complete(part, halo, strips, x, scal)) + source[x] * acc[x]
        if not last:
            send_edges(d, outer_o, inner_o, strip_o, 0, scal)
            return
        s4 = sampled(d, pieces, pick_cell, pick_y)
        energy = jnp.zeros((1, BY), F32)
        for n, values in enumerate((s1[...], s2[...], s3[...], s4)):
            for j in range(16):
                piece = values[:, BY * j : BY * j + BY]
                block[16 * n + j : 16 * n + j + 1, :] = piece
                energy = energy + piece * piece
        block[64:72, :] = jnp.zeros((8, BY), F32)
        block[64:65, :] = energy
        block[65:66, :] = jnp.sum(dot[...], axis=0, keepdims=True)

    return kernel


def sampled(field, pieces, pick_cell, pick_y):
    for x in range(BX):
        high, low = two_pieces(field[x])
        pieces[NZ * x : NZ * x + NZ, :BY] = high
        pieces[NZ * x : NZ * x + NZ, BY:] = low
    at_cell = lax.dot_general(
        pieces[...], pick_cell[...], (((0,), (0,)), ((), ())), preferred_element_type=F32
    )
    chosen = (at_cell[:BY] + at_cell[BY:]) * pick_y[...].astype(F32)
    return jnp.sum(chosen, axis=0, keepdims=True)


def sample_kernel(field, pick_cell, pick_y, out, pieces):
    out[...] = sampled(field, pieces, pick_cell, pick_y)


def pair_kernel(mine, theirs, copies):
    total = mine[...] + theirs[...]
    for i in range(8):
        copies[i] = total


def collect_kernel(arrived, predicted, copies):
    total = arrived[0]
    for i in range(1, 8):
        total = total + arrived[i]
    predicted[...] = total[0:64]
    for i in range(16):
        copies[i] = total[64:72]


def finish_kernel(stats, predicted, scaled, traces, image, residual):
    total = stats[0]
    for i in range(1, 16):
        total = total + stats[i]
    energy = jnp.sum(total[0:1], axis=1, keepdims=True)
    dot = jnp.sum(total[1:2], axis=1, keepdims=True)
    step = dot / (energy + 1e-6)
    image[...] = step * scaled[...]
    for n in range(STEPS):
        for j in range(16):
            at = pl.ds(BY * j, BY)
            row = predicted[16 * n + j : 16 * n + j + 1, :]
            residual[n : n + 1, at] = traces[n : n + 1, at] - step * row


def exchange(outer, inner, strip):
    chips = [(2 * i + 1, (2 * i + 2) % 8) for i in range(4)]
    across = chips + [(b, a) for a, b in chips]
    swap = [(i, i ^ 1) for i in range(8)]
    return (
        lax.ppermute(outer, "gx", across),
        lax.ppermute(inner, "gx", swap),
        lax.ppermute(strip, "gy", [(0, 1), (1, 0)]),
    )


def on_device(older_field, newer_field, velocity, preconditioner, traces,
              receiver_z, receiver_x, receiver_y, aperture_x, aperture_y):
    flat = (NZ * BX, BY)
    newer, *e = call(first_kernel, [FIELD] + edges(1))(newer_field.reshape(flat))
    e = exchange(*e)
    code = receiver_z | (receiver_x << 6) | (receiver_y << 12)
    shot = jnp.concatenate([traces[0], code.astype(F32)], axis=0)
    inj3, pick_cell, pick_y = call(
        prepare_kernel,
        [FIELD, ((512, NREC), BF16), ((BY, NREC), BF16)],
        [pltpu.VMEM((NZ, NREC), BF16), pltpu.VMEM((2 * BY, NREC), BF16)],
    )(shot)

    def injection(n):
        return call(make_inject(n), [FIELD], [pltpu.VMEM((2 * BY, NREC), BF16)], flops=1_000_000_000)(
            shot, pick_cell, pick_y)[0]

    one = call(interior_kernel, [FIELD], [PADDED])
    two = call(interior_kernel, [FIELD] * 2, [PADDED])
    both = jnp.concatenate([older_field.reshape(flat), velocity.reshape(flat)], axis=0)
    older, vel = call(planes_kernel, [FIELD, FIELD])(both)
    acc0, u1, q, *e = call(forward1_kernel, [FIELD] * 3 + edges(2), [HALO])(
        *one(newer), newer, older, vel, inj3, *e)
    e = exchange(*e)
    acc1, u2, p2, q, *e = call(make_forward(1), [FIELD] * 4 + edges(2), [HALO] * 2)(
        *two(u1, q), u1, newer, vel, injection(2), inj3, *e)
    e = exchange(*e)
    acc2, u3, p1, q, *e = call(make_forward(2), [FIELD] * 4 + edges(2), [HALO] * 2)(
        *two(u2, q), u2, u1, vel, injection(1), inj3, p2, *e)
    e = exchange(*e)
    mask, = call(window_kernel, [((BX, 8, BY), F32)])(aperture_x, aperture_y, u2, smem=2)
    acc3, grad = call(last_kernel, [FIELD, (flat, F32)], [HALO] * 2)(
        mask, *two(u3, q), vel, injection(0), inj3, p2, p1, acc0, acc1, acc2, *e)
    parts = lax.all_to_all(grad.reshape(16, 4, BX, BY), "shot", 0, 0, tiled=True)
    scaled, copies, dot = call(
        gradient_kernel, [((32, BY), F32), (flat, F32), ((8, BY), F32)])(
        parts.reshape(flat), preconditioner.reshape(32, BY))
    full = lax.all_to_all(copies.reshape(16, 4, BX, BY), "shot", 0, 0, tiled=True)
    source, d1, *e = call(born1_kernel, [FIELD, FIELD] + edges(1))(
        mask, full.reshape(flat), acc0)
    e = exchange(*e)
    sample = call(sample_kernel, [((1, NREC), F32)], [pltpu.VMEM((512, 2 * BY), BF16)], flops=600_000_000)
    s1, = sample(d1, pick_cell, pick_y)
    d2, *e = call(make_born(1, False), [FIELD] + edges(1), [HALO])(
        *one(d1), d1, d1, source, acc1, vel, *e, s1)
    e = exchange(*e)
    s2, = sample(d2, pick_cell, pick_y)
    d3, *e = call(make_born(2, False), [FIELD] + edges(1), [HALO])(
        *one(d2), d2, d1, source, acc2, vel, *e, s2)
    e = exchange(*e)
    s3, = sample(d3, pick_cell, pick_y)
    block, = call(
        make_born(3, True), [((72, BY), F32)],
        [HALO, pltpu.VMEM((BX, NZ, BY), F32), pltpu.VMEM((512, 2 * BY), BF16)],
    )(*one(d3), d3, d2, source, acc3, vel, *e, pick_cell, pick_y, s1, s2, s3, dot)
    theirs = lax.ppermute(block, "gx", [(i, i ^ 1) for i in range(8)])
    payload, = call(pair_kernel, [((8, 72, BY), F32)])(block, theirs)
    same_core = [[2 * (2 * c + k) + g for c in range(4) for g in range(2)] for k in range(2)]
    arrived = lax.all_to_all(payload, ("gx", "gy"), 0, 0, axis_index_groups=same_core, tiled=True)
    predicted, stats = call(collect_kernel, [((64, BY), F32), ((16, 8, BY), F32)])(arrived)
    stats = lax.all_to_all(stats, "shot", 0, 0, tiled=True)
    image, residual = call(finish_kernel, [((32, BY), F32), ((4, NREC), F32)])(
        stats, predicted, scaled, traces[0])
    return image.reshape(4, BX, BY), residual[None]


def solution(mesh):
    return jax.shard_map(
        on_device,
        mesh=mesh,
        in_specs=(
            P("shot", None, "gx", "gy"),
            P("shot", None, "gx", "gy"),
            P(None, "gx", "gy"),
            P("shot", "gx", "gy"),
            P("shot", None, None),
            P("shot", None),
            P("shot", None),
            P("shot", None),
            P("shot"),
            P("shot"),
        ),
        out_specs=(P("shot", "gx", "gy"), P("shot", None, None)),
        check_vma=False,
    )
```

```python
import jax
import jax.numpy as jnp
from jax import lax
from jax.experimental import pallas as pl
from jax.experimental.pallas import tpu as pltpu
from jax.sharding import PartitionSpec as P

STEPS = 4
NZ, BX, BY = 64, 8, 128
NREC = 2048
F32, BF16, I32 = jnp.float32, jnp.bfloat16, jnp.int32
weights = (-205.0 / 72.0, 8.0 / 5.0, -1.0 / 5.0, 8.0 / 315.0, -1.0 / 560.0)


def position():
    gx, gy = lax.axis_index("gx"), lax.axis_index("gy")
    return gx & 1, gy, gx * BX, gy * BY


def call(kernel, outs, scratch=(), limit=24, flops=10_000_000):
    def run(*args, smem=0, hbm=0):
        spaces = [pltpu.SMEM] * smem + [pltpu.HBM] * hbm
        spaces = spaces + [pltpu.VMEM] * (len(args) - smem - hbm)
        specs = [pl.BlockSpec(memory_space=space) for space in spaces]
        return pl.pallas_call(
            kernel,
            out_shape=[jax.ShapeDtypeStruct(s, d) for s, d in outs],
            in_specs=specs,
            out_specs=[pl.BlockSpec(memory_space=pltpu.VMEM) for _ in outs],
            scratch_shapes=list(scratch),
            compiler_params=pltpu.CompilerParams(vmem_limit_bytes=limit * 1024 * 1024),
            cost_estimate=pl.CostEstimate(
                flops=flops, bytes_accessed=2_000_000, transcendentals=0
            ),
        )(*args)

    return run


def lanes(rows):
    return lax.broadcasted_iota(I32, (rows, BY), 1)


def near_edge(gy, lane):
    return ((gy == 0) & (lane >= BY - 4)) | ((gy == 1) & (lane < 4))


def send_edges(field, outer_ref, inner_ref, strip_ref, slot, scal):
    core, gy = scal[0], scal[1]
    keep = near_edge(gy, lanes(8))
    for i in range(4):
        outer_ref[slot, i] = field[4 * core + i]
        inner_ref[slot, i] = field[4 * (1 - core) + i]
    for half in range(2):
        sums = []
        for j in range(32):
            x, z = 4 * half + j // 8, 8 * (j % 8)
            turned = pltpu.roll(jnp.where(keep, field[x, z : z + 8], 0.0), 4 * j, 1)
            if j < 4:
                sums.append(turned)
            else:
                sums[j % 4] = sums[j % 4] + turned
        strip_ref[slot, 8 * half : 8 * half + 8] = (sums[0] + sums[1]) + (sums[2] + sums[3])


def interior(field, padded, part):
    lane = lanes(NZ)
    zero = jnp.zeros((8, BY), F32)
    for x in range(BX):
        padded[x, 0:8] = zero
        padded[x, 72:80] = zero
        padded[x, 8:72] = field[x]
    for x in range(BX):
        centre = field[x]
        result = (3.0 * weights[0]) * centre
        for k in range(1, 5):
            pairs = padded[x, 8 + k : 72 + k] + padded[x, 8 - k : 72 - k]
            if x + k < BX:
                pairs = pairs + field[x + k]
            if x - k >= 0:
                pairs = pairs + field[x - k]
            right = pltpu.roll(jnp.where(lane < k, 0.0, centre), BY - k, 1)
            left = pltpu.roll(jnp.where(lane >= BY - k, 0.0, centre), k, 1)
            result = result + weights[k] * (pairs + (right + left))
        part[x] = result


def interior_kernel(*refs):
    count = (len(refs) - 1) // 2
    for i in range(count):
        interior(refs[i], refs[-1], refs[count + i])


def receive(halo, outer_ref, inner_ref, strip_ref, slot, scal):
    core, gy = scal[0], scal[1]
    inside = ((scal[2] > 0) | (core == 1)) & ((scal[2] < 7 * BX) | (core == 0))
    for i in range(4):
        halo[4 * core + i] = jnp.where(inside, outer_ref[slot, i], 0.0)
        halo[4 * (1 - core) + i] = inner_ref[slot, i]
    packed = strip_ref[slot]
    place = lanes(16) & 3
    after, before = weights[4] * packed, weights[4] * packed
    for m in range(1, 4):
        after = after + weights[4 - m] * jnp.where(place >= m, pltpu.roll(packed, m, 1), 0.0)
        before = before + weights[4 - m] * jnp.where(place < 4 - m, pltpu.roll(packed, BY - m, 1), 0.0)
    return jnp.where(gy == 0, pltpu.roll(after, BY - 4, 1), pltpu.roll(before, 4, 1))


def complete(part, halo, strips, x, scal):
    keep = near_edge(scal[1], lanes(8))
    pieces = []
    for z in range(8):
        j = 8 * (x % 4) + z
        row = 8 * (x // 4)
        turned = pltpu.roll(strips[row : row + 8], (BY - 4 * j) % BY, 1)
        pieces.append(jnp.where(keep, turned, 0.0))
    result = part[x] + jnp.concatenate(pieces, axis=0)
    for k in range(1, 5):
        if x - k < 0:
            result = result + weights[k] * halo[4 + x - k]
        if x + k >= BX:
            result = result + weights[k] * halo[x + k - 4]
    return result


FIELD = ((BX, NZ, BY), F32)
PADDED = pltpu.VMEM((BX, 80, BY), F32)
HALO = pltpu.VMEM((BX, NZ, BY), F32)


def edges(count):
    return [((count, 4, NZ, BY), F32), ((count, 4, NZ, BY), F32), ((count, 16, BY), F32)]


def first_kernel(newer, newer_out, outer, inner, strip):
    scal = position()
    for x in range(BX):
        newer_out[x] = newer[pl.ds(x, NZ, stride=8), :]
    send_edges(newer_out, outer, inner, strip, 0, scal)


def two_pieces(values):
    high = values.astype(BF16)
    return high, (values - high.astype(F32)).astype(BF16)


def block(i):
    return pl.ds(pl.multiple_of(16 * i, 16), 16)


def wide(row):
    return jnp.broadcast_to(row, (16, NREC)).astype(BF16)


def inject(n, traces, pick_cell, pick_y, spread, inj):
    value = traces[n : n + 1, :]
    coarse = value.astype(BF16).astype(F32)
    high, low = wide(coarse), wide(value - coarse)

    def weigh(i, carry):
        picked = pick_y[block(i), :]
        spread[block(i), :] = picked * high
        spread[block(8 + i), :] = picked * low
        return carry

    lax.fori_loop(0, 8, weigh, 0)
    both = lax.dot_general(
        pick_cell[...], spread[...], (((1,), (1,)), ((), ())), preferred_element_type=F32
    )
    for x in range(BX):
        part = both[NZ * x : NZ * x + NZ]
        inj[x] = part[:, :BY] + part[:, BY:]


def make_inject(n):
    def kernel(shot, pick_cell, pick_y, inj, spread):
        inject(n, shot, pick_cell, pick_y, spread, inj)

    return kernel


def prepare_kernel(shot, inj, pick_cell, pick_y, at_depth, spread):
    scal = position()
    code = shot[4:5, :].astype(I32)
    lat_x = ((code >> 6) & 63) - scal[2]
    lat_y = (code >> 12) - scal[3]
    present = (lat_x >= 0) & (lat_x < BX) & (lat_y >= 0) & (lat_y < BY)
    depth = jnp.where(present, code & 63, -1)
    col = jnp.where(present, lat_y, -1)

    def hits(i, wanted):
        number = lax.broadcasted_iota(I32, (16, NREC), 0) + 16 * i
        return jnp.where(number == wanted, 1.0, 0.0).astype(BF16)

    def depths(i, carry):
        at_depth[block(i), :] = hits(i, depth)
        return carry

    lax.fori_loop(0, 4, depths, 0)

    def planes(x, carry):
        here = wide(jnp.where(lat_x == x, 1.0, 0.0))
        for i in range(4):
            pick_cell[block(4 * x + i), :] = at_depth[16 * i : 16 * i + 16] * here
        return carry

    lax.fori_loop(0, BX, planes, 0)

    def columns(i, carry):
        pick_y[block(i), :] = hits(i, col)
        return carry

    lax.fori_loop(0, 8, columns, 0)
    inject(3, shot, pick_cell, pick_y, spread, inj)


def planes_kernel(both, older, vel):
    for x in range(BX):
        older[x] = both[pl.ds(x, NZ, stride=8), :]
        vel[x] = both[pl.ds(NZ * BX + x, NZ, stride=8), :]


def forward1_kernel(part, newer, older, vel, inj3, outer, inner, strip, acc, nxt, q, outer_o, inner_o, strip_o, halo):
    scal = position()
    strips = receive(halo, outer, inner, strip, 0, scal)
    for x in range(BX):
        a = vel[x] * complete(part, halo, strips, x, scal)
        acc[x] = a
        nxt[x] = (2.0 * newer[x] - older[x]) + a
        q[x] = vel[x] * inj3[x]
    send_edges(nxt, outer_o, inner_o, strip_o, 0, scal)
    send_edges(q, outer_o, inner_o, strip_o, 1, scal)


def make_forward(moment):
    def kernel(part, part_q, newer, older, vel, inj, inj3, *rest):
        scal = position()
        if moment == 2:
            later, rest = rest[0], rest[1:]
        outer, inner, strip, acc, nxt, p, q, outer_o, inner_o, strip_o, halo, halo_q = rest
        strips = receive(halo, outer, inner, strip, 0, scal)
        for x in range(BX):
            a = vel[x] * complete(part, halo, strips, x, scal)
            acc[x] = a
            nxt[x] = (2.0 * newer[x] - older[x]) + a
        send_edges(nxt, outer_o, inner_o, strip_o, 0, scal)
        strips = receive(halo_q, outer, inner, strip, 1, scal)
        for x in range(BX):
            before = 2.0 * inj3[x] if moment == 1 else 2.0 * later[x] - inj3[x]
            value = (before + complete(part_q, halo_q, strips, x, scal)) + inj[x]
            p[x] = value
            q[x] = vel[x] * value
        send_edges(q, outer_o, inner_o, strip_o, 1, scal)

    return kernel


def window_kernel(aperture_x, aperture_y, after, mask):
    _, _, first_x, first_y = position()
    column = lanes(8) + first_y
    inside_y = (column >= aperture_y[0]) & (column < aperture_y[0] + 192)
    for x in range(BX):
        inside_x = (first_x + x >= aperture_x[0]) & (first_x + x < aperture_x[0] + 48)
        mask[x] = jnp.where(inside_y & inside_x, 1.0, 0.0)


def masked(mask, x, values):
    inside = jnp.broadcast_to(mask[x, 0:1], (NZ, BY)) > 0.5
    return jnp.where(inside, values, 0.0)


def last_kernel(mask, part, part_q, vel, inj0, inj3, latest, later, acc0, acc1, acc2, outer, inner, strip, acc3, grad, halo, halo_q):
    scal = position()
    strips = receive(halo, outer, inner, strip, 0, scal)
    strips_q = receive(halo_q, outer, inner, strip, 1, scal)
    for x in range(BX):
        a = vel[x] * complete(part, halo, strips, x, scal)
        acc3[x] = a
        p0 = ((2.0 * later[x] - latest[x]) + complete(part_q, halo_q, strips_q, x, scal)) + inj0[x]
        total = ((a * inj3[x] + acc2[x] * latest[x]) + acc1[x] * later[x]) + acc0[x] * p0
        grad[pl.ds(x, NZ, stride=8), :] = masked(mask, x, total)


def gradient_kernel(parts, pre, scaled, copies, dot):
    total = parts[0:32]
    for s in range(1, 16):
        total = total + parts[32 * s : 32 * s + 32]
    value = pre[...] * total
    scaled[...] = value
    for s in range(16):
        copies[32 * s : 32 * s + 32] = value
    product = total * value
    dot[...] = (product[0:8] + product[8:16]) + (product[16:24] + product[24:32])


def born1_kernel(mask, full, acc0, source, d, outer_o, inner_o, strip_o):
    scal = position()
    for x in range(BX):
        s = masked(mask, x, full[pl.ds(x, NZ, stride=8), :])
        source[x] = s
        d[x] = s * acc0[x]
    send_edges(d, outer_o, inner_o, strip_o, 0, scal)


def make_born(moment, last):
    def kernel(part, now, before, source, acc, vel, outer, inner, strip, *rest):
        scal = position()
        if last:
            pick_cell, pick_y, s1, s2, s3, dot, block, halo, d, pieces = rest
        else:
            samples, d, outer_o, inner_o, strip_o, halo = rest
        strips = receive(halo, outer, inner, strip, 0, scal)
        for x in range(BX):
            base = 2.0 * now[x]
            if moment > 1:
                base = base - before[x]
            d[x] = (base + vel[x] * complete(part, halo, strips, x, scal)) + source[x] * acc[x]
        if not last:
            send_edges(d, outer_o, inner_o, strip_o, 0, scal)
            return
        s4 = sampled(d, pieces, pick_cell, pick_y)
        energy = jnp.zeros((1, BY), F32)
        for n, values in enumerate((s1[...], s2[...], s3[...], s4)):
            for j in range(16):
                piece = values[:, BY * j : BY * j + BY]
                block[16 * n + j : 16 * n + j + 1, :] = piece
                energy = energy + piece * piece
        block[64:72, :] = jnp.zeros((8, BY), F32)
        block[64:65, :] = energy
        block[65:66, :] = jnp.sum(dot[...], axis=0, keepdims=True)

    return kernel


def sampled(field, pieces, pick_cell, pick_y):
    for x in range(BX):
        high, low = two_pieces(field[x])
        pieces[NZ * x : NZ * x + NZ, :BY] = high
        pieces[NZ * x : NZ * x + NZ, BY:] = low
    at_cell = lax.dot_general(
        pieces[...], pick_cell[...], (((0,), (0,)), ((), ())), preferred_element_type=F32
    )
    chosen = (at_cell[:BY] + at_cell[BY:]) * pick_y[...].astype(F32)
    return jnp.sum(chosen, axis=0, keepdims=True)


def sample_kernel(field, pick_cell, pick_y, out, pieces):
    out[...] = sampled(field, pieces, pick_cell, pick_y)


def pair_kernel(mine, theirs, copies):
    total = mine[...] + theirs[...]
    for i in range(8):
        copies[i] = total


def collect_kernel(arrived, predicted, copies):
    total = arrived[0]
    for i in range(1, 8):
        total = total + arrived[i]
    predicted[...] = total[0:64]
    for i in range(16):
        copies[i] = total[64:72]


def finish_kernel(stats, predicted, scaled, traces, image, residual):
    total = stats[0]
    for i in range(1, 16):
        total = total + stats[i]
    energy = jnp.sum(total[0:1], axis=1, keepdims=True)
    dot = jnp.sum(total[1:2], axis=1, keepdims=True)
    step = dot / (energy + 1e-6)
    image[...] = step * scaled[...]
    for n in range(STEPS):
        for j in range(16):
            at = pl.ds(BY * j, BY)
            row = predicted[16 * n + j : 16 * n + j + 1, :]
            residual[n : n + 1, at] = traces[n : n + 1, at] - step * row


def exchange(outer, inner, strip):
    chips = [(2 * i + 1, (2 * i + 2) % 8) for i in range(4)]
    across = chips + [(b, a) for a, b in chips]
    swap = [(i, i ^ 1) for i in range(8)]
    return (
        lax.ppermute(outer, "gx", across),
        lax.ppermute(inner, "gx", swap),
        lax.ppermute(strip, "gy", [(0, 1), (1, 0)]),
    )


def on_device(older_field, newer_field, velocity, preconditioner, traces,
              receiver_z, receiver_x, receiver_y, aperture_x, aperture_y):
    flat = (NZ * BX, BY)
    newer, *e = call(first_kernel, [FIELD] + edges(1))(newer_field.reshape(flat))
    e = exchange(*e)
    def last_row(array):
        return jnp.pad(array, ((STEPS, 0), (0, 0)))

    code = last_row(receiver_z) | (last_row(receiver_x) << 6) | (last_row(receiver_y) << 12)
    shot = jnp.pad(traces[0], ((0, 1), (0, 0))) + code.astype(F32)
    inj3, pick_cell, pick_y = call(
        prepare_kernel,
        [FIELD, ((512, NREC), BF16), ((BY, NREC), BF16)],
        [pltpu.VMEM((NZ, NREC), BF16), pltpu.VMEM((2 * BY, NREC), BF16)],
    )(shot)

    def injection(n):
        return call(make_inject(n), [FIELD], [pltpu.VMEM((2 * BY, NREC), BF16)], flops=1_000_000_000)(
            shot, pick_cell, pick_y)[0]

    one = call(interior_kernel, [FIELD], [PADDED])
    two = call(interior_kernel, [FIELD] * 2, [PADDED])
    both = jnp.concatenate([older_field.reshape(flat), velocity.reshape(flat)], axis=0)
    older, vel = call(planes_kernel, [FIELD, FIELD])(both)
    acc0, u1, q, *e = call(forward1_kernel, [FIELD] * 3 + edges(2), [HALO])(
        *one(newer), newer, older, vel, inj3, *e)
    e = exchange(*e)
    acc1, u2, p2, q, *e = call(make_forward(1), [FIELD] * 4 + edges(2), [HALO] * 2)(
        *two(u1, q), u1, newer, vel, injection(2), inj3, *e)
    e = exchange(*e)
    acc2, u3, p1, q, *e = call(make_forward(2), [FIELD] * 4 + edges(2), [HALO] * 2)(
        *two(u2, q), u2, u1, vel, injection(1), inj3, p2, *e)
    e = exchange(*e)
    mask, = call(window_kernel, [((BX, 8, BY), F32)])(aperture_x, aperture_y, u2, smem=2)
    acc3, grad = call(last_kernel, [FIELD, (flat, F32)], [HALO] * 2)(
        mask, *two(u3, q), vel, injection(0), inj3, p2, p1, acc0, acc1, acc2, *e)
    parts = lax.all_to_all(grad.reshape(16, 4, BX, BY), "shot", 0, 0, tiled=True)
    scaled, copies, dot = call(
        gradient_kernel, [((32, BY), F32), (flat, F32), ((8, BY), F32)])(
        parts.reshape(flat), preconditioner.reshape(32, BY))
    full = lax.all_to_all(copies.reshape(16, 4, BX, BY), "shot", 0, 0, tiled=True)
    source, d1, *e = call(born1_kernel, [FIELD, FIELD] + edges(1))(
        mask, full.reshape(flat), acc0)
    e = exchange(*e)
    sample = call(sample_kernel, [((1, NREC), F32)], [pltpu.VMEM((512, 2 * BY), BF16)], flops=600_000_000)
    s1, = sample(d1, pick_cell, pick_y)
    d2, *e = call(make_born(1, False), [FIELD] + edges(1), [HALO])(
        *one(d1), d1, d1, source, acc1, vel, *e, s1)
    e = exchange(*e)
    s2, = sample(d2, pick_cell, pick_y)
    d3, *e = call(make_born(2, False), [FIELD] + edges(1), [HALO])(
        *one(d2), d2, d1, source, acc2, vel, *e, s2)
    e = exchange(*e)
    s3, = sample(d3, pick_cell, pick_y)
    block, = call(
        make_born(3, True), [((72, BY), F32)],
        [HALO, pltpu.VMEM((BX, NZ, BY), F32), pltpu.VMEM((512, 2 * BY), BF16)],
    )(*one(d3), d3, d2, source, acc3, vel, *e, pick_cell, pick_y, s1, s2, s3, dot)
    theirs = lax.ppermute(block, "gx", [(i, i ^ 1) for i in range(8)])
    payload, = call(pair_kernel, [((8, 72, BY), F32)])(block, theirs)
    same_core = [[2 * (2 * c + k) + g for c in range(4) for g in range(2)] for k in range(2)]
    arrived = lax.all_to_all(payload, ("gx", "gy"), 0, 0, axis_index_groups=same_core, tiled=True)
    predicted, stats = call(collect_kernel, [((64, BY), F32), ((16, 8, BY), F32)])(arrived)
    stats = lax.all_to_all(stats, "shot", 0, 0, tiled=True)
    image, residual = call(finish_kernel, [((32, BY), F32), ((4, NREC), F32)])(
        stats, predicted, scaled, traces[0])
    return image.reshape(4, BX, BY), residual[None]


def solution(mesh):
    return jax.shard_map(
        on_device,
        mesh=mesh,
        in_specs=(
            P("shot", None, "gx", "gy"),
            P("shot", None, "gx", "gy"),
            P(None, "gx", "gy"),
            P("shot", "gx", "gy"),
            P("shot", None, None),
            P("shot", None),
            P("shot", None),
            P("shot", None),
            P("shot"),
            P("shot"),
        ),
        out_specs=(P("shot", "gx", "gy"), P("shot", None, None)),
        check_vma=False,
    )
```

```python
import jax
import jax.numpy as jnp
from jax import lax
from jax.experimental import pallas as pl
from jax.experimental.pallas import tpu as pltpu
from jax.sharding import PartitionSpec as P

STEPS = 4
NZ, BX, BY = 64, 8, 128
NREC = 2048
F32, BF16, I32 = jnp.float32, jnp.bfloat16, jnp.int32
weights = (-205.0 / 72.0, 8.0 / 5.0, -1.0 / 5.0, 8.0 / 315.0, -1.0 / 560.0)


def position():
    gx, gy = lax.axis_index("gx"), lax.axis_index("gy")
    return gx & 1, gy, gx * BX, gy * BY


def call(kernel, outs, scratch=(), limit=24, flops=10_000_000):
    def run(*args, smem=0, hbm=0):
        spaces = [pltpu.SMEM] * smem + [pltpu.HBM] * hbm
        spaces = spaces + [pltpu.VMEM] * (len(args) - smem - hbm)
        specs = [pl.BlockSpec(memory_space=space) for space in spaces]
        return pl.pallas_call(
            kernel,
            out_shape=[jax.ShapeDtypeStruct(s, d) for s, d in outs],
            in_specs=specs,
            out_specs=[pl.BlockSpec(memory_space=pltpu.VMEM) for _ in outs],
            scratch_shapes=list(scratch),
            compiler_params=pltpu.CompilerParams(vmem_limit_bytes=limit * 1024 * 1024),
            cost_estimate=pl.CostEstimate(
                flops=flops, bytes_accessed=2_000_000, transcendentals=0
            ),
        )(*args)

    return run


def lanes(rows):
    return lax.broadcasted_iota(I32, (rows, BY), 1)


def near_edge(gy, lane):
    return ((gy == 0) & (lane >= BY - 4)) | ((gy == 1) & (lane < 4))


def send_edges(field, outer_ref, inner_ref, strip_ref, slot, scal):
    core = scal[0]
    for i in range(4):
        outer_ref[slot, i] = field[4 * core + i]
        inner_ref[slot, i] = field[4 * (1 - core) + i]
    pack(field, strip_ref, slot, scal)


def pack(field, strip_ref, slot, scal):
    keep = near_edge(scal[1], lanes(8))
    for half in range(2):
        sums = []
        for j in range(32):
            x, z = 4 * half + j // 8, 8 * (j % 8)
            turned = pltpu.roll(jnp.where(keep, field[x, z : z + 8], 0.0), 4 * j, 1)
            if j < 4:
                sums.append(turned)
            else:
                sums[j % 4] = sums[j % 4] + turned
        strip_ref[slot, 8 * half : 8 * half + 8] = (sums[0] + sums[1]) + (sums[2] + sums[3])


def interior(field, padded, part):
    lane = lanes(NZ)
    zero = jnp.zeros((8, BY), F32)
    for x in range(BX):
        padded[x, 0:8] = zero
        padded[x, 72:80] = zero
        padded[x, 8:72] = field[x]
    for x in range(BX):
        centre = field[x]
        result = (3.0 * weights[0]) * centre
        for k in range(1, 5):
            pairs = padded[x, 8 + k : 72 + k] + padded[x, 8 - k : 72 - k]
            if x + k < BX:
                pairs = pairs + field[x + k]
            if x - k >= 0:
                pairs = pairs + field[x - k]
            right = pltpu.roll(jnp.where(lane < k, 0.0, centre), BY - k, 1)
            left = pltpu.roll(jnp.where(lane >= BY - k, 0.0, centre), k, 1)
            result = result + weights[k] * (pairs + (right + left))
        part[x] = result


def interior_kernel(*refs):
    count = (len(refs) - 1) // 2
    for i in range(count):
        interior(refs[i], refs[-1], refs[count + i])


def receive(halo, outer_ref, inner_ref, strip_ref, slot, scal):
    core, gy = scal[0], scal[1]
    inside = ((scal[2] > 0) | (core == 1)) & ((scal[2] < 7 * BX) | (core == 0))
    for i in range(4):
        outer, inner = outer_ref[slot, i], inner_ref[slot, i]
        halo[4 * core + i] = jnp.where(inside, outer, 0.0)
        halo[4 * (1 - core) + i] = inner
    packed = strip_ref[slot]
    place = lanes(16) & 3
    after, before = weights[4] * packed, weights[4] * packed
    for m in range(1, 4):
        after = after + weights[4 - m] * jnp.where(place >= m, pltpu.roll(packed, m, 1), 0.0)
        before = before + weights[4 - m] * jnp.where(place < 4 - m, pltpu.roll(packed, BY - m, 1), 0.0)
    return jnp.where(gy == 0, pltpu.roll(after, BY - 4, 1), pltpu.roll(before, 4, 1))


def complete(part, halo, strips, x, scal):
    keep = near_edge(scal[1], lanes(8))
    pieces = []
    for z in range(8):
        j = 8 * (x % 4) + z
        row = 8 * (x // 4)
        turned = pltpu.roll(strips[row : row + 8], (BY - 4 * j) % BY, 1)
        pieces.append(jnp.where(keep, turned, 0.0))
    result = part[x] + jnp.concatenate(pieces, axis=0)
    for k in range(1, 5):
        if x - k < 0:
            result = result + weights[k] * halo[4 + x - k]
        if x + k >= BX:
            result = result + weights[k] * halo[x + k - 4]
    return result


FIELD = ((BX, NZ, BY), F32)
PADDED = pltpu.VMEM((BX, 80, BY), F32)
HALO = pltpu.VMEM((BX, NZ, BY), F32)


def edges(count):
    return [((count, 4, NZ, BY), F32), ((count, 4, NZ, BY), F32), ((count, 16, BY), F32)]


def first_kernel(fields, newer, older, vel, outer, inner, strip):
    for i, out in enumerate((newer, older, vel)):
        for x in range(BX):
            out[x] = fields[pl.ds(NZ * BX * i + x, NZ, stride=8), :]
    send_edges(newer, outer, inner, strip, 0, position())


def two_pieces(values):
    high = values.astype(BF16)
    return high, (values - high.astype(F32)).astype(BF16)


def block(i):
    return pl.ds(pl.multiple_of(16 * i, 16), 16)


def wide(row):
    return jnp.broadcast_to(row, (16, NREC)).astype(BF16)


def inject(n, traces, pick_cell, pick_y, spread, inj):
    value = traces[n : n + 1, :]
    coarse = value.astype(BF16).astype(F32)
    high, low = wide(coarse), wide(value - coarse)

    def weigh(i, carry):
        picked = pick_y[block(i), :]
        spread[block(i), :] = picked * high
        spread[block(8 + i), :] = picked * low
        return carry

    lax.fori_loop(0, 8, weigh, 0)
    both = lax.dot_general(
        pick_cell[...], spread[...], (((1,), (1,)), ((), ())), preferred_element_type=F32
    )
    for x in range(BX):
        part = both[NZ * x : NZ * x + NZ]
        inj[x] = part[:, :BY] + part[:, BY:]


def make_inject(n):
    def kernel(shot, pick_cell, pick_y, inj, spread):
        inject(n, shot, pick_cell, pick_y, spread, inj)

    return kernel


def prepare_kernel(shot, inj, pick_cell, pick_y, at_depth, spread):
    scal = position()
    code = shot[4:5, :].astype(I32)
    lat_x = ((code >> 6) & 63) - scal[2]
    lat_y = (code >> 12) - scal[3]
    present = (lat_x >= 0) & (lat_x < BX) & (lat_y >= 0) & (lat_y < BY)
    depth = jnp.where(present, code & 63, -1)
    col = jnp.where(present, lat_y, -1)

    def hits(i, wanted):
        number = lax.broadcasted_iota(I32, (16, NREC), 0) + 16 * i
        return jnp.where(number == wanted, 1.0, 0.0).astype(BF16)

    def depths(i, carry):
        at_depth[block(i), :] = hits(i, depth)
        return carry

    lax.fori_loop(0, 4, depths, 0)

    def planes(x, carry):
        here = wide(jnp.where(lat_x == x, 1.0, 0.0))
        for i in range(4):
            pick_cell[block(4 * x + i), :] = at_depth[16 * i : 16 * i + 16] * here
        return carry

    lax.fori_loop(0, BX, planes, 0)

    def columns(i, carry):
        pick_y[block(i), :] = hits(i, col)
        return carry

    lax.fori_loop(0, 8, columns, 0)
    inject(3, shot, pick_cell, pick_y, spread, inj)


def forward1_kernel(part, newer, older, vel, inj3, outer, inner, strip, acc, nxt, q, outer_o, inner_o, strip_o, halo):
    scal = position()
    strips = receive(halo, outer, inner, strip, 0, scal)
    for x in range(BX):
        a = vel[x] * complete(part, halo, strips, x, scal)
        acc[x] = a
        nxt[x] = (2.0 * newer[x] - older[x]) + a
        q[x] = vel[x] * inj3[x]
    send_edges(nxt, outer_o, inner_o, strip_o, 0, scal)
    send_edges(q, outer_o, inner_o, strip_o, 1, scal)


def make_forward(moment):
    def kernel(part, part_q, newer, older, vel, inj, inj3, *rest):
        scal = position()
        if moment == 2:
            later, rest = rest[0], rest[1:]
        outer, inner, strip, acc, nxt, p, q, outer_o, inner_o, strip_o, halo, halo_q = rest
        strips = receive(halo, outer, inner, strip, 0, scal)
        for x in range(BX):
            a = vel[x] * complete(part, halo, strips, x, scal)
            acc[x] = a
            nxt[x] = (2.0 * newer[x] - older[x]) + a
        send_edges(nxt, outer_o, inner_o, strip_o, 0, scal)
        strips = receive(halo_q, outer, inner, strip, 1, scal)
        for x in range(BX):
            before = 2.0 * inj3[x] if moment == 1 else 2.0 * later[x] - inj3[x]
            value = (before + complete(part_q, halo_q, strips, x, scal)) + inj[x]
            p[x] = value
            q[x] = vel[x] * value
        send_edges(q, outer_o, inner_o, strip_o, 1, scal)

    return kernel


def window_kernel(aperture_x, aperture_y, after, mask):
    _, _, first_x, first_y = position()
    column = lanes(8) + first_y
    inside_y = (column >= aperture_y[0]) & (column < aperture_y[0] + 192)
    for x in range(BX):
        inside_x = (first_x + x >= aperture_x[0]) & (first_x + x < aperture_x[0] + 48)
        mask[x] = jnp.where(inside_y & inside_x, 1.0, 0.0)


def masked(mask, x, values):
    inside = jnp.broadcast_to(mask[x, 0:1], (NZ, BY)) > 0.5
    return jnp.where(inside, values, 0.0)


def last_kernel(mask, part, part_q, vel, inj0, inj3, latest, later, acc0, acc1, acc2, outer, inner, strip, acc3, grad, halo, halo_q):
    scal = position()
    strips = receive(halo, outer, inner, strip, 0, scal)
    strips_q = receive(halo_q, outer, inner, strip, 1, scal)
    for x in range(BX):
        a = vel[x] * complete(part, halo, strips, x, scal)
        acc3[x] = a
        p0 = ((2.0 * later[x] - latest[x]) + complete(part_q, halo_q, strips_q, x, scal)) + inj0[x]
        total = ((a * inj3[x] + acc2[x] * latest[x]) + acc1[x] * later[x]) + acc0[x] * p0
        grad[pl.ds(x, NZ, stride=8), :] = masked(mask, x, total)


def gradient_kernel(parts, pre, scaled, copies, dot):
    total = parts[0:32]
    for s in range(1, 16):
        total = total + parts[32 * s : 32 * s + 32]
    value = pre[...] * total
    scaled[...] = value
    for s in range(16):
        copies[32 * s : 32 * s + 32] = value
    product = total * value
    dot[...] = (product[0:8] + product[8:16]) + (product[16:24] + product[24:32])


def born1_kernel(mask, full, acc0, source, d, outer_o, inner_o, strip_o):
    scal = position()
    for x in range(BX):
        s = masked(mask, x, full[pl.ds(x, NZ, stride=8), :])
        source[x] = s
        d[x] = s * acc0[x]
    send_edges(d, outer_o, inner_o, strip_o, 0, scal)


def make_born(moment, last):
    def kernel(part, now, before, source, acc, vel, outer, inner, strip, *rest):
        scal = position()
        if last:
            pick_cell, pick_y, s1, s2, s3, dot, block, halo, d, pieces = rest
        else:
            samples, d, outer_o, inner_o, strip_o, halo = rest
        strips = receive(halo, outer, inner, strip, 0, scal)
        for x in range(BX):
            base = 2.0 * now[x]
            if moment > 1:
                base = base - before[x]
            d[x] = (base + vel[x] * complete(part, halo, strips, x, scal)) + source[x] * acc[x]
        if not last:
            send_edges(d, outer_o, inner_o, strip_o, 0, scal)
            return
        s4 = sampled(d, pieces, pick_cell, pick_y)
        energy = jnp.zeros((1, BY), F32)
        for n, values in enumerate((s1[...], s2[...], s3[...], s4)):
            for j in range(16):
                piece = values[:, BY * j : BY * j + BY]
                block[16 * n + j : 16 * n + j + 1, :] = piece
                energy = energy + piece * piece
        block[64:72, :] = jnp.zeros((8, BY), F32)
        block[64:65, :] = energy
        block[65:66, :] = jnp.sum(dot[...], axis=0, keepdims=True)

    return kernel


def sampled(field, pieces, pick_cell, pick_y):
    for x in range(BX):
        high, low = two_pieces(field[x])
        pieces[NZ * x : NZ * x + NZ, :BY] = high
        pieces[NZ * x : NZ * x + NZ, BY:] = low
    at_cell = lax.dot_general(
        pieces[...], pick_cell[...], (((0,), (0,)), ((), ())), preferred_element_type=F32
    )
    chosen = (at_cell[:BY] + at_cell[BY:]) * pick_y[...].astype(F32)
    return jnp.sum(chosen, axis=0, keepdims=True)


def sample_kernel(field, pick_cell, pick_y, out, pieces):
    out[...] = sampled(field, pieces, pick_cell, pick_y)


def pair_kernel(mine, theirs, copies):
    total = mine[...] + theirs[...]
    for i in range(8):
        copies[i] = total


def collect_kernel(arrived, predicted, copies):
    total = arrived[0]
    for i in range(1, 8):
        total = total + arrived[i]
    predicted[...] = total[0:64]
    for i in range(16):
        copies[i] = total[64:72]


def finish_kernel(stats, predicted, scaled, traces, image, residual):
    total = stats[0]
    for i in range(1, 16):
        total = total + stats[i]
    energy = jnp.sum(total[0:1], axis=1, keepdims=True)
    dot = jnp.sum(total[1:2], axis=1, keepdims=True)
    step = dot / (energy + 1e-6)
    image[...] = step * scaled[...]
    for n in range(STEPS):
        for j in range(16):
            at = pl.ds(BY * j, BY)
            row = predicted[16 * n + j : 16 * n + j + 1, :]
            residual[n : n + 1, at] = traces[n : n + 1, at] - step * row


def exchange(outer, inner, strip):
    chips = [(2 * i + 1, (2 * i + 2) % 8) for i in range(4)]
    across = chips + [(b, a) for a, b in chips]
    swap = [(i, i ^ 1) for i in range(8)]
    return (
        lax.ppermute(outer, "gx", across),
        lax.ppermute(inner, "gx", swap),
        lax.ppermute(strip, "gy", [(0, 1), (1, 0)]),
    )


def on_device(older_field, newer_field, velocity, preconditioner, traces,
              receiver_z, receiver_x, receiver_y, aperture_x, aperture_y):
    flat = (NZ * BX, BY)
    block = newer_field.reshape(flat)
    fields = jnp.concatenate([block, older_field.reshape(flat), velocity.reshape(flat)], axis=0)
    newer, older, vel, *e = call(first_kernel, [FIELD] * 3 + edges(1))(fields)
    e = exchange(*e)
    def last_row(array):
        return jnp.pad(array, ((STEPS, 0), (0, 0)))

    code = last_row(receiver_z) | (last_row(receiver_x) << 6) | (last_row(receiver_y) << 12)
    shot = jnp.pad(traces[0], ((0, 1), (0, 0))) + code.astype(F32)
    inj3, pick_cell, pick_y = call(
        prepare_kernel,
        [FIELD, ((512, NREC), BF16), ((BY, NREC), BF16)],
        [pltpu.VMEM((NZ, NREC), BF16), pltpu.VMEM((2 * BY, NREC), BF16)],
    )(shot)

    def injection(n):
        return call(make_inject(n), [FIELD], [pltpu.VMEM((2 * BY, NREC), BF16)], flops=1_000_000_000)(
            shot, pick_cell, pick_y)[0]

    one = call(interior_kernel, [FIELD], [PADDED])
    two = call(interior_kernel, [FIELD] * 2, [PADDED])
    acc0, u1, q, *e = call(forward1_kernel, [FIELD] * 3 + edges(2), [HALO])(
        *one(newer), newer, older, vel, inj3, *e)
    e = exchange(*e)
    acc1, u2, p2, q, *e = call(make_forward(1), [FIELD] * 4 + edges(2), [HALO] * 2)(
        *two(u1, q), u1, newer, vel, injection(2), inj3, *e)
    e = exchange(*e)
    acc2, u3, p1, q, *e = call(make_forward(2), [FIELD] * 4 + edges(2), [HALO] * 2)(
        *two(u2, q), u2, u1, vel, injection(1), inj3, p2, *e)
    e = exchange(*e)
    mask, = call(window_kernel, [((BX, 8, BY), F32)])(aperture_x, aperture_y, u2, smem=2)
    acc3, grad = call(last_kernel, [FIELD, (flat, F32)], [HALO] * 2)(
        mask, *two(u3, q), vel, injection(0), inj3, p2, p1, acc0, acc1, acc2, *e)
    parts = lax.all_to_all(grad.reshape(16, 4, BX, BY), "shot", 0, 0, tiled=True)
    scaled, copies, dot = call(
        gradient_kernel, [((32, BY), F32), (flat, F32), ((8, BY), F32)])(
        parts.reshape(flat), preconditioner.reshape(32, BY))
    full = lax.all_to_all(copies.reshape(16, 4, BX, BY), "shot", 0, 0, tiled=True)
    source, d1, *e = call(born1_kernel, [FIELD, FIELD] + edges(1))(
        mask, full.reshape(flat), acc0)
    e = exchange(*e)
    sample = call(sample_kernel, [((1, NREC), F32)], [pltpu.VMEM((512, 2 * BY), BF16)], flops=600_000_000)
    s1, = sample(d1, pick_cell, pick_y)
    d2, *e = call(make_born(1, False), [FIELD] + edges(1), [HALO])(
        *one(d1), d1, d1, source, acc1, vel, *e, s1)
    e = exchange(*e)
    s2, = sample(d2, pick_cell, pick_y)
    d3, *e = call(make_born(2, False), [FIELD] + edges(1), [HALO])(
        *one(d2), d2, d1, source, acc2, vel, *e, s2)
    e = exchange(*e)
    s3, = sample(d3, pick_cell, pick_y)
    block, = call(
        make_born(3, True), [((72, BY), F32)],
        [HALO, pltpu.VMEM((BX, NZ, BY), F32), pltpu.VMEM((512, 2 * BY), BF16)],
    )(*one(d3), d3, d2, source, acc3, vel, *e, pick_cell, pick_y, s1, s2, s3, dot)
    theirs = lax.ppermute(block, "gx", [(i, i ^ 1) for i in range(8)])
    payload, = call(pair_kernel, [((8, 72, BY), F32)])(block, theirs)
    same_core = [[2 * (2 * c + k) + g for c in range(4) for g in range(2)] for k in range(2)]
    arrived = lax.all_to_all(payload, ("gx", "gy"), 0, 0, axis_index_groups=same_core, tiled=True)
    predicted, stats = call(collect_kernel, [((64, BY), F32), ((16, 8, BY), F32)])(arrived)
    stats = lax.all_to_all(stats, "shot", 0, 0, tiled=True)
    image, residual = call(finish_kernel, [((32, BY), F32), ((4, NREC), F32)])(
        stats, predicted, scaled, shot)
    return image.reshape(4, BX, BY), residual[None]


def solution(mesh):
    return jax.shard_map(
        on_device,
        mesh=mesh,
        in_specs=(
            P("shot", None, "gx", "gy"),
            P("shot", None, "gx", "gy"),
            P(None, "gx", "gy"),
            P("shot", "gx", "gy"),
            P("shot", None, None),
            P("shot", None),
            P("shot", None),
            P("shot", None),
            P("shot"),
            P("shot"),
        ),
        out_specs=(P("shot", "gx", "gy"), P("shot", None, None)),
        check_vma=False,
    )
```

```python
import jax
import jax.numpy as jnp
from jax import lax
from jax.experimental import pallas as pl
from jax.experimental.pallas import tpu as pltpu
from jax.sharding import PartitionSpec as P

STEPS = 4
NZ, BX, BY = 64, 8, 128
NREC = 2048
F32, BF16, I32 = jnp.float32, jnp.bfloat16, jnp.int32
weights = (-205.0 / 72.0, 8.0 / 5.0, -1.0 / 5.0, 8.0 / 315.0, -1.0 / 560.0)


def position():
    gx, gy = lax.axis_index("gx"), lax.axis_index("gy")
    return gx & 1, gy, gx * BX, gy * BY


def call(kernel, outs, scratch=(), limit=24, flops=10_000_000):
    def run(*args, smem=0, hbm=0):
        spaces = [pltpu.SMEM] * smem + [pltpu.HBM] * hbm
        spaces = spaces + [pltpu.VMEM] * (len(args) - smem - hbm)
        specs = [pl.BlockSpec(memory_space=space) for space in spaces]
        return pl.pallas_call(
            kernel,
            out_shape=[jax.ShapeDtypeStruct(s, d) for s, d in outs],
            in_specs=specs,
            out_specs=[pl.BlockSpec(memory_space=pltpu.VMEM) for _ in outs],
            scratch_shapes=list(scratch),
            compiler_params=pltpu.CompilerParams(vmem_limit_bytes=limit * 1024 * 1024),
            cost_estimate=pl.CostEstimate(
                flops=flops, bytes_accessed=2_000_000, transcendentals=0
            ),
        )(*args)

    return run


def lanes(rows):
    return lax.broadcasted_iota(I32, (rows, BY), 1)


def near_edge(gy, lane):
    return ((gy == 0) & (lane >= BY - 4)) | ((gy == 1) & (lane < 4))


def send_edges(field, outer_ref, inner_ref, strip_ref, slot, scal):
    core, gy = scal[0], scal[1]
    keep = near_edge(gy, lanes(8))
    for i in range(4):
        outer_ref[slot, i] = field[4 * core + i]
        inner_ref[slot, i] = field[4 * (1 - core) + i]
    for half in range(2):
        sums = []
        for j in range(32):
            x, z = 4 * half + j // 8, 8 * (j % 8)
            turned = pltpu.roll(jnp.where(keep, field[x, z : z + 8], 0.0), 4 * j, 1)
            if j < 4:
                sums.append(turned)
            else:
                sums[j % 4] = sums[j % 4] + turned
        strip_ref[slot, 8 * half : 8 * half + 8] = (sums[0] + sums[1]) + (sums[2] + sums[3])


def interior(field, padded, part):
    lane = lanes(NZ)
    zero = jnp.zeros((8, BY), F32)
    for x in range(BX):
        padded[x, 0:8] = zero
        padded[x, 72:80] = zero
        padded[x, 8:72] = field[x]
    for x in range(BX):
        centre = field[x]
        result = (3.0 * weights[0]) * centre
        for k in range(1, 5):
            pairs = padded[x, 8 + k : 72 + k] + padded[x, 8 - k : 72 - k]
            if x + k < BX:
                pairs = pairs + field[x + k]
            if x - k >= 0:
                pairs = pairs + field[x - k]
            right = pltpu.roll(jnp.where(lane < k, 0.0, centre), BY - k, 1)
            left = pltpu.roll(jnp.where(lane >= BY - k, 0.0, centre), k, 1)
            result = result + weights[k] * (pairs + (right + left))
        part[x] = result


def interior_kernel(*refs):
    count = (len(refs) - 1) // 2
    for i in range(count):
        interior(refs[i], refs[-1], refs[count + i])


def receive(halo, outer_ref, inner_ref, strip_ref, slot, scal):
    core, gy = scal[0], scal[1]
    inside = ((scal[2] > 0) | (core == 1)) & ((scal[2] < 7 * BX) | (core == 0))
    for i in range(4):
        halo[4 * core + i] = jnp.where(inside, outer_ref[slot, i], 0.0)
        halo[4 * (1 - core) + i] = inner_ref[slot, i]
    packed = strip_ref[slot]
    place = lanes(16) & 3
    after, before = weights[4] * packed, weights[4] * packed
    for m in range(1, 4):
        after = after + weights[4 - m] * jnp.where(place >= m, pltpu.roll(packed, m, 1), 0.0)
        before = before + weights[4 - m] * jnp.where(place < 4 - m, pltpu.roll(packed, BY - m, 1), 0.0)
    return jnp.where(gy == 0, pltpu.roll(after, BY - 4, 1), pltpu.roll(before, 4, 1))


def complete(part, halo, strips, x, scal):
    keep = near_edge(scal[1], lanes(8))
    pieces = []
    for z in range(8):
        j = 8 * (x % 4) + z
        row = 8 * (x // 4)
        turned = pltpu.roll(strips[row : row + 8], (BY - 4 * j) % BY, 1)
        pieces.append(jnp.where(keep, turned, 0.0))
    result = part[x] + jnp.concatenate(pieces, axis=0)
    for k in range(1, 5):
        if x - k < 0:
            result = result + weights[k] * halo[4 + x - k]
        if x + k >= BX:
            result = result + weights[k] * halo[x + k - 4]
    return result


FIELD = ((BX, NZ, BY), F32)
PADDED = pltpu.VMEM((BX, 80, BY), F32)
HALO = pltpu.VMEM((BX, NZ, BY), F32)


def edges(count):
    return [((count, 4, NZ, BY), F32), ((count, 4, NZ, BY), F32), ((count, 16, BY), F32)]


def first_kernel(newer, newer_out, outer, inner, strip):
    scal = position()
    for x in range(BX):
        newer_out[x] = newer[pl.ds(x, NZ, stride=8), :]
    send_edges(newer_out, outer, inner, strip, 0, scal)


def two_pieces(values):
    high = values.astype(BF16)
    return high, (values - high.astype(F32)).astype(BF16)


def block(i):
    return pl.ds(pl.multiple_of(16 * i, 16), 16)


def wide(row):
    return jnp.broadcast_to(row, (16, NREC)).astype(BF16)


def inject(n, traces, pick_cell, pick_y, spread, inj):
    value = traces[n : n + 1, :]
    coarse = value.astype(BF16).astype(F32)
    high, low = wide(coarse), wide(value - coarse)

    def weigh(i, carry):
        picked = pick_y[block(i), :]
        spread[block(i), :] = picked * high
        spread[block(8 + i), :] = picked * low
        return carry

    lax.fori_loop(0, 8, weigh, 0)
    both = lax.dot_general(
        pick_cell[...], spread[...], (((1,), (1,)), ((), ())), preferred_element_type=F32
    )
    for x in range(BX):
        part = both[NZ * x : NZ * x + NZ]
        inj[x] = part[:, :BY] + part[:, BY:]


def make_inject(n):
    def kernel(shot, pick_cell, pick_y, inj, spread):
        inject(n, shot, pick_cell, pick_y, spread, inj)

    return kernel


def prepare_kernel(shot, inj, pick_cell, pick_y, at_depth, spread):
    scal = position()
    code = shot[4:5, :].astype(I32)
    lat_x = ((code >> 6) & 63) - scal[2]
    lat_y = (code >> 12) - scal[3]
    present = (lat_x >= 0) & (lat_x < BX) & (lat_y >= 0) & (lat_y < BY)
    depth = jnp.where(present, code & 63, -1)
    col = jnp.where(present, lat_y, -1)

    def hits(i, wanted):
        number = lax.broadcasted_iota(I32, (16, NREC), 0) + 16 * i
        return jnp.where(number == wanted, 1.0, 0.0).astype(BF16)

    def depths(i, carry):
        at_depth[block(i), :] = hits(i, depth)
        return carry

    lax.fori_loop(0, 4, depths, 0)

    def planes(x, carry):
        here = wide(jnp.where(lat_x == x, 1.0, 0.0))
        for i in range(4):
            pick_cell[block(4 * x + i), :] = at_depth[16 * i : 16 * i + 16] * here
        return carry

    lax.fori_loop(0, BX, planes, 0)

    def columns(i, carry):
        pick_y[block(i), :] = hits(i, col)
        return carry

    lax.fori_loop(0, 8, columns, 0)
    inject(3, shot, pick_cell, pick_y, spread, inj)


def planes_kernel(both, older, vel):
    for x in range(BX):
        older[x] = both[pl.ds(x, NZ, stride=8), :]
        vel[x] = both[pl.ds(NZ * BX + x, NZ, stride=8), :]


def forward1_kernel(part, newer, older, vel, inj3, outer, inner, strip, acc, nxt, q, outer_o, inner_o, strip_o, halo):
    scal = position()
    strips = receive(halo, outer, inner, strip, 0, scal)
    for x in range(BX):
        a = vel[x] * complete(part, halo, strips, x, scal)
        acc[x] = a
        nxt[x] = (2.0 * newer[x] - older[x]) + a
        q[x] = vel[x] * inj3[x]
    send_edges(nxt, outer_o, inner_o, strip_o, 0, scal)
    send_edges(q, outer_o, inner_o, strip_o, 1, scal)


def make_forward(moment):
    def kernel(part, part_q, newer, older, vel, inj, inj3, *rest):
        scal = position()
        if moment == 2:
            later, rest = rest[0], rest[1:]
        outer, inner, strip, acc, nxt, p, q, outer_o, inner_o, strip_o, halo, halo_q = rest
        strips = receive(halo, outer, inner, strip, 0, scal)
        for x in range(BX):
            a = vel[x] * complete(part, halo, strips, x, scal)
            acc[x] = a
            nxt[x] = (2.0 * newer[x] - older[x]) + a
        send_edges(nxt, outer_o, inner_o, strip_o, 0, scal)
        strips = receive(halo_q, outer, inner, strip, 1, scal)
        for x in range(BX):
            before = 2.0 * inj3[x] if moment == 1 else 2.0 * later[x] - inj3[x]
            value = (before + complete(part_q, halo_q, strips, x, scal)) + inj[x]
            p[x] = value
            q[x] = vel[x] * value
        send_edges(q, outer_o, inner_o, strip_o, 1, scal)

    return kernel


def window_kernel(aperture_x, aperture_y, after, mask):
    _, _, first_x, first_y = position()
    column = lanes(8) + first_y
    inside_y = (column >= aperture_y[0]) & (column < aperture_y[0] + 192)
    for x in range(BX):
        inside_x = (first_x + x >= aperture_x[0]) & (first_x + x < aperture_x[0] + 48)
        mask[x] = jnp.where(inside_y & inside_x, 1.0, 0.0)


def masked(mask, x, values):
    inside = jnp.broadcast_to(mask[x, 0:1], (NZ, BY)) > 0.5
    return jnp.where(inside, values, 0.0)


def last_kernel(mask, part, part_q, vel, inj0, inj3, latest, later, acc0, acc1, acc2, outer, inner, strip, acc3, grad, halo, halo_q):
    scal = position()
    strips = receive(halo, outer, inner, strip, 0, scal)
    strips_q = receive(halo_q, outer, inner, strip, 1, scal)
    for x in range(BX):
        a = vel[x] * complete(part, halo, strips, x, scal)
        acc3[x] = a
        p0 = ((2.0 * later[x] - latest[x]) + complete(part_q, halo_q, strips_q, x, scal)) + inj0[x]
        total = ((a * inj3[x] + acc2[x] * latest[x]) + acc1[x] * later[x]) + acc0[x] * p0
        grad[pl.ds(x, NZ, stride=8), :] = masked(mask, x, total)


def gradient_kernel(parts, pre, scaled, copies, dot):
    total = parts[0:32]
    for s in range(1, 16):
        total = total + parts[32 * s : 32 * s + 32]
    value = pre[...] * total
    scaled[...] = value
    for s in range(16):
        copies[32 * s : 32 * s + 32] = value
    product = total * value
    dot[...] = (product[0:8] + product[8:16]) + (product[16:24] + product[24:32])


def born1_kernel(mask, full, acc0, source, d, outer_o, inner_o, strip_o):
    scal = position()
    for x in range(BX):
        s = masked(mask, x, full[pl.ds(x, NZ, stride=8), :])
        source[x] = s
        d[x] = s * acc0[x]
    send_edges(d, outer_o, inner_o, strip_o, 0, scal)


def make_born(moment, last):
    def kernel(part, now, before, source, acc, vel, outer, inner, strip, *rest):
        scal = position()
        if last:
            pick_cell, pick_y, s1, s2, s3, dot, block, halo, d, pieces = rest
        else:
            samples, d, outer_o, inner_o, strip_o, halo = rest
        strips = receive(halo, outer, inner, strip, 0, scal)
        for x in range(BX):
            base = 2.0 * now[x]
            if moment > 1:
                base = base - before[x]
            d[x] = (base + vel[x] * complete(part, halo, strips, x, scal)) + source[x] * acc[x]
        if not last:
            send_edges(d, outer_o, inner_o, strip_o, 0, scal)
            return
        s4 = sampled(d, pieces, pick_cell, pick_y)
        energy = jnp.zeros((1, BY), F32)
        for n, values in enumerate((s1[...], s2[...], s3[...], s4)):
            for j in range(16):
                piece = values[:, BY * j : BY * j + BY]
                block[16 * n + j : 16 * n + j + 1, :] = piece
                energy = energy + piece * piece
        block[64:72, :] = jnp.zeros((8, BY), F32)
        block[64:65, :] = energy
        block[65:66, :] = jnp.sum(dot[...], axis=0, keepdims=True)

    return kernel


def sampled(field, pieces, pick_cell, pick_y):
    for x in range(BX):
        high, low = two_pieces(field[x])
        pieces[NZ * x : NZ * x + NZ, :BY] = high
        pieces[NZ * x : NZ * x + NZ, BY:] = low
    at_cell = lax.dot_general(
        pieces[...], pick_cell[...], (((0,), (0,)), ((), ())), preferred_element_type=F32
    )
    chosen = (at_cell[:BY] + at_cell[BY:]) * pick_y[...].astype(F32)
    return jnp.sum(chosen, axis=0, keepdims=True)


def sample_kernel(field, pick_cell, pick_y, out, pieces):
    out[...] = sampled(field, pieces, pick_cell, pick_y)


def pair_kernel(mine, theirs, copies):
    own = pl.ds(pl.multiple_of(32 * position()[0], 8), 32)
    samples = mine[own, :] + theirs[own, :]
    sums = mine[64:72] + theirs[64:72]
    for i in range(8):
        copies[i, 0:32] = samples
        copies[i, 32:40] = sums


def collect_kernel(arrived, half, copies):
    total = arrived[0]
    for i in range(1, 8):
        total = total + arrived[i]
    half[...] = total[0:32]
    for i in range(16):
        copies[i] = total[32:40]


def finish_kernel(stats, half, other, scaled, traces, image, residual):
    core = position()[0]
    predicted = (jnp.where(core == 0, half[...], other[...]), jnp.where(core == 0, other[...], half[...]))
    total = stats[0]
    for i in range(1, 16):
        total = total + stats[i]
    energy = jnp.sum(total[0:1], axis=1, keepdims=True)
    dot = jnp.sum(total[1:2], axis=1, keepdims=True)
    step = dot / (energy + 1e-6)
    image[...] = step * scaled[...]
    for n in range(STEPS):
        for j in range(16):
            at = pl.ds(BY * j, BY)
            number = 16 * (n % 2) + j
            row = predicted[n // 2][number : number + 1]
            residual[n : n + 1, at] = traces[n : n + 1, at] - step * row


def exchange(outer, inner, strip):
    chips = [(2 * i + 1, (2 * i + 2) % 8) for i in range(4)]
    across = chips + [(b, a) for a, b in chips]
    swap = [(i, i ^ 1) for i in range(8)]
    return (
        lax.ppermute(outer, "gx", across),
        lax.ppermute(inner, "gx", swap),
        lax.ppermute(strip, "gy", [(0, 1), (1, 0)]),
    )


def on_device(older_field, newer_field, velocity, preconditioner, traces,
              receiver_z, receiver_x, receiver_y, aperture_x, aperture_y):
    flat = (NZ * BX, BY)
    newer, *e = call(first_kernel, [FIELD] + edges(1))(newer_field.reshape(flat))
    e = exchange(*e)
    def last_row(array):
        return jnp.pad(array, ((STEPS, 0), (0, 0)))

    code = last_row(receiver_z) | (last_row(receiver_x) << 6) | (last_row(receiver_y) << 12)
    shot = jnp.pad(traces[0], ((0, 1), (0, 0))) + code.astype(F32)
    inj3, pick_cell, pick_y = call(
        prepare_kernel,
        [FIELD, ((512, NREC), BF16), ((BY, NREC), BF16)],
        [pltpu.VMEM((NZ, NREC), BF16), pltpu.VMEM((2 * BY, NREC), BF16)],
    )(shot)

    def injection(n):
        return call(make_inject(n), [FIELD], [pltpu.VMEM((2 * BY, NREC), BF16)], flops=1_000_000_000)(
            shot, pick_cell, pick_y)[0]

    one = call(interior_kernel, [FIELD], [PADDED])
    two = call(interior_kernel, [FIELD] * 2, [PADDED])
    both = jnp.concatenate([older_field.reshape(flat), velocity.reshape(flat)], axis=0)
    older, vel = call(planes_kernel, [FIELD, FIELD])(both)
    acc0, u1, q, *e = call(forward1_kernel, [FIELD] * 3 + edges(2), [HALO])(
        *one(newer), newer, older, vel, inj3, *e)
    e = exchange(*e)
    acc1, u2, p2, q, *e = call(make_forward(1), [FIELD] * 4 + edges(2), [HALO] * 2)(
        *two(u1, q), u1, newer, vel, injection(2), inj3, *e)
    e = exchange(*e)
    acc2, u3, p1, q, *e = call(make_forward(2), [FIELD] * 4 + edges(2), [HALO] * 2)(
        *two(u2, q), u2, u1, vel, injection(1), inj3, p2, *e)
    e = exchange(*e)
    mask, = call(window_kernel, [((BX, 8, BY), F32)])(aperture_x, aperture_y, u2, smem=2)
    acc3, grad = call(last_kernel, [FIELD, (flat, F32)], [HALO] * 2)(
        mask, *two(u3, q), vel, injection(0), inj3, p2, p1, acc0, acc1, acc2, *e)
    parts = lax.all_to_all(grad.reshape(16, 4, BX, BY), "shot", 0, 0, tiled=True)
    scaled, copies, dot = call(
        gradient_kernel, [((32, BY), F32), (flat, F32), ((8, BY), F32)])(
        parts.reshape(flat), preconditioner.reshape(32, BY))
    full = lax.all_to_all(copies.reshape(16, 4, BX, BY), "shot", 0, 0, tiled=True)
    source, d1, *e = call(born1_kernel, [FIELD, FIELD] + edges(1))(
        mask, full.reshape(flat), acc0)
    e = exchange(*e)
    sample = call(sample_kernel, [((1, NREC), F32)], [pltpu.VMEM((512, 2 * BY), BF16)], flops=600_000_000)
    s1, = sample(d1, pick_cell, pick_y)
    d2, *e = call(make_born(1, False), [FIELD] + edges(1), [HALO])(
        *one(d1), d1, d1, source, acc1, vel, *e, s1)
    e = exchange(*e)
    s2, = sample(d2, pick_cell, pick_y)
    d3, *e = call(make_born(2, False), [FIELD] + edges(1), [HALO])(
        *one(d2), d2, d1, source, acc2, vel, *e, s2)
    e = exchange(*e)
    s3, = sample(d3, pick_cell, pick_y)
    block, = call(
        make_born(3, True), [((72, BY), F32)],
        [HALO, pltpu.VMEM((BX, NZ, BY), F32), pltpu.VMEM((512, 2 * BY), BF16)],
    )(*one(d3), d3, d2, source, acc3, vel, *e, pick_cell, pick_y, s1, s2, s3, dot)
    swap = [(i, i ^ 1) for i in range(8)]
    theirs = lax.ppermute(block, "gx", swap)
    payload, = call(pair_kernel, [((8, 40, BY), F32)])(block, theirs)
    same_core = [[2 * (2 * c + k) + g for c in range(4) for g in range(2)] for k in range(2)]
    arrived = lax.all_to_all(payload, ("gx", "gy"), 0, 0, axis_index_groups=same_core, tiled=True)
    half, stats = call(collect_kernel, [((32, BY), F32), ((16, 8, BY), F32)])(arrived)
    other = lax.ppermute(half, "gx", swap)
    stats = lax.all_to_all(stats, "shot", 0, 0, tiled=True)
    image, residual = call(finish_kernel, [((32, BY), F32), ((4, NREC), F32)])(
        stats, half, other, scaled, traces[0])
    return image.reshape(4, BX, BY), residual[None]


def solution(mesh):
    return jax.shard_map(
        on_device,
        mesh=mesh,
        in_specs=(
            P("shot", None, "gx", "gy"),
            P("shot", None, "gx", "gy"),
            P(None, "gx", "gy"),
            P("shot", "gx", "gy"),
            P("shot", None, None),
            P("shot", None),
            P("shot", None),
            P("shot", None),
            P("shot"),
            P("shot"),
        ),
        out_specs=(P("shot", "gx", "gy"), P("shot", None, None)),
        check_vma=False,
    )
```

```python
import jax
import jax.numpy as jnp
from jax import lax
from jax.experimental import pallas as pl
from jax.experimental.pallas import tpu as pltpu
from jax.sharding import PartitionSpec as P

STEPS = 4
NZ, BX, BY = 64, 8, 128
NREC = 2048
F32, BF16, I32 = jnp.float32, jnp.bfloat16, jnp.int32
weights = (-205.0 / 72.0, 8.0 / 5.0, -1.0 / 5.0, 8.0 / 315.0, -1.0 / 560.0)


def position():
    gx, gy = lax.axis_index("gx"), lax.axis_index("gy")
    return gx & 1, gy, gx * BX, gy * BY


def call(kernel, outs, scratch=(), limit=24, flops=10_000_000):
    def run(*args, smem=0, hbm=0):
        spaces = [pltpu.SMEM] * smem + [pltpu.HBM] * hbm
        spaces = spaces + [pltpu.VMEM] * (len(args) - smem - hbm)
        specs = [pl.BlockSpec(memory_space=space) for space in spaces]
        return pl.pallas_call(
            kernel,
            out_shape=[jax.ShapeDtypeStruct(s, d) for s, d in outs],
            in_specs=specs,
            out_specs=[pl.BlockSpec(memory_space=pltpu.VMEM) for _ in outs],
            scratch_shapes=list(scratch),
            compiler_params=pltpu.CompilerParams(vmem_limit_bytes=limit * 1024 * 1024),
            cost_estimate=pl.CostEstimate(
                flops=flops, bytes_accessed=2_000_000, transcendentals=0
            ),
        )(*args)

    return run


def lanes(rows):
    return lax.broadcasted_iota(I32, (rows, BY), 1)


def near_edge(gy, lane):
    return ((gy == 0) & (lane >= BY - 4)) | ((gy == 1) & (lane < 4))


def send_edges(field, outer_ref, inner_ref, strip_ref, slot, scal):
    core, gy = scal[0], scal[1]
    keep = near_edge(gy, lanes(8))
    for i in range(4):
        outer_ref[slot, i] = field[4 * core + i]
        inner_ref[slot, i] = field[4 * (1 - core) + i]
    for half in range(2):
        sums = []
        for j in range(32):
            x, z = 4 * half + j // 8, 8 * (j % 8)
            turned = pltpu.roll(jnp.where(keep, field[x, z : z + 8], 0.0), 4 * j, 1)
            if j < 4:
                sums.append(turned)
            else:
                sums[j % 4] = sums[j % 4] + turned
        strip_ref[slot, 8 * half : 8 * half + 8] = (sums[0] + sums[1]) + (sums[2] + sums[3])


def interior(field, padded, part):
    lane = lanes(NZ)
    zero = jnp.zeros((8, BY), F32)
    for x in range(BX):
        padded[x, 0:8] = zero
        padded[x, 72:80] = zero
        padded[x, 8:72] = field[x]
    for x in range(BX):
        centre = field[x]
        result = (3.0 * weights[0]) * centre
        for k in range(1, 5):
            pairs = padded[x, 8 + k : 72 + k] + padded[x, 8 - k : 72 - k]
            if x + k < BX:
                pairs = pairs + field[x + k]
            if x - k >= 0:
                pairs = pairs + field[x - k]
            right = pltpu.roll(jnp.where(lane < k, 0.0, centre), BY - k, 1)
            left = pltpu.roll(jnp.where(lane >= BY - k, 0.0, centre), k, 1)
            result = result + weights[k] * (pairs + (right + left))
        part[x] = result


def interior_kernel(*refs):
    count = (len(refs) - 1) // 2
    for i in range(count):
        interior(refs[i], refs[-1], refs[count + i])


def receive(halo, outer_ref, inner_ref, strip_ref, slot, scal):
    core, gy = scal[0], scal[1]
    inside = ((scal[2] > 0) | (core == 1)) & ((scal[2] < 7 * BX) | (core == 0))
    for i in range(4):
        halo[4 * core + i] = jnp.where(inside, outer_ref[slot, i], 0.0)
        halo[4 * (1 - core) + i] = inner_ref[slot, i]
    packed = strip_ref[slot]
    place = lanes(16) & 3
    after, before = weights[4] * packed, weights[4] * packed
    for m in range(1, 4):
        after = after + weights[4 - m] * jnp.where(place >= m, pltpu.roll(packed, m, 1), 0.0)
        before = before + weights[4 - m] * jnp.where(place < 4 - m, pltpu.roll(packed, BY - m, 1), 0.0)
    return jnp.where(gy == 0, pltpu.roll(after, BY - 4, 1), pltpu.roll(before, 4, 1))


def complete(part, halo, strips, x, scal):
    keep = near_edge(scal[1], lanes(8))
    pieces = []
    for z in range(8):
        j = 8 * (x % 4) + z
        row = 8 * (x // 4)
        turned = pltpu.roll(strips[row : row + 8], (BY - 4 * j) % BY, 1)
        pieces.append(jnp.where(keep, turned, 0.0))
    result = part[x] + jnp.concatenate(pieces, axis=0)
    for k in range(1, 5):
        if x - k < 0:
            result = result + weights[k] * halo[4 + x - k]
        if x + k >= BX:
            result = result + weights[k] * halo[x + k - 4]
    return result


FIELD = ((BX, NZ, BY), F32)
PADDED = pltpu.VMEM((BX, 80, BY), F32)
HALO = pltpu.VMEM((BX, NZ, BY), F32)


def edges(count):
    return [((count, 4, NZ, BY), F32), ((count, 4, NZ, BY), F32), ((count, 16, BY), F32)]


def first_kernel(newer, newer_out, outer, inner, strip):
    scal = position()
    for x in range(BX):
        newer_out[x] = newer[pl.ds(x, NZ, stride=8), :]
    send_edges(newer_out, outer, inner, strip, 0, scal)


def two_pieces(values):
    high = values.astype(BF16)
    return high, (values - high.astype(F32)).astype(BF16)


def block(i):
    return pl.ds(pl.multiple_of(16 * i, 16), 16)


def wide(row):
    return jnp.broadcast_to(row, (16, NREC)).astype(BF16)


def inject(n, traces, pick_cell, pick_y, spread, inj):
    value = traces[n : n + 1, :]
    coarse = value.astype(BF16).astype(F32)
    high, low = wide(coarse), wide(value - coarse)

    def weigh(i, carry):
        picked = pick_y[block(i), :]
        spread[block(i), :] = picked * high
        spread[block(8 + i), :] = picked * low
        return carry

    lax.fori_loop(0, 8, weigh, 0)
    both = lax.dot_general(
        pick_cell[...], spread[...], (((1,), (1,)), ((), ())), preferred_element_type=F32
    )
    for x in range(BX):
        part = both[NZ * x : NZ * x + NZ]
        inj[x] = part[:, :BY] + part[:, BY:]


def make_inject(n):
    def kernel(shot, pick_cell, pick_y, inj, spread):
        inject(n, shot, pick_cell, pick_y, spread, inj)

    return kernel


def prepare_kernel(shot, inj, pick_cell, pick_y, at_depth, spread):
    scal = position()
    code = shot[4:5, :].astype(I32)
    lat_x = ((code >> 6) & 63) - scal[2]
    lat_y = (code >> 12) - scal[3]
    present = (lat_x >= 0) & (lat_x < BX) & (lat_y >= 0) & (lat_y < BY)
    depth = jnp.where(present, code & 63, -1)
    col = jnp.where(present, lat_y, -1)

    def hits(i, wanted):
        number = lax.broadcasted_iota(I32, (16, NREC), 0) + 16 * i
        return jnp.where(number == wanted, 1.0, 0.0).astype(BF16)

    def depths(i, carry):
        at_depth[block(i), :] = hits(i, depth)
        return carry

    lax.fori_loop(0, 4, depths, 0)

    def planes(x, carry):
        here = wide(jnp.where(lat_x == x, 1.0, 0.0))
        for i in range(4):
            pick_cell[block(4 * x + i), :] = at_depth[16 * i : 16 * i + 16] * here
        return carry

    lax.fori_loop(0, BX, planes, 0)

    def columns(i, carry):
        pick_y[block(i), :] = hits(i, col)
        return carry

    lax.fori_loop(0, 8, columns, 0)
    inject(3, shot, pick_cell, pick_y, spread, inj)


def planes_kernel(both, older, vel):
    for x in range(BX):
        older[x] = both[pl.ds(x, NZ, stride=8), :]
        vel[x] = both[pl.ds(NZ * BX + x, NZ, stride=8), :]


def forward1_kernel(part, newer, older, vel, inj3, outer, inner, strip, acc, nxt, q, outer_o, inner_o, strip_o, halo):
    scal = position()
    strips = receive(halo, outer, inner, strip, 0, scal)
    for x in range(BX):
        a = vel[x] * complete(part, halo, strips, x, scal)
        acc[x] = a
        nxt[x] = (2.0 * newer[x] - older[x]) + a
        q[x] = vel[x] * inj3[x]
    send_edges(nxt, outer_o, inner_o, strip_o, 0, scal)
    send_edges(q, outer_o, inner_o, strip_o, 1, scal)


def make_forward(moment):
    def kernel(part, part_q, newer, older, vel, inj, inj3, *rest):
        scal = position()
        if moment == 2:
            later, rest = rest[0], rest[1:]
        outer, inner, strip, acc, nxt, p, q, outer_o, inner_o, strip_o, halo, halo_q = rest
        strips = receive(halo, outer, inner, strip, 0, scal)
        for x in range(BX):
            a = vel[x] * complete(part, halo, strips, x, scal)
            acc[x] = a
            nxt[x] = (2.0 * newer[x] - older[x]) + a
        send_edges(nxt, outer_o, inner_o, strip_o, 0, scal)
        strips = receive(halo_q, outer, inner, strip, 1, scal)
        for x in range(BX):
            before = 2.0 * inj3[x] if moment == 1 else 2.0 * later[x] - inj3[x]
            value = (before + complete(part_q, halo_q, strips, x, scal)) + inj[x]
            p[x] = value
            q[x] = vel[x] * value
        send_edges(q, outer_o, inner_o, strip_o, 1, scal)

    return kernel


def window_kernel(aperture_x, aperture_y, after, mask):
    _, _, first_x, first_y = position()
    column = lanes(8) + first_y
    inside_y = (column >= aperture_y[0]) & (column < aperture_y[0] + 192)
    for x in range(BX):
        inside_x = (first_x + x >= aperture_x[0]) & (first_x + x < aperture_x[0] + 48)
        mask[x] = jnp.where(inside_y & inside_x, 1.0, 0.0)


def masked(mask, x, values):
    inside = jnp.broadcast_to(mask[x, 0:1], (NZ, BY)) > 0.5
    return jnp.where(inside, values, 0.0)


def last_kernel(mask, part, part_q, vel, inj0, inj3, latest, later, acc0, acc1, acc2, outer, inner, strip, acc3, grad, halo, halo_q):
    scal = position()
    strips = receive(halo, outer, inner, strip, 0, scal)
    strips_q = receive(halo_q, outer, inner, strip, 1, scal)
    for x in range(BX):
        a = vel[x] * complete(part, halo, strips, x, scal)
        acc3[x] = a
        p0 = ((2.0 * later[x] - latest[x]) + complete(part_q, halo_q, strips_q, x, scal)) + inj0[x]
        total = ((a * inj3[x] + acc2[x] * latest[x]) + acc1[x] * later[x]) + acc0[x] * p0
        grad[pl.ds(x, NZ, stride=8), :] = masked(mask, x, total)


def gradient_kernel(parts, pre, scaled, copies, dot):
    total = parts[0:32]
    for s in range(1, 16):
        total = total + parts[32 * s : 32 * s + 32]
    value = pre[...] * total
    scaled[...] = value
    for s in range(16):
        copies[32 * s : 32 * s + 32] = value
    product = total * value
    dot[...] = (product[0:8] + product[8:16]) + (product[16:24] + product[24:32])


def born1_kernel(mask, full, acc0, source, d, outer_o, inner_o, strip_o):
    scal = position()
    for x in range(BX):
        s = masked(mask, x, full[pl.ds(x, NZ, stride=8), :])
        source[x] = s
        d[x] = s * acc0[x]
    send_edges(d, outer_o, inner_o, strip_o, 0, scal)


def make_born(moment, last):
    def kernel(part, now, before, source, acc, vel, outer, inner, strip, *rest):
        scal = position()
        if last:
            pick_cell, pick_y, s1, s2, s3, dot, block, halo, d, pieces = rest
        else:
            samples, d, outer_o, inner_o, strip_o, halo = rest
        strips = receive(halo, outer, inner, strip, 0, scal)
        for x in range(BX):
            base = 2.0 * now[x]
            if moment > 1:
                base = base - before[x]
            d[x] = (base + vel[x] * complete(part, halo, strips, x, scal)) + source[x] * acc[x]
        if not last:
            send_edges(d, outer_o, inner_o, strip_o, 0, scal)
            return
        s4 = sampled(d, pieces, pick_cell, pick_y)
        energy = jnp.zeros((1, BY), F32)
        for n, values in enumerate((s1[...], s2[...], s3[...], s4)):
            for j in range(16):
                piece = values[:, BY * j : BY * j + BY]
                block[16 * n + j : 16 * n + j + 1, :] = piece
                energy = energy + piece * piece
        block[64:72, :] = jnp.zeros((8, BY), F32)
        block[64:65, :] = energy
        block[65:66, :] = jnp.sum(dot[...], axis=0, keepdims=True)

    return kernel


def sampled(field, pieces, pick_cell, pick_y):
    for x in range(BX):
        high, low = two_pieces(field[x])
        pieces[NZ * x : NZ * x + NZ, :BY] = high
        pieces[NZ * x : NZ * x + NZ, BY:] = low
    at_cell = lax.dot_general(
        pieces[...], pick_cell[...], (((0,), (0,)), ((), ())), preferred_element_type=F32
    )
    chosen = (at_cell[:BY] + at_cell[BY:]) * pick_y[...].astype(F32)
    return jnp.sum(chosen, axis=0, keepdims=True)


def sample_kernel(field, pick_cell, pick_y, out, pieces):
    out[...] = sampled(field, pieces, pick_cell, pick_y)


def pair_kernel(mine, theirs, copies):
    own = pl.ds(pl.multiple_of(32 * position()[0], 8), 32)
    samples = mine[own, :] + theirs[own, :]
    sums = mine[64:72] + theirs[64:72]
    for i in range(8):
        copies[i, 0:32] = samples
        copies[i, 32:40] = sums


def half_kernel(arrived, half):
    total = arrived[0, 0:32]
    for i in range(1, 8):
        total = total + arrived[i, 0:32]
    half[...] = total


def collect_kernel(arrived, copies):
    total = arrived[0, 32:40]
    for i in range(1, 8):
        total = total + arrived[i, 32:40]
    for i in range(16):
        copies[i] = total


def finish_kernel(stats, half, other, scaled, traces, image, residual):
    core = position()[0]
    predicted = (jnp.where(core == 0, half[...], other[...]), jnp.where(core == 0, other[...], half[...]))
    total = stats[0]
    for i in range(1, 16):
        total = total + stats[i]
    energy = jnp.sum(total[0:1], axis=1, keepdims=True)
    dot = jnp.sum(total[1:2], axis=1, keepdims=True)
    step = dot / (energy + 1e-6)
    image[...] = step * scaled[...]
    for n in range(STEPS):
        for j in range(16):
            at = pl.ds(BY * j, BY)
            number = 16 * (n % 2) + j
            row = predicted[n // 2][number : number + 1]
            residual[n : n + 1, at] = traces[n : n + 1, at] - step * row


def exchange(outer, inner, strip):
    chips = [(2 * i + 1, (2 * i + 2) % 8) for i in range(4)]
    across = chips + [(b, a) for a, b in chips]
    swap = [(i, i ^ 1) for i in range(8)]
    return (
        lax.ppermute(outer, "gx", across),
        lax.ppermute(inner, "gx", swap),
        lax.ppermute(strip, "gy", [(0, 1), (1, 0)]),
    )


def on_device(older_field, newer_field, velocity, preconditioner, traces,
              receiver_z, receiver_x, receiver_y, aperture_x, aperture_y):
    flat = (NZ * BX, BY)
    newer, *e = call(first_kernel, [FIELD] + edges(1))(newer_field.reshape(flat))
    e = exchange(*e)
    def last_row(array):
        return jnp.pad(array, ((STEPS, 0), (0, 0)))

    code = last_row(receiver_z) | (last_row(receiver_x) << 6) | (last_row(receiver_y) << 12)
    shot = jnp.pad(traces[0], ((0, 1), (0, 0))) + code.astype(F32)
    inj3, pick_cell, pick_y = call(
        prepare_kernel,
        [FIELD, ((512, NREC), BF16), ((BY, NREC), BF16)],
        [pltpu.VMEM((NZ, NREC), BF16), pltpu.VMEM((2 * BY, NREC), BF16)],
    )(shot)

    def injection(n):
        return call(make_inject(n), [FIELD], [pltpu.VMEM((2 * BY, NREC), BF16)], flops=1_000_000_000)(
            shot, pick_cell, pick_y)[0]

    one = call(interior_kernel, [FIELD], [PADDED])
    two = call(interior_kernel, [FIELD] * 2, [PADDED])
    both = jnp.concatenate([older_field.reshape(flat), velocity.reshape(flat)], axis=0)
    older, vel = call(planes_kernel, [FIELD, FIELD])(both)
    acc0, u1, q, *e = call(forward1_kernel, [FIELD] * 3 + edges(2), [HALO])(
        *one(newer), newer, older, vel, inj3, *e)
    e = exchange(*e)
    acc1, u2, p2, q, *e = call(make_forward(1), [FIELD] * 4 + edges(2), [HALO] * 2)(
        *two(u1, q), u1, newer, vel, injection(2), inj3, *e)
    e = exchange(*e)
    acc2, u3, p1, q, *e = call(make_forward(2), [FIELD] * 4 + edges(2), [HALO] * 2)(
        *two(u2, q), u2, u1, vel, injection(1), inj3, p2, *e)
    e = exchange(*e)
    mask, = call(window_kernel, [((BX, 8, BY), F32)])(aperture_x, aperture_y, u2, smem=2)
    acc3, grad = call(last_kernel, [FIELD, (flat, F32)], [HALO] * 2)(
        mask, *two(u3, q), vel, injection(0), inj3, p2, p1, acc0, acc1, acc2, *e)
    parts = lax.all_to_all(grad.reshape(16, 4, BX, BY), "shot", 0, 0, tiled=True)
    scaled, copies, dot = call(
        gradient_kernel, [((32, BY), F32), (flat, F32), ((8, BY), F32)])(
        parts.reshape(flat), preconditioner.reshape(32, BY))
    full = lax.all_to_all(copies.reshape(16, 4, BX, BY), "shot", 0, 0, tiled=True)
    source, d1, *e = call(born1_kernel, [FIELD, FIELD] + edges(1))(
        mask, full.reshape(flat), acc0)
    e = exchange(*e)
    sample = call(sample_kernel, [((1, NREC), F32)], [pltpu.VMEM((512, 2 * BY), BF16)], flops=600_000_000)
    s1, = sample(d1, pick_cell, pick_y)
    d2, *e = call(make_born(1, False), [FIELD] + edges(1), [HALO])(
        *one(d1), d1, d1, source, acc1, vel, *e, s1)
    e = exchange(*e)
    s2, = sample(d2, pick_cell, pick_y)
    d3, *e = call(make_born(2, False), [FIELD] + edges(1), [HALO])(
        *one(d2), d2, d1, source, acc2, vel, *e, s2)
    e = exchange(*e)
    s3, = sample(d3, pick_cell, pick_y)
    block, = call(
        make_born(3, True), [((72, BY), F32)],
        [HALO, pltpu.VMEM((BX, NZ, BY), F32), pltpu.VMEM((512, 2 * BY), BF16)],
    )(*one(d3), d3, d2, source, acc3, vel, *e, pick_cell, pick_y, s1, s2, s3, dot)
    swap = [(i, i ^ 1) for i in range(8)]
    theirs = lax.ppermute(block, "gx", swap)
    payload, = call(pair_kernel, [((8, 40, BY), F32)])(block, theirs)
    same_core = [[2 * (2 * c + k) + g for c in range(4) for g in range(2)] for k in range(2)]
    arrived = lax.all_to_all(payload, ("gx", "gy"), 0, 0, axis_index_groups=same_core, tiled=True)
    stats, = call(collect_kernel, [((16, 8, BY), F32)])(arrived)
    half, = call(half_kernel, [((32, BY), F32)])(arrived)
    other = lax.ppermute(half, "gx", swap)
    stats = lax.all_to_all(stats, "shot", 0, 0, tiled=True)
    image, residual = call(finish_kernel, [((32, BY), F32), ((4, NREC), F32)])(
        stats, half, other, scaled, traces[0])
    return image.reshape(4, BX, BY), residual[None]


def solution(mesh):
    return jax.shard_map(
        on_device,
        mesh=mesh,
        in_specs=(
            P("shot", None, "gx", "gy"),
            P("shot", None, "gx", "gy"),
            P(None, "gx", "gy"),
            P("shot", "gx", "gy"),
            P("shot", None, None),
            P("shot", None),
            P("shot", None),
            P("shot", None),
            P("shot"),
            P("shot"),
        ),
        out_specs=(P("shot", "gx", "gy"), P("shot", None, None)),
        check_vma=False,
    )
```

```python
import jax
import jax.numpy as jnp
from jax import lax
from jax.experimental import pallas as pl
from jax.experimental.pallas import tpu as pltpu
from jax.sharding import PartitionSpec as P

STEPS = 4
NZ, BX, BY = 64, 8, 128
NREC = 2048
F32, BF16, I32 = jnp.float32, jnp.bfloat16, jnp.int32
weights = (-205.0 / 72.0, 8.0 / 5.0, -1.0 / 5.0, 8.0 / 315.0, -1.0 / 560.0)


def position():
    gx, gy = lax.axis_index("gx"), lax.axis_index("gy")
    return gx & 1, gy, gx * BX, gy * BY


def call(kernel, outs, scratch=(), limit=24, flops=10_000_000):
    def run(*args, smem=0, hbm=0):
        spaces = [pltpu.SMEM] * smem + [pltpu.HBM] * hbm
        spaces = spaces + [pltpu.VMEM] * (len(args) - smem - hbm)
        specs = [pl.BlockSpec(memory_space=space) for space in spaces]
        return pl.pallas_call(
            kernel,
            out_shape=[jax.ShapeDtypeStruct(s, d) for s, d in outs],
            in_specs=specs,
            out_specs=[pl.BlockSpec(memory_space=pltpu.VMEM) for _ in outs],
            scratch_shapes=list(scratch),
            compiler_params=pltpu.CompilerParams(vmem_limit_bytes=limit * 1024 * 1024),
            cost_estimate=pl.CostEstimate(
                flops=flops, bytes_accessed=2_000_000, transcendentals=0
            ),
        )(*args)

    return run


def lanes(rows):
    return lax.broadcasted_iota(I32, (rows, BY), 1)


def near_edge(gy, lane):
    return ((gy == 0) & (lane >= BY - 4)) | ((gy == 1) & (lane < 4))


def send_edges(field, outer_ref, inner_ref, strip_ref, slot, scal):
    core = scal[0]
    for i in range(4):
        outer_ref[slot, i] = field[4 * core + i]
        inner_ref[slot, i] = field[4 * (1 - core) + i]
    pack(field, strip_ref, slot, scal)


def pack(field, strip_ref, slot, scal):
    keep = near_edge(scal[1], lanes(8))
    for half in range(2):
        sums = []
        for j in range(32):
            x, z = 4 * half + j // 8, 8 * (j % 8)
            turned = pltpu.roll(jnp.where(keep, field[x, z : z + 8], 0.0), 4 * j, 1)
            if j < 4:
                sums.append(turned)
            else:
                sums[j % 4] = sums[j % 4] + turned
        strip_ref[slot, 8 * half : 8 * half + 8] = (sums[0] + sums[1]) + (sums[2] + sums[3])


def interior(field, padded, part):
    lane = lanes(NZ)
    zero = jnp.zeros((8, BY), F32)
    for x in range(BX):
        padded[x, 0:8] = zero
        padded[x, 72:80] = zero
        padded[x, 8:72] = field[x]
    for x in range(BX):
        centre = field[x]
        result = (3.0 * weights[0]) * centre
        for k in range(1, 5):
            pairs = padded[x, 8 + k : 72 + k] + padded[x, 8 - k : 72 - k]
            if x + k < BX:
                pairs = pairs + field[x + k]
            if x - k >= 0:
                pairs = pairs + field[x - k]
            right = pltpu.roll(jnp.where(lane < k, 0.0, centre), BY - k, 1)
            left = pltpu.roll(jnp.where(lane >= BY - k, 0.0, centre), k, 1)
            result = result + weights[k] * (pairs + (right + left))
        part[x] = result


def interior_kernel(*refs):
    count = (len(refs) - 1) // 2
    for i in range(count):
        interior(refs[i], refs[-1], refs[count + i])


def receive(halo, outer_ref, inner_ref, strip_ref, slot, scal):
    core, gy = scal[0], scal[1]
    inside = ((scal[2] > 0) | (core == 1)) & ((scal[2] < 7 * BX) | (core == 0))
    for i in range(4):
        outer, inner = outer_ref[slot, i], inner_ref[slot, i]
        halo[4 * core + i] = jnp.where(inside, outer, 0.0)
        halo[4 * (1 - core) + i] = inner
    packed = strip_ref[slot]
    place = lanes(16) & 3
    after, before = weights[4] * packed, weights[4] * packed
    for m in range(1, 4):
        after = after + weights[4 - m] * jnp.where(place >= m, pltpu.roll(packed, m, 1), 0.0)
        before = before + weights[4 - m] * jnp.where(place < 4 - m, pltpu.roll(packed, BY - m, 1), 0.0)
    return jnp.where(gy == 0, pltpu.roll(after, BY - 4, 1), pltpu.roll(before, 4, 1))


def complete(part, halo, strips, x, scal):
    keep = near_edge(scal[1], lanes(8))
    pieces = []
    for z in range(8):
        j = 8 * (x % 4) + z
        row = 8 * (x // 4)
        turned = pltpu.roll(strips[row : row + 8], (BY - 4 * j) % BY, 1)
        pieces.append(jnp.where(keep, turned, 0.0))
    result = part[x] + jnp.concatenate(pieces, axis=0)
    for k in range(1, 5):
        if x - k < 0:
            result = result + weights[k] * halo[4 + x - k]
        if x + k >= BX:
            result = result + weights[k] * halo[x + k - 4]
    return result


FIELD = ((BX, NZ, BY), F32)
PADDED = pltpu.VMEM((BX, 80, BY), F32)
HALO = pltpu.VMEM((BX, NZ, BY), F32)


def edges(count):
    return [((count, 4, NZ, BY), F32), ((count, 4, NZ, BY), F32), ((count, 16, BY), F32)]


def first_kernel(fields, newer, older, vel, outer, inner, strip):
    for i, out in enumerate((newer, older, vel)):
        for x in range(BX):
            out[x] = fields[pl.ds(NZ * BX * i + x, NZ, stride=8), :]
    send_edges(newer, outer, inner, strip, 0, position())


def two_pieces(values):
    high = values.astype(BF16)
    return high, (values - high.astype(F32)).astype(BF16)


def block(i):
    return pl.ds(pl.multiple_of(16 * i, 16), 16)


def wide(row):
    return jnp.broadcast_to(row, (16, NREC)).astype(BF16)


def inject(n, traces, pick_cell, pick_y, spread, inj):
    value = traces[n : n + 1, :]
    coarse = value.astype(BF16).astype(F32)
    high, low = wide(coarse), wide(value - coarse)

    def weigh(i, carry):
        picked = pick_y[block(i), :]
        spread[block(i), :] = picked * high
        spread[block(8 + i), :] = picked * low
        return carry

    lax.fori_loop(0, 8, weigh, 0)
    both = lax.dot_general(
        pick_cell[...], spread[...], (((1,), (1,)), ((), ())), preferred_element_type=F32
    )
    for x in range(BX):
        part = both[NZ * x : NZ * x + NZ]
        inj[x] = part[:, :BY] + part[:, BY:]


def make_inject(n):
    def kernel(shot, pick_cell, pick_y, inj, spread):
        inject(n, shot, pick_cell, pick_y, spread, inj)

    return kernel


def prepare_kernel(shot, inj, pick_cell, pick_y, at_depth, spread):
    scal = position()
    code = shot[4:5, :].astype(I32)
    lat_x = ((code >> 6) & 63) - scal[2]
    lat_y = (code >> 12) - scal[3]
    present = (lat_x >= 0) & (lat_x < BX) & (lat_y >= 0) & (lat_y < BY)
    depth = jnp.where(present, code & 63, -1)
    col = jnp.where(present, lat_y, -1)

    def hits(i, wanted):
        number = lax.broadcasted_iota(I32, (16, NREC), 0) + 16 * i
        return jnp.where(number == wanted, 1.0, 0.0).astype(BF16)

    def depths(i, carry):
        at_depth[block(i), :] = hits(i, depth)
        return carry

    lax.fori_loop(0, 4, depths, 0)

    def planes(x, carry):
        here = wide(jnp.where(lat_x == x, 1.0, 0.0))
        for i in range(4):
            pick_cell[block(4 * x + i), :] = at_depth[16 * i : 16 * i + 16] * here
        return carry

    lax.fori_loop(0, BX, planes, 0)

    def columns(i, carry):
        pick_y[block(i), :] = hits(i, col)
        return carry

    lax.fori_loop(0, 8, columns, 0)
    inject(3, shot, pick_cell, pick_y, spread, inj)


def forward1_kernel(part, newer, older, vel, inj3, outer, inner, strip, acc, nxt, q, outer_o, inner_o, strip_o, halo):
    scal = position()
    strips = receive(halo, outer, inner, strip, 0, scal)
    for x in range(BX):
        a = vel[x] * complete(part, halo, strips, x, scal)
        acc[x] = a
        nxt[x] = (2.0 * newer[x] - older[x]) + a
        q[x] = vel[x] * inj3[x]
    send_edges(nxt, outer_o, inner_o, strip_o, 0, scal)
    send_edges(q, outer_o, inner_o, strip_o, 1, scal)


def make_forward(moment):
    def kernel(part, part_q, newer, older, vel, inj, inj3, *rest):
        scal = position()
        if moment == 2:
            later, rest = rest[0], rest[1:]
        outer, inner, strip, acc, nxt, p, q, outer_o, inner_o, strip_o, halo, halo_q = rest
        strips = receive(halo, outer, inner, strip, 0, scal)
        for x in range(BX):
            a = vel[x] * complete(part, halo, strips, x, scal)
            acc[x] = a
            nxt[x] = (2.0 * newer[x] - older[x]) + a
        send_edges(nxt, outer_o, inner_o, strip_o, 0, scal)
        strips = receive(halo_q, outer, inner, strip, 1, scal)
        for x in range(BX):
            before = 2.0 * inj3[x] if moment == 1 else 2.0 * later[x] - inj3[x]
            value = (before + complete(part_q, halo_q, strips, x, scal)) + inj[x]
            p[x] = value
            q[x] = vel[x] * value
        send_edges(q, outer_o, inner_o, strip_o, 1, scal)

    return kernel


def window_kernel(aperture_x, aperture_y, after, mask):
    _, _, first_x, first_y = position()
    column = lanes(8) + first_y
    inside_y = (column >= aperture_y[0]) & (column < aperture_y[0] + 192)
    for x in range(BX):
        inside_x = (first_x + x >= aperture_x[0]) & (first_x + x < aperture_x[0] + 48)
        mask[x] = jnp.where(inside_y & inside_x, 1.0, 0.0)


def masked(mask, x, values):
    inside = jnp.broadcast_to(mask[x, 0:1], (NZ, BY)) > 0.5
    return jnp.where(inside, values, 0.0)


def last_kernel(mask, part, part_q, vel, inj0, inj3, latest, later, acc0, acc1, acc2, outer, inner, strip, acc3, grad, halo, halo_q):
    scal = position()
    strips = receive(halo, outer, inner, strip, 0, scal)
    strips_q = receive(halo_q, outer, inner, strip, 1, scal)
    for x in range(BX):
        a = vel[x] * complete(part, halo, strips, x, scal)
        acc3[x] = a
        p0 = ((2.0 * later[x] - latest[x]) + complete(part_q, halo_q, strips_q, x, scal)) + inj0[x]
        total = ((a * inj3[x] + acc2[x] * latest[x]) + acc1[x] * later[x]) + acc0[x] * p0
        grad[pl.ds(x, NZ, stride=8), :] = masked(mask, x, total)


def gradient_kernel(parts, pre, scaled, copies, dot):
    total = parts[0:32]
    for s in range(1, 16):
        total = total + parts[32 * s : 32 * s + 32]
    value = pre[...] * total
    scaled[...] = value
    for s in range(16):
        copies[32 * s : 32 * s + 32] = value
    product = total * value
    dot[...] = (product[0:8] + product[8:16]) + (product[16:24] + product[24:32])


def born1_kernel(mask, full, acc0, source, d, outer_o, inner_o, strip_o):
    scal = position()
    for x in range(BX):
        s = masked(mask, x, full[pl.ds(x, NZ, stride=8), :])
        source[x] = s
        d[x] = s * acc0[x]
    send_edges(d, outer_o, inner_o, strip_o, 0, scal)


def make_born(moment, last):
    def kernel(part, now, before, source, acc, vel, outer, inner, strip, *rest):
        scal = position()
        if last:
            pick_cell, pick_y, s1, s2, s3, dot, block, halo, d, pieces = rest
        else:
            samples, d, outer_o, inner_o, strip_o, halo = rest
        strips = receive(halo, outer, inner, strip, 0, scal)
        for x in range(BX):
            base = 2.0 * now[x]
            if moment > 1:
                base = base - before[x]
            d[x] = (base + vel[x] * complete(part, halo, strips, x, scal)) + source[x] * acc[x]
        if not last:
            send_edges(d, outer_o, inner_o, strip_o, 0, scal)
            return
        s4 = sampled(d, pieces, pick_cell, pick_y)
        energy = jnp.zeros((1, BY), F32)
        for n, values in enumerate((s1[...], s2[...], s3[...], s4)):
            for j in range(16):
                piece = values[:, BY * j : BY * j + BY]
                block[16 * n + j : 16 * n + j + 1, :] = piece
                energy = energy + piece * piece
        block[64:72, :] = jnp.zeros((8, BY), F32)
        block[64:65, :] = energy
        block[65:66, :] = jnp.sum(dot[...], axis=0, keepdims=True)

    return kernel


def sampled(field, pieces, pick_cell, pick_y):
    for x in range(BX):
        high, low = two_pieces(field[x])
        pieces[NZ * x : NZ * x + NZ, :BY] = high
        pieces[NZ * x : NZ * x + NZ, BY:] = low
    at_cell = lax.dot_general(
        pieces[...], pick_cell[...], (((0,), (0,)), ((), ())), preferred_element_type=F32
    )
    chosen = (at_cell[:BY] + at_cell[BY:]) * pick_y[...].astype(F32)
    return jnp.sum(chosen, axis=0, keepdims=True)


def sample_kernel(field, pick_cell, pick_y, out, pieces):
    out[...] = sampled(field, pieces, pick_cell, pick_y)


def pair_kernel(mine, theirs, copies):
    own = pl.ds(pl.multiple_of(32 * position()[0], 8), 32)
    samples = mine[own, :] + theirs[own, :]
    sums = mine[64:72] + theirs[64:72]
    for i in range(8):
        copies[i, 0:32] = samples
        copies[i, 32:40] = sums


def collect_kernel(arrived, half, copies):
    total = arrived[0]
    for i in range(1, 8):
        total = total + arrived[i]
    half[...] = total[0:32]
    for i in range(16):
        copies[i] = total[32:40]


def finish_kernel(stats, half, other, scaled, traces, image, residual):
    core = position()[0]
    predicted = (jnp.where(core == 0, half[...], other[...]), jnp.where(core == 0, other[...], half[...]))
    total = stats[0]
    for i in range(1, 16):
        total = total + stats[i]
    energy = jnp.sum(total[0:1], axis=1, keepdims=True)
    dot = jnp.sum(total[1:2], axis=1, keepdims=True)
    step = dot / (energy + 1e-6)
    image[...] = step * scaled[...]
    for n in range(STEPS):
        for j in range(16):
            at = pl.ds(BY * j, BY)
            number = 16 * (n % 2) + j
            row = predicted[n // 2][number : number + 1]
            residual[n : n + 1, at] = traces[n : n + 1, at] - step * row


def exchange(outer, inner, strip):
    chips = [(2 * i + 1, (2 * i + 2) % 8) for i in range(4)]
    across = chips + [(b, a) for a, b in chips]
    swap = [(i, i ^ 1) for i in range(8)]
    return (
        lax.ppermute(outer, "gx", across),
        lax.ppermute(inner, "gx", swap),
        lax.ppermute(strip, "gy", [(0, 1), (1, 0)]),
    )


def on_device(older_field, newer_field, velocity, preconditioner, traces,
              receiver_z, receiver_x, receiver_y, aperture_x, aperture_y):
    flat = (NZ * BX, BY)
    block = newer_field.reshape(flat)
    fields = jnp.concatenate([block, older_field.reshape(flat), velocity.reshape(flat)], axis=0)
    newer, older, vel, *e = call(first_kernel, [FIELD] * 3 + edges(1))(fields)
    e = exchange(*e)
    def last_row(array):
        return jnp.pad(array, ((STEPS, 0), (0, 0)))

    code = last_row(receiver_z) | (last_row(receiver_x) << 6) | (last_row(receiver_y) << 12)
    shot = jnp.pad(traces[0], ((0, 1), (0, 0))) + code.astype(F32)
    inj3, pick_cell, pick_y = call(
        prepare_kernel,
        [FIELD, ((512, NREC), BF16), ((BY, NREC), BF16)],
        [pltpu.VMEM((NZ, NREC), BF16), pltpu.VMEM((2 * BY, NREC), BF16)],
    )(shot)

    def injection(n):
        return call(make_inject(n), [FIELD], [pltpu.VMEM((2 * BY, NREC), BF16)], flops=1_000_000_000)(
            shot, pick_cell, pick_y)[0]

    one = call(interior_kernel, [FIELD], [PADDED])
    two = call(interior_kernel, [FIELD] * 2, [PADDED])
    acc0, u1, q, *e = call(forward1_kernel, [FIELD] * 3 + edges(2), [HALO])(
        *one(newer), newer, older, vel, inj3, *e)
    e = exchange(*e)
    acc1, u2, p2, q, *e = call(make_forward(1), [FIELD] * 4 + edges(2), [HALO] * 2)(
        *two(u1, q), u1, newer, vel, injection(2), inj3, *e)
    e = exchange(*e)
    acc2, u3, p1, q, *e = call(make_forward(2), [FIELD] * 4 + edges(2), [HALO] * 2)(
        *two(u2, q), u2, u1, vel, injection(1), inj3, p2, *e)
    e = exchange(*e)
    mask, = call(window_kernel, [((BX, 8, BY), F32)])(aperture_x, aperture_y, u2, smem=2)
    acc3, grad = call(last_kernel, [FIELD, (flat, F32)], [HALO] * 2)(
        mask, *two(u3, q), vel, injection(0), inj3, p2, p1, acc0, acc1, acc2, *e)
    parts = lax.all_to_all(grad.reshape(16, 4, BX, BY), "shot", 0, 0, tiled=True)
    scaled, copies, dot = call(
        gradient_kernel, [((32, BY), F32), (flat, F32), ((8, BY), F32)])(
        parts.reshape(flat), preconditioner.reshape(32, BY))
    full = lax.all_to_all(copies.reshape(16, 4, BX, BY), "shot", 0, 0, tiled=True)
    source, d1, *e = call(born1_kernel, [FIELD, FIELD] + edges(1))(
        mask, full.reshape(flat), acc0)
    e = exchange(*e)
    sample = call(sample_kernel, [((1, NREC), F32)], [pltpu.VMEM((512, 2 * BY), BF16)], flops=600_000_000)
    s1, = sample(d1, pick_cell, pick_y)
    d2, *e = call(make_born(1, False), [FIELD] + edges(1), [HALO])(
        *one(d1), d1, d1, source, acc1, vel, *e, s1)
    e = exchange(*e)
    s2, = sample(d2, pick_cell, pick_y)
    d3, *e = call(make_born(2, False), [FIELD] + edges(1), [HALO])(
        *one(d2), d2, d1, source, acc2, vel, *e, s2)
    e = exchange(*e)
    s3, = sample(d3, pick_cell, pick_y)
    block, = call(
        make_born(3, True), [((72, BY), F32)],
        [HALO, pltpu.VMEM((BX, NZ, BY), F32), pltpu.VMEM((512, 2 * BY), BF16)],
    )(*one(d3), d3, d2, source, acc3, vel, *e, pick_cell, pick_y, s1, s2, s3, dot)
    swap = [(i, i ^ 1) for i in range(8)]
    theirs = lax.ppermute(block, "gx", swap)
    payload, = call(pair_kernel, [((8, 40, BY), F32)])(block, theirs)
    same_core = [[2 * (2 * c + k) + g for c in range(4) for g in range(2)] for k in range(2)]
    arrived = lax.all_to_all(payload, ("gx", "gy"), 0, 0, axis_index_groups=same_core, tiled=True)
    half, stats = call(collect_kernel, [((32, BY), F32), ((16, 8, BY), F32)])(arrived)
    other = lax.ppermute(half, "gx", swap)
    stats = lax.all_to_all(stats, "shot", 0, 0, tiled=True)
    image, residual = call(finish_kernel, [((32, BY), F32), ((4, NREC), F32)])(
        stats, half, other, scaled, shot)
    return image.reshape(4, BX, BY), residual[None]


def solution(mesh):
    return jax.shard_map(
        on_device,
        mesh=mesh,
        in_specs=(
            P("shot", None, "gx", "gy"),
            P("shot", None, "gx", "gy"),
            P(None, "gx", "gy"),
            P("shot", "gx", "gy"),
            P("shot", None, None),
            P("shot", None),
            P("shot", None),
            P("shot", None),
            P("shot"),
            P("shot"),
        ),
        out_specs=(P("shot", "gx", "gy"), P("shot", None, None)),
        check_vma=False,
    )
```
